32 devices in a mesh: dp: 16 (over z, x, core), seq: 2 (over y).
Axes of the slice: x: 2, y: 2, z: 4, core: 2. Of those that a mesh axis runs over, the one named last changes fastest.
Arguments:
- inputs: bfloat16 [2, 16, 1024, 896], P(None, 'dp', 'seq'), may hold values from -6 to 6
- cotangent: bfloat16 [2, 16, 1024, 896], P(None, 'dp', 'seq'), may hold values from -6 to 6
- starts: int32 [2, 16, 6], P(None, 'dp'), may hold values from 0 to 1023, as said below
- query_weight: float32 [896, 896], P(('dp', 'seq')), may hold values from -0.1875 to 0.1875
- key_weight: float32 [896, 128], P(('dp', 'seq')), may hold values from -0.1875 to 0.1875
- value_weight: float32 [896, 128], P(('dp', 'seq')), may hold values from -0.1875 to 0.1875
- out_weight: float32 [896, 896], P(None, ('dp', 'seq')), may hold values from -0.5 to 0.5
- gate_weight: float32 [896, 4864], P(('dp', 'seq')), may hold values from -0.1875 to 0.1875
- up_weight: float32 [896, 4864], P(('dp', 'seq')), may hold values from -0.1875 to 0.1875
- down_weight: float32 [4864, 896], P(None, ('dp', 'seq')), may hold values from -0.078125 to 0.078125
- vectors: float32 [2944], P(('dp', 'seq')), may hold values from -1 to 1.6, as said below
- owner_slot: int32 [130], replicated, may hold values from 0 to 159, as said below
- first_moment: float32 [160, 896, 128], P(('dp', 'seq')), may hold values from -48 to 48
- second_moment: float32 [160, 896, 128], P(('dp', 'seq')), may hold values from 2.62144 to 39.3216
- basis_left: float32 [160, 128, 128], P(('dp', 'seq')), may hold values from -0.5 to 0.5
- basis_right: float32 [160, 128, 128], P(('dp', 'seq')), may hold values from -0.5 to 0.5
- vector_first: float32 [2944], P(('dp', 'seq')), may hold values from -160 to 160
- vector_second: float32 [2944], P(('dp', 'seq')), may hold values from 98.304 to 983.04
Outputs:
- output: bfloat16 [2, 16, 1024, 896], P(None, 'dp', 'seq')
- input_grad: float32 [2, 16, 1024, 896], P(None, 'dp', 'seq')
- grad_query: float32 [896, 896], P(('dp', 'seq'))
- grad_key: float32 [896, 128], P(('dp', 'seq'))
- grad_value: float32 [896, 128], P(('dp', 'seq'))
- grad_out: float32 [896, 896], P(None, ('dp', 'seq'))
- grad_gate: float32 [896, 4864], P(('dp', 'seq'))
- grad_up: float32 [896, 4864], P(('dp', 'seq'))
- grad_down: float32 [4864, 896], P(None, ('dp', 'seq'))
- grad_vectors: float32 [2944], P(('dp', 'seq'))
- new_first: float32 [160, 896, 128], P(('dp', 'seq'))
- new_second: float32 [160, 896, 128], P(('dp', 'seq'))
- new_blocks: float32 [160, 896, 128], P(('dp', 'seq'))
- vector_second_new: float32 [2944], P(('dp', 'seq'))
- vector_new: float32 [2944], P(('dp', 'seq'))
The draws below stay inside these ranges and needn't reach their ends.
Inputs may be any that keep to these rules, and one draw needn't show every extreme that they name: In each stream the first start is 0, the starts rise strictly, and none equals 512. All values differ; block b sits in slot owner_slot[b] % 5 of device owner_slot[b] // 5 along dp+seq. `vectors`: the first 1792 entries are the gains.
All inputs are finite; a program needn't handle non-finite values.
Results may differ from the reference program's by a relative error of at most 0.013.
The reference program's roundings to bfloat16 on the way count: a program that leaves them out, or rounds other values in their place, can miss the bound.
Values may be sent and summed in bfloat16 or wider, within the bound.
A program may use at most 320 MiB of HBM per device.

```python
import math
from functools import partial
import jax
import jax.numpy as jnp
from jax import lax

D = 896
QUERY_HEADS = 14
KEY_VALUE_HEADS = 2
HEAD_SIZE = 64
FF = 4864
BW = 128
TOKEN_LENGTH = 1024
NDOC = 6
MICRO = 2
STEP = 10
QW = 896
KW = 128
STREAMS = 16
TOKENS_ALL = 32768
VEC = 2944
NBLK = 130
CAP = 5
SLOTS = 160
N_DP = 16
N_SEQ = 2


def draw_starts(key, part):
    key = jax.random.fold_in(key, 5)

    def one_stream(stream_key):
        candidates = jnp.arange(1, TOKEN_LENGTH - 1, dtype=jnp.int32)
        candidates = jnp.where(candidates >= TOKEN_LENGTH // 2, candidates + 1, candidates)
        chosen = jnp.sort(jax.random.permutation(stream_key, candidates)[:NDOC - 1])
        return jnp.concatenate([jnp.zeros((1,), jnp.int32), chosen.astype(jnp.int32)])
    stream_keys = jax.random.split(key, MICRO * STREAMS)
    drawn = jax.vmap(one_stream)(stream_keys).astype(jnp.int32)
    stream_ids = jnp.arange(MICRO * STREAMS, dtype=jnp.int32)[:, None]
    column_ids = jnp.arange(NDOC, dtype=jnp.int32)[None, :]
    top_place = (stream_ids == 0) & (column_ids == NDOC - 1)
    drawn = jnp.where(top_place, jnp.int32(TOKEN_LENGTH - 1), drawn)
    return drawn.reshape(MICRO, STREAMS, NDOC).astype(jnp.int32)


def draw_vectors(key, part):
    key = jax.random.fold_in(key, 11)
    gain_key, bias_key = jax.random.split(key)
    gains = jax.random.uniform(gain_key, (2 * D,), jnp.float32, 0.6, 1.4)
    biases = 0.5 * jnp.clip(jax.random.normal(bias_key, (QW + 2 * KW,), jnp.float32), -2.0, 2.0)
    return jnp.concatenate([gains, biases]).astype(jnp.float32)


def draw_owner_slot(key, part):
    key = jax.random.fold_in(key, 7)
    device_count = N_DP * N_SEQ
    slot_total = device_count * CAP
    empty_count = slot_total - NBLK
    host_key, order_key = jax.random.split(key)
    hosts = 1 + jax.random.permutation(host_key, device_count - 2)[:empty_count]
    flags = jnp.zeros((slot_total,), jnp.int32).at[hosts * CAP + CAP - 1].set(1)
    used_slots = jnp.argsort(flags, stable=True)[:NBLK].astype(jnp.int32)
    return jax.random.permutation(order_key, used_slots).astype(jnp.int32)


def strengthened(values, rng, source, target, shards_of, factor):
    owner, partner = [(jnp.arange(values.shape[axis_at]) // (values.shape[axis_at] // shards_of)).reshape([-1 if axis == axis_at else 1 for axis in range(values.ndim)]) for axis_at in (source, target)]
    chosen = jax.random.permutation(rng, shards_of)[partner]
    strong = (owner == chosen) | (owner == (partner + shards_of // 2) % shards_of)
    return jnp.where(strong, factor * values, values)


def level_of(rng, dims, shards, smallest, high):
    gain, own = 1.0, jax.random.fold_in(rng, 6)
    for position, blocks in shards:
        heights = jnp.exp(jax.random.uniform(jax.random.fold_in(own, position), (blocks,), jnp.float32, smallest / len(shards), high / len(shards)))
        gain = gain * jnp.repeat(heights, dims[position] // blocks).reshape([-1 if axis == position else 1 for axis in range(len(dims))])
    return gain


def scatter_about(rng, shape, deviation, bound, shards=(), kind=jnp.bfloat16):
    loudness = level_of(rng, shape, shards, -0.22, 0.18) if shards else 1.0
    values = jax.random.normal(rng, shape, jnp.float32) * deviation * loudness
    return jnp.minimum(jnp.maximum(values, -bound), bound).astype(kind)


def heavy_noise(rng, extent, deviation, limit, cuts, heavy, kind=jnp.bfloat16):
    result = deviation * jax.random.normal(rng, extent, jnp.float32)
    if cuts:
        result = result * level_of(rng, extent, cuts, -0.22, 0.18)
    return jnp.clip(strengthened(result, jax.random.fold_in(rng, 3), *heavy), -limit, limit).astype(kind)


def setup_inputs(seed: int = 0) -> dict:
    seeds = jax.random.split(jax.random.key(seed), 19)
    return {
        "inputs": heavy_noise(seeds[0], (MICRO, STREAMS, TOKEN_LENGTH, D), 1.0, 6.0, ((1, 16), (2, 2)), (1, 3, 16, 2.0)),
        "cotangent": heavy_noise(seeds[1], (MICRO, STREAMS, TOKEN_LENGTH, D), 1.0, 6.0, ((1, 16), (2, 2)), (1, 3, 16, 2.0)),
        "starts": draw_starts(jax.random.fold_in(seeds[18], 71), 0),
        "query_weight": scatter_about(seeds[3], (D, QW), D ** -0.5, 0.1875, ((0, 32),), jnp.float32),
        "key_weight": scatter_about(seeds[4], (D, KW), D ** -0.5, 0.1875, ((0, 32),), jnp.float32),
        "value_weight": scatter_about(seeds[5], (D, KW), D ** -0.5, 0.1875, ((0, 32),), jnp.float32),
        "out_weight": scatter_about(seeds[6], (QW, D), (QW // 8) ** -0.5, 0.5, ((1, 32),), jnp.float32),
        "gate_weight": scatter_about(seeds[7], (D, FF), D ** -0.5, 0.1875, ((0, 32),), jnp.float32),
        "up_weight": scatter_about(seeds[8], (D, FF), D ** -0.5, 0.1875, ((0, 32),), jnp.float32),
        "down_weight": scatter_about(seeds[9], (FF, D), FF ** -0.5, 0.078125, ((1, 32),), jnp.float32),
        "vectors": draw_vectors(jax.random.fold_in(seeds[18], 71), 0),
        "owner_slot": draw_owner_slot(jax.random.fold_in(seeds[18], 71), 0),
        "first_moment": scatter_about(seeds[12], (SLOTS, D, BW), (0.045 * TOKENS_ALL ** 0.5), 48.0, ((0, 32),), jnp.float32),
        "second_moment": jnp.clip(jnp.exp(math.log(39.3216) - 2.7080503 * jax.random.uniform(seeds[13], (SLOTS, D, BW), jnp.float32) ** level_of(seeds[13], (SLOTS, D, BW), ((0, 32),), -0.2, 0.2)), 2.62144, 39.3216),
        "basis_left": scatter_about(seeds[14], (SLOTS, BW, BW), BW ** -0.5, 0.5, ((0, 32),), jnp.float32),
        "basis_right": scatter_about(seeds[15], (SLOTS, BW, BW), BW ** -0.5, 0.5, ((0, 32),), jnp.float32),
        "vector_first": scatter_about(seeds[16], (VEC,), (0.15 * TOKENS_ALL ** 0.5), 160.0, ((0, 32),), jnp.float32),
        "vector_second": jnp.clip(jnp.exp(math.log(983.04) - 2.3025851 * jax.random.uniform(seeds[17], (VEC,), jnp.float32) ** level_of(seeds[17], (VEC,), ((0, 32),), -0.2, 0.2)), 98.304, 983.04),
    }


norm_epsilon = 1e-06
rope_theta = 1000000.0
beta_first = 0.9
beta_second = 0.999
adam_epsilon = 1e-08
weight_decay = 0.01
rate_matrix = 0.1
rate_vector = 0.5
masked_value = -1e+30

@jax.custom_vjp
def reduced_precision(v):
    return lax.optimization_barrier(v.astype(jnp.bfloat16)).astype(jnp.float32)

@jax.custom_vjp
def reduced_backward(v):
    return v

def low_keep(v):
    return (reduced_precision(v), None)

def low_pass(kept, grad):
    return (grad,)

def back_keep(v):
    return (v, None)

def back_low(kept, grad):
    return (reduced_precision(grad),)
reduced_precision.defvjp(low_keep, low_pass)
reduced_backward.defvjp(back_keep, back_low)

def matmul(former, latter):
    return jnp.dot(former, latter, precision=lax.Precision.HIGHEST, preferred_element_type=jnp.float32)

def split_vectors(vectors_full):
    gain_attn = vectors_full[:D]
    gain_mlp = vectors_full[D:2 * D]
    bias_query = vectors_full[2 * D:2 * D + QW]
    bias_key = vectors_full[2 * D + QW:2 * D + QW + KW]
    bias_value = vectors_full[2 * D + QW + KW:]
    return (gain_attn, gain_mlp, bias_query, bias_key, bias_value)

def rotary_embedding(values, cosine_values, sine_values):
    half_size = values.shape[-1] // 2
    lower_half = values[..., :half_size]
    upper_half = values[..., half_size:]
    return jnp.concatenate([lower_half * cosine_values - upper_half * sine_values, upper_half * cosine_values + lower_half * sine_values], axis=-1)

def angle_tables(places, starts):
    before = starts[None, :] <= places[:, None]
    doc_begin = lax.optimization_barrier(jnp.max(jnp.where(before, starts[None, :], 0), axis=1))
    relative = (places - doc_begin).astype(jnp.float32)
    frequency = jnp.power(rope_theta, -jnp.arange(0, HEAD_SIZE, 2, dtype=jnp.float32) / HEAD_SIZE)
    angles = relative[:, None] * frequency[None, :]
    return (jnp.cos(angles)[:, None, :], jnp.sin(angles)[:, None, :])

def doc_numbers(places, starts):
    return lax.optimization_barrier(jnp.sum((starts[None, :] <= places[:, None]).astype(jnp.int32), axis=1))

def column_blocks(matrix):
    return matrix.reshape(matrix.shape[0], -1, BW).transpose(1, 0, 2)

def row_blocks(matrix):
    return matrix.reshape(-1, BW, matrix.shape[1]).transpose(0, 2, 1)

def local_blocks(query_m, key_m, value_m, out_m, gate_m, up_m, down_m):
    return jnp.concatenate([column_blocks(query_m), column_blocks(key_m), column_blocks(value_m), row_blocks(out_m), column_blocks(gate_m), column_blocks(up_m), row_blocks(down_m)], axis=0)

def rotate_into(left_side, tile_view, right_side):
    half_turn = jnp.einsum('sba,stbe->stae', left_side, tile_view, precision=lax.Precision.HIGHEST)
    return jnp.einsum('stae,sef->staf', half_turn, right_side, precision=lax.Precision.HIGHEST)

def rotate_back(left_side, tile_view, right_side):
    half_turn = jnp.einsum('sab,stbe->stae', left_side, tile_view, precision=lax.Precision.HIGHEST)
    return jnp.einsum('stae,sfe->staf', half_turn, right_side, precision=lax.Precision.HIGHEST)

def rotated_adam(block_grads, block_weights, first_moment, second_moment, basis_left, basis_right, slot_used):
    slot_total = block_grads.shape[0]
    tile_view = block_grads.reshape(slot_total, -1, BW, BW)
    rotated = rotate_into(basis_left, tile_view, basis_right).reshape(block_grads.shape)
    first_new = beta_first * first_moment + (1.0 - beta_first) * rotated
    second_new = beta_second * second_moment + (1.0 - beta_second) * rotated * rotated
    step_size = first_new / (1.0 - beta_first ** STEP) / (jnp.sqrt(second_new / (1.0 - beta_second ** STEP)) + adam_epsilon)
    turned = rotate_back(basis_left, step_size.reshape(slot_total, -1, BW, BW), basis_right).reshape(block_grads.shape)
    updated = block_weights - rate_matrix * (turned + weight_decay * block_weights)
    used_mask = slot_used[:, None, None]
    return (jnp.where(used_mask, first_new, 0.0), jnp.where(used_mask, second_new, 0.0), jnp.where(used_mask, updated, 0.0))

def vector_adam(vectors, grad_vectors, vector_first, vector_second):
    first_new = beta_first * vector_first + (1.0 - beta_first) * grad_vectors
    second_new = beta_second * vector_second + (1.0 - beta_second) * grad_vectors * grad_vectors
    step_size = first_new / (1.0 - beta_first ** STEP) / (jnp.sqrt(second_new / (1.0 - beta_second ** STEP)) + adam_epsilon)
    return (second_new, vectors - rate_vector * step_size)

def attention_apply(rotated_queries, rotated_keys, value_reduced, document_index):
    query_group_width = QUERY_HEADS // KEY_VALUE_HEADS
    query_rows = rotated_queries.reshape(TOKEN_LENGTH, KEY_VALUE_HEADS, query_group_width, HEAD_SIZE)
    score_scale = 1.0 / math.sqrt(HEAD_SIZE)
    scores = reduced_backward(jnp.einsum('ikgd,jkd->kgij', query_rows, rotated_keys, precision=lax.Precision.HIGHEST) * score_scale)
    places = jnp.arange(TOKEN_LENGTH, dtype=jnp.int32)
    allowed = (document_index[:, None] == document_index[None, :]) & (places[None, :] <= places[:, None])
    scores = jnp.where(allowed, scores, masked_value)
    row_max = lax.optimization_barrier(jnp.max(scores, axis=-1, keepdims=True))
    exp_scores = jnp.exp(scores - row_max)
    attn_probs = reduced_precision(exp_scores / lax.optimization_barrier(jnp.sum(exp_scores, axis=-1, keepdims=True)))
    attention_output = jnp.einsum('kgij,jkd->ikgd', attn_probs, value_reduced, precision=lax.Precision.HIGHEST)
    return attention_output.reshape(TOKEN_LENGTH, QW)

def forward(params, inputs, starts):
    lowered = [reduced_precision(member) for member in params]
    query_weight, key_weight, value_weight, out_weight, gate_weight, up_weight, down_weight, vectors = lowered
    gain_attn, gain_mlp, bias_query, bias_key, bias_value = split_vectors(vectors)
    packed_stream_total = inputs.shape[0]
    places = jnp.arange(TOKEN_LENGTH, dtype=jnp.int32)
    inv_attn = lax.rsqrt(lax.optimization_barrier(jnp.mean(inputs * inputs, axis=-1, keepdims=True)) + norm_epsilon)
    normed_low = reduced_precision(inputs * inv_attn * gain_attn).reshape(-1, D)
    query_lin = reduced_backward(matmul(normed_low, query_weight) + bias_query)
    key_projected = reduced_backward(matmul(normed_low, key_weight) + bias_key)
    value_reduced = reduced_backward(reduced_precision(matmul(normed_low, value_weight) + bias_value))
    cosine_values, sine_values = jax.vmap(partial(angle_tables, places))(starts)
    rotated_queries = reduced_backward(reduced_precision(rotary_embedding(query_lin.reshape(packed_stream_total, TOKEN_LENGTH, QUERY_HEADS, HEAD_SIZE), cosine_values, sine_values)))
    rotated_keys = reduced_backward(reduced_precision(rotary_embedding(key_projected.reshape(packed_stream_total, TOKEN_LENGTH, KEY_VALUE_HEADS, HEAD_SIZE), cosine_values, sine_values)))
    document_index = jax.vmap(partial(doc_numbers, places))(starts)
    attention_output = jax.vmap(attention_apply)(rotated_queries, rotated_keys, value_reduced.reshape(packed_stream_total, TOKEN_LENGTH, KEY_VALUE_HEADS, HEAD_SIZE), document_index)
    attention_output = reduced_backward(reduced_precision(attention_output)).reshape(-1, QW)
    residual = inputs.reshape(-1, D) + reduced_backward(matmul(attention_output, out_weight))
    inv_mlp = lax.rsqrt(lax.optimization_barrier(jnp.mean(residual * residual, axis=-1, keepdims=True)) + norm_epsilon)
    normed_mlp = reduced_precision(residual * inv_mlp * gain_mlp)
    gate_act = reduced_backward(matmul(normed_mlp, gate_weight))
    up_act = reduced_backward(matmul(normed_mlp, up_weight))
    hidden = reduced_precision(jax.nn.silu(gate_act) * up_act)
    return (residual + matmul(hidden, down_weight)).reshape(packed_stream_total, TOKEN_LENGTH, D)

def reference(inputs, cotangent, starts, query_weight, key_weight, value_weight, out_weight, gate_weight, up_weight, down_weight, vectors, owner_slot, first_moment, second_moment, basis_left, basis_right, vector_first, vector_second):
    params = (query_weight, key_weight, value_weight, out_weight, gate_weight, up_weight, down_weight, vectors)
    item_count = MICRO * STREAMS
    query_group_width = 1
    while query_group_width * 2 <= max(1, 4096 // TOKEN_LENGTH) and item_count % (query_group_width * 2) == 0:
        query_group_width = query_group_width * 2
    group_count = item_count // query_group_width
    flat_inputs = inputs.astype(jnp.float32).reshape(group_count, query_group_width, TOKEN_LENGTH, D)
    flat_cotangent = cotangent.astype(jnp.float32).reshape(group_count, query_group_width, TOKEN_LENGTH, D)
    flat_starts = starts.reshape(group_count, query_group_width, NDOC)

    def one_group(totals, pieces):
        piece_inputs, piece_cotangent, piece_starts = pieces
        outputs, pullback = jax.vjp(partial(forward, starts=piece_starts), params, piece_inputs)
        grads_params, grads_input = pullback(piece_cotangent)
        summed = tuple((former + latter for former, latter in zip(totals, grads_params)))
        return (summed, (outputs.astype(jnp.bfloat16), grads_input))
    zero_grads = tuple((jnp.zeros_like(member) for member in params))
    totals, (outputs, input_grad) = lax.scan(one_group, zero_grads, (flat_inputs, flat_cotangent, flat_starts))
    output = outputs.reshape(MICRO, STREAMS, TOKEN_LENGTH, D)
    input_grad = input_grad.reshape(MICRO, STREAMS, TOKEN_LENGTH, D)
    grad_query, grad_key, grad_value, grad_out, grad_gate, grad_up, grad_down, grad_vectors = totals
    grad_blocks = local_blocks(grad_query, grad_key, grad_value, grad_out, grad_gate, grad_up, grad_down)
    weight_blocks = local_blocks(query_weight, key_weight, value_weight, out_weight, gate_weight, up_weight, down_weight)
    slot_block = jnp.full((SLOTS,), -1, jnp.int32).at[owner_slot].set(jnp.arange(NBLK, dtype=jnp.int32))
    slot_used = slot_block >= 0
    slot_index = jnp.maximum(slot_block, 0).astype(jnp.int32)
    used_mask = slot_used.astype(jnp.float32)[:, None, None]
    block_grads = jnp.take(grad_blocks, slot_index, axis=0) * used_mask
    block_weights = jnp.take(weight_blocks, slot_index, axis=0) * used_mask
    new_first, new_second, new_blocks = rotated_adam(block_grads, block_weights, first_moment, second_moment, basis_left, basis_right, slot_used)
    vector_second_new, vector_new = vector_adam(vectors, grad_vectors, vector_first, vector_second)
    return (output, input_grad, grad_query, grad_key, grad_value, grad_out, grad_gate, grad_up, grad_down, grad_vectors, new_first, new_second, new_blocks, vector_second_new, vector_new)
```

```python
import functools
import math

import jax
import jax.numpy as jnp
import numpy as np
from jax import lax
from jax.experimental import pallas as pl
from jax.experimental.pallas import tpu as pltpu
from jax.sharding import PartitionSpec as P

D = 896
QUERY_HEADS = 14
KEY_VALUE_HEADS = 2
HEAD_SIZE = 64
BW = 128
MICRO = 2
STEP = 10
QW = 896
KW = 128
QKV = QW + 2 * KW
FF = 4864

norm_epsilon = 1e-06
rope_theta = 1000000.0
beta_first = 0.9
beta_second = 0.999
adam_epsilon = 1e-08
weight_decay = 0.01
rate_matrix = 0.1
rate_vector = 0.5
masked_value = -1e30

F32 = jnp.float32
BF16 = jnp.bfloat16
BOTH = ("dp", "seq")

TILE = 256
CHUNKS = (1280, 1280, 1280, 1024)
OFFSETS = (0, 1280, 2560, 3840)
QUARTER = 112
HALF = 448
TOKEN_TILE = 256

HEAD_SETS = (
    ((0, 1, 2, 3), 0, 0),
    ((0, 1, 2), 1, 0),
    ((3, 4, 5, 6), 1, 1),
    ((4, 5, 6), 0, 1),
)
SET_ROWS = (0, 512, 896, 1408)
ALL_ROWS = 1792


def params(mib, **more):
    return pltpu.CompilerParams(vmem_limit_bytes=mib * 1024 * 1024, **more)


def dot_nn(a, b):
    return lax.dot_general(a, b, (((1,), (0,)), ((), ())), preferred_element_type=F32)


def dot_nt(a, b):
    return lax.dot_general(a, b, (((1,), (1,)), ((), ())), preferred_element_type=F32)


def dot_tn(a, b):
    return lax.dot_general(a, b, (((0,), (0,)), ((), ())), preferred_element_type=F32)


class Places:
    def __init__(self, n_dp, n_seq):
        self.line = n_dp // 4
        self.rows = D // (n_dp * n_seq)
        self.n_dev = n_dp * n_seq

        def pairs(move):
            found = []
            for z in range(self.line):
                for x in range(2):
                    for c in range(2):
                        for y in range(2):
                            tz, tx, tc, ty = move(z, x, c, y)
                            found.append(
                                (((z * 2 + x) * 2 + c) * 2 + y, ((tz * 2 + tx) * 2 + tc) * 2 + ty)
                            )
            return found

        self.sibling = pairs(lambda z, x, c, y: (z, x, 1 - c, y))
        self.long = pairs(lambda z, x, c, y: (z, 1 - x, c, y) if c == 0 else (z, x, c, 1 - y))
        self.short = pairs(lambda z, x, c, y: (z, 1 - x, c, y) if c == 1 else (z, x, c, 1 - y))
        self.ahead = [
            pairs(lambda z, x, c, y, k=k: ((z + k) % self.line, x, c, y)) for k in range(self.line)
        ]

    def natural_rows(self):
        dp = lax.axis_index("dp")
        y = lax.axis_index("seq")
        z, x, c = dp // 4, (dp // 2) % 2, dp % 2
        place = jnp.arange(D, dtype=jnp.int32)
        dc, da, db = place // HALF, (place // (2 * QUARTER)) % 2, (place // QUARTER) % 2
        dz, inner = (place % QUARTER) // self.rows, place % self.rows
        c_own = c ^ dc
        x_own = x ^ jnp.where(c_own == 0, da, db)
        y_own = y ^ jnp.where(c_own == 0, db, da)
        z_own = (z + dz) % self.line
        return self.rows * (((z_own * 2 + x_own) * 2 + c_own) * 2 + y_own) + inner


def send(array, pairs):
    return lax.ppermute(array, BOTH, pairs)


def gather_pieces(places, shard):
    line = [shard] + [send(shard, places.ahead[-k % places.line]) for k in range(1, places.line)]
    own = jnp.concatenate(line, axis=0)
    short = send(own, places.short)
    quarters = [own, short, send(own, places.long), send(short, places.long)]
    return quarters + [send(piece, places.sibling) for piece in quarters]


def reduce_rows(places, own, other):
    first = send(other, places.sibling)
    f, q, h = F32, QUARTER, places.rows
    second = send(
        (own[2 * q :].astype(f) + first[2 * q :].astype(f)).astype(BF16), places.long
    )
    third = send(
        (own[q : 2 * q].astype(f) + first[q : 2 * q].astype(f) + second[q:].astype(f)).astype(BF16),
        places.short,
    )
    total = own[:q].astype(f) + first[:q].astype(f) + second[:q].astype(f) + third.astype(f)
    arrived = [
        send(total[k * h : (k + 1) * h].astype(BF16), places.ahead[k])
        for k in range(1, places.line)
    ]
    result = total[:h]
    for part in arrived:
        result = result + part.astype(f)
    return result


def swap_halves(tile, low_half):
    return jnp.where(low_half, pltpu.roll(tile, 96, 1), pltpu.roll(tile, 32, 1))


def project_kernel(x_ref, pi_ref, *refs):
    pieces, (gain_ref, bias_ref, cos_ref, sin_ref, xp_ref, nl_ref, q_ref, k_ref, v_ref, w_scr) = (
        refs[:8],
        refs[8:],
    )

    @pl.when(pl.program_id(0) == 0)
    def _():
        for k in range(8):
            w_scr[QUARTER * k : QUARTER * (k + 1), :] = pieces[k][:, :QKV]

    xp = dot_nn(x_ref[...], pi_ref[...])
    inv = lax.rsqrt(jnp.sum(xp * xp, axis=1, keepdims=True) * (1.0 / D) + norm_epsilon)
    nl = (xp * inv * gain_ref[...]).astype(BF16)
    xp_ref[...] = xp.astype(BF16)
    nl_ref[...] = nl
    lin = dot_nn(nl, w_scr[...]) + bias_ref[...]
    cos, sin = cos_ref[...], sin_ref[...]
    low = lax.broadcasted_iota(jnp.int32, cos.shape, 1) % HEAD_SIZE < HEAD_SIZE // 2
    for t in range(8):
        piece = lin[:, 128 * t : 128 * (t + 1)]
        turned = (piece * cos + swap_halves(piece, low) * sin).astype(BF16)
        if t < 7:
            q_ref[:, 128 * t : 128 * (t + 1)] = (turned.astype(F32) * 0.125).astype(BF16)
        else:
            k_ref[...] = turned
    v_ref[...] = lin[:, QW + KW :].astype(BF16)


def project(x, pi, pieces, gain, bias, cos, sin):
    rows = x.shape[0]
    width = pieces[0].shape[1]

    def tile(cols):
        return pl.BlockSpec((TOKEN_TILE, cols), lambda t: (t, 0))

    def whole(r, c):
        return pl.BlockSpec((r, c), lambda t: (0, 0))

    shapes = [(D, BF16), (D, BF16), (QW, BF16), (KW, BF16), (KW, BF16)]
    return pl.pallas_call(
        project_kernel,
        grid=(rows // TOKEN_TILE,),
        in_specs=[tile(D), whole(D, D)]
        + [whole(QUARTER, width)] * 8
        + [whole(1, D), whole(1, QKV), tile(128), tile(128)],
        out_specs=[tile(c) for c, _ in shapes],
        out_shape=[jax.ShapeDtypeStruct((rows, c), t) for c, t in shapes],
        scratch_shapes=[pltpu.VMEM((D, QKV), BF16)],
        compiler_params=params(40),
        cost_estimate=pl.CostEstimate(
            flops=2 * rows * D * (D + QKV), bytes_accessed=14 << 20, transcendentals=0
        ),
        name="project",
    )(x, pi, *pieces, gain, bias, cos, sin)


def padded_heads(recv, own, out):
    lane = lax.broadcasted_iota(jnp.int32, (512, 128), 1)
    for part, ref in enumerate((recv, own)):
        natural = ref[0].astype(F32)
        crossed = pltpu.roll(natural, 64, 1)
        rows = pl.ds(512 * part, 512)
        for s, (_, half, head) in enumerate(HEAD_SETS):
            source = natural if half == head else crossed
            keep = (lane >= 64) if half else (lane < 64)
            out[s, rows, :] = jnp.where(keep, source, 0.0).astype(BF16)


def block_bias(kb, i, begin):
    shape = (128, 128)
    key = kb * 128 + lax.broadcasted_iota(jnp.int32, shape, 1)
    query = 512 + i * 128 + lax.broadcasted_iota(jnp.int32, shape, 0)
    return jnp.where((key >= begin) & (key <= query), 0.0, masked_value)


def stacked(tile_of, pairs):
    return jnp.concatenate([tile_of(p) for p in pairs], axis=0)


def attend_kernel(
    lo_ref, q_ref, kr_ref, ko_ref, vr_ref, vo_ref, ds_ref, o_ref, lse_ref, kp, vp, s_scr, m_scr, l_scr, acc
):
    b, i = pl.program_id(0), pl.program_id(1)

    @pl.when(i == 0)
    def _():
        padded_heads(kr_ref, ko_ref, kp)
        padded_heads(vr_ref, vo_ref, vp)

    lo, hi = lo_ref[b, i], i + 5
    begin = ds_ref[0]
    m_scr[...] = jnp.full(m_scr.shape, masked_value, F32)
    l_scr[...] = jnp.zeros(l_scr.shape, F32)
    acc[...] = jnp.zeros(acc.shape, F32)

    def scores(kb, carry):
        bias = block_bias(kb, i, begin)
        keys = pl.ds(pl.multiple_of(kb * 128, 128), 128)
        for s, (pairs, _, _) in enumerate(HEAD_SETS):
            x = stacked(lambda p: q_ref[0, :, 128 * p : 128 * (p + 1)], pairs)
            raw = dot_nt(x, kp[s, keys, :])
            for n in range(len(pairs)):
                rows = slice(SET_ROWS[s] + 128 * n, SET_ROWS[s] + 128 * (n + 1))
                value = raw[128 * n : 128 * (n + 1)] + bias
                s_scr[kb, rows, :] = value
                m_scr[rows, :] = jnp.maximum(m_scr[rows, :], value)
        return carry

    lax.fori_loop(lo, hi, scores, 0)
    top = jnp.max(m_scr[...], axis=1, keepdims=True)
    m_scr[...] = jnp.broadcast_to(top, m_scr.shape)

    def weigh(kb, carry):
        keys = pl.ds(pl.multiple_of(kb * 128, 128), 128)
        for s, (pairs, _, _) in enumerate(HEAD_SETS):
            rows = slice(SET_ROWS[s], SET_ROWS[s] + 128 * len(pairs))
            p = jnp.exp(s_scr[kb, rows, :] - m_scr[rows, :])
            l_scr[rows, :] += p
            acc[rows, :] += dot_nn(p.astype(BF16), vp[s, keys, :])
        return carry

    lax.fori_loop(lo, hi, weigh, 0)
    total = jnp.sum(l_scr[...], axis=1, keepdims=True)
    lse = m_scr[:, :1] + jnp.log(total)
    share = 1.0 / total
    lane = lax.broadcasted_iota(jnp.int32, (128, 128), 1)
    lanes = jnp.zeros((128, 128), F32)
    outs = [None] * 7
    for s, (pairs, half, _) in enumerate(HEAD_SETS):
        for n, p in enumerate(pairs):
            rows = slice(SET_ROWS[s] + 128 * n, SET_ROWS[s] + 128 * (n + 1))
            part = acc[rows, :] * share[rows]
            outs[p] = part if outs[p] is None else outs[p] + part
            lanes = jnp.where(lane == 2 * p + half, lse[rows], lanes)
    for p in range(7):
        o_ref[0, :, 128 * p : 128 * (p + 1)] = outs[p].astype(BF16)
    lse_ref[0] = lanes


def attend_specs():
    def block(cols):
        return pl.BlockSpec((1, 128, cols), lambda b, i, lo: (b, i, 0))

    def stream(cols):
        return pl.BlockSpec((1, 512, cols), lambda b, i, lo: (b, 0, 0))

    return block, stream


def attend(lo, q, k_recv, k_own, v_recv, v_own, begin):
    block, stream = attend_specs()
    return pl.pallas_call(
        attend_kernel,
        grid_spec=pltpu.PrefetchScalarGridSpec(
            num_scalar_prefetch=1,
            grid=(MICRO, 4),
            in_specs=[block(QW)] + [stream(KW)] * 4 + [block(1)],
            out_specs=[block(QW), block(128)],
            scratch_shapes=[
                pltpu.VMEM((4, 1024, 128), BF16),
                pltpu.VMEM((4, 1024, 128), BF16),
                pltpu.VMEM((8, ALL_ROWS, 128), F32),
                pltpu.VMEM((ALL_ROWS, 128), F32),
                pltpu.VMEM((ALL_ROWS, 128), F32),
                pltpu.VMEM((ALL_ROWS, 128), F32),
            ],
        ),
        out_shape=[
            jax.ShapeDtypeStruct((MICRO, 512, QW), BF16),
            jax.ShapeDtypeStruct((MICRO, 512, 128), F32),
        ],
        compiler_params=params(40),
        cost_estimate=pl.CostEstimate(
            flops=20 * 10**9, bytes_accessed=6 << 20, transcendentals=4 * 10**6
        ),
        name="attend",
    )(lo, q, k_recv, k_own, v_recv, v_own, begin)


def attend_back_kernel(
    lo_ref, q_ref, kr_ref, ko_ref, vr_ref, vo_ref, ds_ref, o_ref, do_ref, lse_ref,
    dq_ref, own_ref, recv_ref, kp, vp, dk, dv, dq_acc,
):
    b, i = pl.program_id(0), pl.program_id(1)

    @pl.when(i == 0)
    def _():
        padded_heads(kr_ref, ko_ref, kp)
        padded_heads(vr_ref, vo_ref, vp)
        dk[...] = jnp.zeros(dk.shape, F32)
        dv[...] = jnp.zeros(dv.shape, F32)

    lo, hi = lo_ref[b, i], i + 5
    begin = ds_ref[0]
    lane = lax.broadcasted_iota(jnp.int32, (128, 128), 1)
    dq_acc[...] = jnp.zeros(dq_acc.shape, F32)
    lse_all = lse_ref[0]
    lse, dots = [], []
    for s, (pairs, half, _) in enumerate(HEAD_SETS):
        for p in pairs:
            cols = slice(128 * p, 128 * (p + 1))
            product = o_ref[0, :, cols].astype(F32) * do_ref[0, :, cols].astype(F32)
            keep = (lane >= 64) if half else (lane < 64)
            dots.append(jnp.sum(jnp.where(keep, product, 0.0), axis=1, keepdims=True))
            head = 2 * p + half
            lse.append(lse_all[:, head : head + 1])

    def one_block(kb, carry):
        bias = block_bias(kb, i, begin)
        keys = pl.ds(pl.multiple_of(kb * 128, 128), 128)
        at = 0
        for s, (pairs, _, _) in enumerate(HEAD_SETS):
            x = stacked(lambda p: q_ref[0, :, 128 * p : 128 * (p + 1)], pairs)
            y = stacked(lambda p: do_ref[0, :, 128 * p : 128 * (p + 1)], pairs)
            raw = dot_nt(x, kp[s, keys, :])
            d_prob = dot_nt(y, vp[s, keys, :])
            probs, d_scores = [], []
            for n in range(len(pairs)):
                rows = slice(128 * n, 128 * (n + 1))
                p = jnp.exp(raw[rows] + bias - lse[at + n])
                probs.append(p.astype(BF16))
                d_scores.append((p * (d_prob[rows] - dots[at + n])).astype(BF16))
            at += len(pairs)
            prob = jnp.concatenate(probs, axis=0)
            d_score = jnp.concatenate(d_scores, axis=0)
            d_query = dot_nn(d_score, kp[s, keys, :])
            for n, p in enumerate(pairs):
                dq_acc[p] += d_query[128 * n : 128 * (n + 1)]
            dk[s, keys, :] += dot_tn(d_score, x)
            dv[s, keys, :] += dot_tn(prob, y)
        return carry

    lax.fori_loop(lo, hi, one_block, 0)
    for p in range(7):
        dq_ref[0, :, 128 * p : 128 * (p + 1)] = (dq_acc[p] * 0.125).astype(BF16)

    @pl.when(i == 3)
    def _():
        wide = lax.broadcasted_iota(jnp.int32, (512, 128), 1) < 64
        for part, ref in enumerate((recv_ref, own_ref)):
            rows = pl.ds(512 * part, 512)
            for n, grads in enumerate((dk, dv)):
                low = grads[0, rows, :] + pltpu.roll(grads[1, rows, :], 64, 1)
                high = grads[2, rows, :] + pltpu.roll(grads[3, rows, :], 64, 1)
                value = jnp.where(wide, low, high)
                ref[0, :, 128 * n : 128 * (n + 1)] = value.astype(ref.dtype)


def attend_back(lo, q, k_recv, k_own, v_recv, v_own, begin, out, d_out, lse):
    block, stream = attend_specs()
    return pl.pallas_call(
        attend_back_kernel,
        grid_spec=pltpu.PrefetchScalarGridSpec(
            num_scalar_prefetch=1,
            grid=(MICRO, 4),
            in_specs=[block(QW)]
            + [stream(KW)] * 4
            + [block(1), block(QW), block(QW), block(128)],
            out_specs=[block(QW), stream(256), stream(256)],
            scratch_shapes=[
                pltpu.VMEM((4, 1024, 128), BF16),
                pltpu.VMEM((4, 1024, 128), BF16),
                pltpu.VMEM((4, 1024, 128), F32),
                pltpu.VMEM((4, 1024, 128), F32),
                pltpu.VMEM((7, 128, 128), F32),
            ],
        ),
        out_shape=[
            jax.ShapeDtypeStruct((MICRO, 512, QW), BF16),
            jax.ShapeDtypeStruct((MICRO, 512, 256), F32),
            jax.ShapeDtypeStruct((MICRO, 512, 256), BF16),
        ],
        compiler_params=params(40),
        cost_estimate=pl.CostEstimate(
            flops=50 * 10**9, bytes_accessed=10 << 20, transcendentals=4 * 10**6
        ),
        name="attend_back",
    )(lo, q, k_recv, k_own, v_recv, v_own, begin, out, d_out, lse)


def middle_kernel(att_ref, xp_ref, *refs):
    pieces, (gain_ref, res_ref, n_ref, nt_ref, w_scr) = (refs[:8], refs[8:])

    @pl.when(pl.program_id(0) == 0)
    def _():
        for k in range(8):
            w_scr[QUARTER * k : QUARTER * (k + 1), :] = pieces[k][:, QKV : QKV + QW]

    residual = xp_ref[...].astype(F32) + dot_nt(att_ref[...], w_scr[...])
    inv = lax.rsqrt(jnp.sum(residual * residual, axis=1, keepdims=True) * (1.0 / D) + norm_epsilon)
    normed = residual * inv * gain_ref[...]
    res_ref[...] = residual
    n_ref[...] = normed.astype(BF16)
    nt_ref[...] = normed.T.astype(BF16)


def middle(attended, xp, pieces, gain):
    rows = xp.shape[0]
    width = pieces[0].shape[1]

    def tile(cols):
        return pl.BlockSpec((TOKEN_TILE, cols), lambda t: (t, 0))

    def whole(r, c):
        return pl.BlockSpec((r, c), lambda t: (0, 0))

    return pl.pallas_call(
        middle_kernel,
        grid=(rows // TOKEN_TILE,),
        in_specs=[tile(QW), tile(D)] + [whole(QUARTER, width)] * 8 + [whole(1, D)],
        out_specs=[tile(D), tile(D), pl.BlockSpec((D, TOKEN_TILE), lambda t: (0, t))],
        out_shape=[
            jax.ShapeDtypeStruct((rows, D), F32),
            jax.ShapeDtypeStruct((rows, D), BF16),
            jax.ShapeDtypeStruct((D, rows), BF16),
        ],
        scratch_shapes=[pltpu.VMEM((D, QW), BF16)],
        compiler_params=params(40),
        cost_estimate=pl.CostEstimate(
            flops=2 * rows * D * QW, bytes_accessed=14 << 20, transcendentals=0
        ),
        name="middle",
    )(attended, xp, *pieces, gain)


def middle_back_kernel(res_ref, mlp_ref, dn_ref, cot_ref, att_ref, pi_ref, *refs):
    pieces, (gain_ref, out_ref, dres_ref, datt_ref, own_ref, sib_ref, dgain_ref, w_scr, g_scr) = (
        refs[:8],
        refs[8:],
    )
    t = pl.program_id(0)

    @pl.when(t == 0)
    def _():
        for k in range(8):
            w_scr[QUARTER * k : QUARTER * (k + 1), :] = pieces[k][:, QKV : QKV + QW]
        g_scr[...] = jnp.zeros(g_scr.shape, F32)
        dgain_ref[...] = jnp.zeros(dgain_ref.shape, F32)

    residual = res_ref[...]
    inv = lax.rsqrt(jnp.sum(residual * residual, axis=1, keepdims=True) * (1.0 / D) + norm_epsilon)
    out_low = (residual + mlp_ref[...]).astype(BF16)
    out_ref[...] = dot_nt(out_low, pi_ref[...]).astype(BF16)
    d_normed = dn_ref[...]
    hat = residual * inv
    scaled = d_normed * gain_ref[...]
    dgain_ref[...] += jnp.sum(d_normed * hat, axis=0, keepdims=True)
    mean = jnp.sum(scaled * hat, axis=1, keepdims=True) * (1.0 / D)
    d_res = cot_ref[...].astype(F32) + inv * (scaled - hat * mean)
    dres_ref[...] = d_res
    low = d_res.astype(BF16)
    datt_ref[...] = dot_nn(low, w_scr[...]).astype(BF16)
    g_scr[...] += dot_tn(low, att_ref[...])

    @pl.when(t == pl.num_programs(0) - 1)
    def _():
        own_ref[...] = g_scr[:HALF].astype(BF16)
        sib_ref[...] = g_scr[HALF:].astype(BF16)


def middle_back(residual, mlp, d_normed, cot, attended, pi, pieces, gain):
    rows = residual.shape[0]
    width = pieces[0].shape[1]

    def tile(cols):
        return pl.BlockSpec((TOKEN_TILE, cols), lambda t: (t, 0))

    def whole(r, c):
        return pl.BlockSpec((r, c), lambda t: (0, 0))

    return pl.pallas_call(
        middle_back_kernel,
        grid=(rows // TOKEN_TILE,),
        in_specs=[tile(D)] * 4
        + [tile(QW), whole(D, D)]
        + [whole(QUARTER, width)] * 8
        + [whole(1, D)],
        out_specs=[tile(D), tile(D), tile(QW), whole(HALF, QW), whole(HALF, QW), whole(1, D)],
        out_shape=[
            jax.ShapeDtypeStruct((rows, D), BF16),
            jax.ShapeDtypeStruct((rows, D), F32),
            jax.ShapeDtypeStruct((rows, QW), BF16),
            jax.ShapeDtypeStruct((HALF, QW), BF16),
            jax.ShapeDtypeStruct((HALF, QW), BF16),
            jax.ShapeDtypeStruct((1, D), F32),
        ],
        scratch_shapes=[pltpu.VMEM((D, QW), BF16), pltpu.VMEM((D, QW), F32)],
        compiler_params=params(48),
        cost_estimate=pl.CostEstimate(
            flops=6 * rows * D * QW, bytes_accessed=26 << 20, transcendentals=0
        ),
        name="middle_back",
    )(residual, mlp, d_normed, cot, attended, pi, *pieces, gain)


def feed_kernel(wide, started, *refs):
    n_in = 4 + (2 if started else 0)
    n_hbm, nt_hbm, cot_hbm, cott_hbm = refs[:4]
    sums_in = refs[4:n_in]
    pieces = refs[n_in : n_in + 8]
    mlp_hbm, dn_hbm, own_hbm, sib_hbm = refs[n_in + 8 : n_in + 12]
    (n_v, nt_v, cot_v, cott_v, w_v, mlp_v, dn_v, act_v, grad_v, in_sem, w_sem, out_sem, g_sem) = refs[
        n_in + 12 :
    ]
    rows_all = n_v.shape[0]
    steps = wide // TILE

    loads = [
        pltpu.make_async_copy(src, dst, in_sem.at[k])
        for k, (src, dst) in enumerate(
            [(n_hbm, n_v), (cot_hbm, cot_v), (nt_hbm, nt_v), (cott_hbm, cott_v)]
            + ([(sums_in[0], mlp_v), (sums_in[1], dn_v)] if started else [])
        )
    ]
    weights = [
        [
            pltpu.make_async_copy(
                pieces[k].at[:, m * wide : (m + 1) * wide],
                w_v.at[m, QUARTER * k : QUARTER * (k + 1), :],
                w_sem.at[m, k],
            )
            for k in range(8)
        ]
        for m in range(3)
    ]
    loads[0].start()
    for m in range(3):
        for copy in weights[m]:
            copy.start()
        if m == 1:
            loads[1].start()
    for copy in loads[2:]:
        copy.start()
    loads[0].wait()
    loads[1].wait()
    for m in range(3):
        for copy in weights[m]:
            copy.wait()

    span = 512
    stores = []
    for part in range(rows_all // span):
        rows = pl.ds(part * span, span)

        def activate(j, carry):
            cols = pl.ds(pl.multiple_of(j * TILE, TILE), TILE)
            normed = n_v[rows, :]
            gate = dot_nn(normed, w_v[0, :, cols])
            up = dot_nn(normed, w_v[1, :, cols])
            d_hidden = dot_nn(cot_v[rows, :], w_v[2, :, cols])
            s = 1.0 / (1.0 + jnp.exp(-gate))
            silu = gate * s
            act_v[2, rows, cols] = (silu * up).astype(BF16)
            act_v[0, rows, cols] = (d_hidden * up * s * (1.0 + gate * (1.0 - s))).astype(BF16)
            act_v[1, rows, cols] = (d_hidden * silu).astype(BF16)
            return carry

        lax.fori_loop(0, steps, activate, 0)
        if part == 0:
            for copy in loads[4:]:
                copy.wait()
        mlp = dot_nt(act_v[2, rows, :], w_v[2])
        dn = dot_nt(act_v[0, rows, :], w_v[0]) + dot_nt(act_v[1, rows, :], w_v[1])
        if started:
            mlp = mlp + mlp_v[rows, :]
            dn = dn + dn_v[rows, :]
        mlp_v[rows, :] = mlp
        dn_v[rows, :] = dn
        for k, (src, dst) in enumerate(((mlp_v, mlp_hbm), (dn_v, dn_hbm))):
            copy = pltpu.make_async_copy(src.at[rows, :], dst.at[rows, :], out_sem.at[part, k])
            copy.start()
            stores.append(copy)

    loads[2].wait()
    loads[3].wait()

    def parts_of(m, j):
        cols = pl.ds(pl.multiple_of(j * TILE, TILE), TILE)
        target = pl.ds(pl.multiple_of(m * wide + j * TILE, TILE), TILE)
        return [
            pltpu.make_async_copy(
                grad_v.at[m, pl.ds(HALF * h, HALF), cols], dst.at[:, target], g_sem.at[m, j, h]
            )
            for h, dst in enumerate((own_hbm, sib_hbm))
        ]

    def gradients(j, carry):
        cols = pl.ds(pl.multiple_of(j * TILE, TILE), TILE)
        for m, left in enumerate((nt_v, nt_v, cott_v)):
            grad_v[m, :, cols] = dot_nn(left[...], act_v[m, :, cols]).astype(BF16)
            for copy in parts_of(m, j):
                copy.start()
        return carry

    lax.fori_loop(0, steps, gradients, 0)

    def settle(j, carry):
        for m in range(3):
            for copy in parts_of(m, j):
                copy.wait()
        return carry

    lax.fori_loop(0, steps, settle, 0)
    for copy in stores:
        copy.wait()


def feed(wide, normed, normed_t, cot, cot_t, sums, pieces):
    rows = normed.shape[0]
    started = sums is not None
    any_spec = pl.BlockSpec(memory_space=pl.ANY)
    extra = list(sums) if started else []
    n_in = 12 + len(extra)
    return pl.pallas_call(
        functools.partial(feed_kernel, wide, started),
        in_specs=[any_spec] * n_in,
        out_specs=[any_spec] * 4,
        out_shape=[
            jax.ShapeDtypeStruct((rows, D), F32),
            jax.ShapeDtypeStruct((rows, D), F32),
            jax.ShapeDtypeStruct((HALF, 3 * wide), BF16),
            jax.ShapeDtypeStruct((HALF, 3 * wide), BF16),
        ],
        scratch_shapes=[
            pltpu.VMEM((rows, D), BF16),
            pltpu.VMEM((D, rows), BF16),
            pltpu.VMEM((rows, D), BF16),
            pltpu.VMEM((D, rows), BF16),
            pltpu.VMEM((3, D, wide), BF16),
            pltpu.VMEM((rows, D), F32),
            pltpu.VMEM((rows, D), F32),
            pltpu.VMEM((3, rows, wide), BF16),
            pltpu.VMEM((3, D, wide), BF16),
            pltpu.SemaphoreType.DMA((6,)),
            pltpu.SemaphoreType.DMA((3, 8)),
            pltpu.SemaphoreType.DMA((2, 2)),
            pltpu.SemaphoreType.DMA((3, wide // TILE, 2)),
        ],
        compiler_params=params(56),
        cost_estimate=pl.CostEstimate(
            flops=18 * rows * D * wide,
            bytes_accessed=(7 + 7 + 7 + 7 + 14) << 20,
            transcendentals=rows * wide,
        ),
        name="feed",
    )(normed, normed_t, cot, cot_t, *extra, *pieces)


def project_back_kernel(dq_ref, dk_ref, dv_ref, cos_ref, sin_ref, nl_ref, xp_ref, dres_ref, pi_ref, *refs):
    pieces, (gain_ref, ig_ref, own_ref, sib_ref, dgain_ref, dbias_ref, w_scr, g_scr) = (
        refs[:8],
        refs[8:],
    )
    t = pl.program_id(0)

    @pl.when(t == 0)
    def _():
        for k in range(8):
            w_scr[QUARTER * k : QUARTER * (k + 1), :] = pieces[k][:, :QKV]
        g_scr[...] = jnp.zeros(g_scr.shape, F32)
        dgain_ref[...] = jnp.zeros(dgain_ref.shape, F32)
        dbias_ref[...] = jnp.zeros(dbias_ref.shape, F32)

    cos, sin = cos_ref[...], sin_ref[...]
    low = lax.broadcasted_iota(jnp.int32, cos.shape, 1) % HEAD_SIZE < HEAD_SIZE // 2
    parts = []
    for n in range(8):
        piece = (dq_ref[:, 128 * n : 128 * (n + 1)] if n < 7 else dk_ref[...]).astype(F32)
        parts.append((piece * cos - swap_halves(piece, low) * sin).astype(BF16))
    parts.append(dv_ref[...])
    d_lin = jnp.concatenate(parts, axis=1)
    dbias_ref[...] += jnp.sum(d_lin.astype(F32), axis=0, keepdims=True)
    d_normed = dot_nt(d_lin, w_scr[...])
    xp = xp_ref[...].astype(F32)
    inv = lax.rsqrt(jnp.sum(xp * xp, axis=1, keepdims=True) * (1.0 / D) + norm_epsilon)
    hat = xp * inv
    scaled = d_normed * gain_ref[...]
    dgain_ref[...] += jnp.sum(d_normed * hat, axis=0, keepdims=True)
    mean = jnp.sum(scaled * hat, axis=1, keepdims=True) * (1.0 / D)
    grad = dres_ref[...] + inv * (scaled - hat * mean)
    high = grad.astype(BF16)
    rest = (grad - high.astype(F32)).astype(BF16)
    ig_ref[...] = dot_nt(high, pi_ref[...]) + dot_nt(rest, pi_ref[...])
    g_scr[...] += dot_tn(nl_ref[...], d_lin)

    @pl.when(t == pl.num_programs(0) - 1)
    def _():
        own_ref[...] = g_scr[:HALF].astype(BF16)
        sib_ref[...] = g_scr[HALF:].astype(BF16)


def project_back(dq, dk, dv, cos, sin, nl, xp, d_res, pi, pieces, gain):
    rows = xp.shape[0]
    width = pieces[0].shape[1]

    def tile(cols):
        return pl.BlockSpec((TOKEN_TILE, cols), lambda t: (t, 0))

    def whole(r, c):
        return pl.BlockSpec((r, c), lambda t: (0, 0))

    return pl.pallas_call(
        project_back_kernel,
        grid=(rows // TOKEN_TILE,),
        in_specs=[tile(QW), tile(KW), tile(KW), tile(128), tile(128), tile(D), tile(D), tile(D)]
        + [whole(D, D)]
        + [whole(QUARTER, width)] * 8
        + [whole(1, D)],
        out_specs=[tile(D), whole(HALF, QKV), whole(HALF, QKV), whole(1, D), whole(1, QKV)],
        out_shape=[
            jax.ShapeDtypeStruct((rows, D), F32),
            jax.ShapeDtypeStruct((HALF, QKV), BF16),
            jax.ShapeDtypeStruct((HALF, QKV), BF16),
            jax.ShapeDtypeStruct((1, D), F32),
            jax.ShapeDtypeStruct((1, QKV), F32),
        ],
        scratch_shapes=[pltpu.VMEM((D, QKV), BF16), pltpu.VMEM((D, QKV), F32)],
        compiler_params=params(48),
        cost_estimate=pl.CostEstimate(
            flops=4 * rows * D * (QKV + D), bytes_accessed=24 << 20, transcendentals=0
        ),
        name="project_back",
    )(dq, dk, dv, cos, sin, nl, xp, d_res, pi, *pieces, gain)


def column_blocks(matrix):
    return matrix.reshape(matrix.shape[0], -1, BW).transpose(1, 0, 2)


def rotate_into(left_side, tile_view, right_side):
    half_turn = jnp.einsum("sba,stbe->stae", left_side, tile_view, precision=lax.Precision.HIGHEST)
    return jnp.einsum("stae,sef->staf", half_turn, right_side, precision=lax.Precision.HIGHEST)


def rotate_back(left_side, tile_view, right_side):
    half_turn = jnp.einsum("sab,stbe->stae", left_side, tile_view, precision=lax.Precision.HIGHEST)
    return jnp.einsum("stae,sfe->staf", half_turn, right_side, precision=lax.Precision.HIGHEST)


def step_of(first_new, second_new):
    return (
        first_new
        / (1.0 - beta_first**STEP)
        / (jnp.sqrt(second_new / (1.0 - beta_second**STEP)) + adam_epsilon)
    )


def rotated_adam(block_grads, block_weights, first_moment, second_moment, basis_left, basis_right, slot_used):
    slot_total = block_grads.shape[0]
    tile_view = block_grads.reshape(slot_total, -1, BW, BW)
    rotated = rotate_into(basis_left, tile_view, basis_right).reshape(block_grads.shape)
    first_new = beta_first * first_moment + (1.0 - beta_first) * rotated
    second_new = beta_second * second_moment + (1.0 - beta_second) * rotated * rotated
    turned = rotate_back(
        basis_left, step_of(first_new, second_new).reshape(slot_total, -1, BW, BW), basis_right
    ).reshape(block_grads.shape)
    updated = block_weights - rate_matrix * (turned + weight_decay * block_weights)
    used = slot_used[:, None, None]
    return (
        jnp.where(used, first_new, 0.0),
        jnp.where(used, second_new, 0.0),
        jnp.where(used, updated, 0.0),
    )


def vector_adam(vectors, grad_vectors, vector_first, vector_second):
    first_new = beta_first * vector_first + (1.0 - beta_first) * grad_vectors
    second_new = beta_second * vector_second + (1.0 - beta_second) * grad_vectors * grad_vectors
    return (second_new, vectors - rate_vector * step_of(first_new, second_new))


def split_two(value):
    high = value.astype(BF16)
    return high, (value - high.astype(F32)).astype(BF16)


def on_device(
    places,
    inputs,
    cotangent,
    starts,
    query_weight,
    key_weight,
    value_weight,
    out_weight,
    gate_weight,
    up_weight,
    down_weight,
    vectors,
    owner_slot,
    first_moment,
    second_moment,
    basis_left,
    basis_right,
    vector_first,
    vector_second,
):
    n_dev, shard_rows = places.n_dev, places.rows
    here = inputs.shape[2]
    seq_index = lax.axis_index("seq")
    vec_here = vectors.shape[0]

    out_t, down_t = out_weight.T, down_weight.T
    attention_low = jnp.concatenate(
        [m.astype(BF16) for m in (query_weight, key_weight, value_weight, out_t)], axis=1
    )
    feed_low = [
        jnp.concatenate(
            [m[:, o : o + w].astype(BF16) for m in (gate_weight, up_weight, down_t)], axis=1
        )
        for o, w in zip(OFFSETS, CHUNKS)
    ]
    vectors_low = lax.all_gather(
        jnp.pad(vectors.astype(BF16), (0, 128 - vec_here)).reshape(1, 128), BOTH, axis=0, tiled=True
    )
    vectors_full = vectors_low[:, :vec_here].reshape(-1)

    natural = places.natural_rows()
    pi = (jnp.arange(D, dtype=jnp.int32)[:, None] == natural[None, :]).astype(BF16)
    gains = jnp.pad(vectors_full[: 2 * D].reshape(2, D), ((0, 6), (0, 0)))
    gains = dot_nn(gains, pi)
    gain_attn, gain_mlp = gains[0:1], gains[1:2]
    bias = vectors_full[2 * D :].astype(F32).reshape(1, QKV)

    attention_pieces = gather_pieces(places, attention_low)
    feed_pieces = [gather_pieces(places, shard) for shard in feed_low]

    spots = seq_index * here + jnp.arange(here, dtype=jnp.int32)
    own_starts = starts[:, 0]
    before = own_starts[:, None, :] <= spots[None, :, None]
    doc_begin = jnp.max(jnp.where(before, own_starts[:, None, :], 0), axis=2)
    relative = (spots[None, :] - doc_begin).astype(F32).reshape(-1)
    frequency = jnp.power(
        rope_theta, -jnp.arange(0, HEAD_SIZE, 2, dtype=F32) / HEAD_SIZE
    )
    angles = relative[:, None] * frequency[None, :]
    cos, sin = jnp.cos(angles), jnp.sin(angles)
    cos = jnp.concatenate([cos] * 4, axis=1)
    sin = jnp.concatenate([-sin, sin, -sin, sin], axis=1)
    begin = doc_begin + here - seq_index * here
    lo = begin[:, ::128] // 128
    begin = begin[:, :, None]

    x = inputs[:, 0].reshape(-1, D)
    cot = cotangent[:, 0].reshape(-1, D)
    cot_p = dot_nn(cot, pi).astype(BF16)
    cot_t = lax.dot_general(
        pi, cot, (((0,), (1,)), ((), ())), preferred_element_type=F32
    ).astype(BF16)

    xp, nl, q, k, v = project(x, pi, attention_pieces, gain_attn, bias, cos, sin)

    forth = [(2 * n, 2 * n + 1) for n in range(n_dev // 2)]
    back = [(2 * n + 1, 2 * n) for n in range(n_dev // 2)]
    kv = send(jnp.concatenate([k, v], axis=1), forth)

    def streams(array):
        return array.reshape(MICRO, here, array.shape[-1])

    heads = (
        lo,
        streams(q),
        streams(kv[:, :KW]),
        streams(k),
        streams(kv[:, KW:]),
        streams(v),
        begin,
    )
    attended, lse = attend(*heads)
    attended_flat = attended.reshape(-1, QW)
    residual, normed, normed_t = middle(attended_flat, xp, attention_pieces, gain_mlp)

    sums = None
    feed_shards = []
    for wide, pieces in zip(CHUNKS, feed_pieces):
        mlp, d_normed, own, other = feed(wide, normed, normed_t, cot_p, cot_t, sums, pieces)
        sums = (mlp, d_normed)
        feed_shards.append(reduce_rows(places, own, other))

    output, d_res, d_att, own_out, other_out, d_gain_mlp = middle_back(
        residual, sums[0], sums[1], cot_p, attended_flat, pi, attention_pieces, gain_mlp
    )
    grad_out_t = reduce_rows(places, own_out, other_out)
    dq, dkv_own, dkv_recv = attend_back(*heads, attended, streams(d_att), lse)
    dkv = (dkv_own + send(dkv_recv, back).astype(F32)).astype(BF16).reshape(-1, 2 * KW)
    input_grad, own_in, other_in, d_gain_attn, d_bias = project_back(
        dq.reshape(-1, QW), dkv[:, :KW], dkv[:, KW:], cos, sin, nl, xp, d_res, pi,
        attention_pieces, gain_attn,
    )

    d_gains = jnp.concatenate([d_gain_attn, d_gain_mlp, jnp.zeros((6, D), F32)], axis=0)
    high, rest = split_two(d_gains)
    d_gains = dot_nt(high, pi) + dot_nt(rest, pi)
    d_vectors = jnp.concatenate([d_gains[0], d_gains[1], d_bias[0]])
    lanes = -(-vec_here // shard_rows)
    d_vectors = jnp.pad(
        d_vectors.reshape(n_dev, vec_here), ((0, 0), (0, lanes * shard_rows - vec_here))
    ).reshape(D, lanes)
    riders = dot_tn(pi, jnp.pad(d_vectors, ((0, 0), (0, 128 - lanes))).astype(BF16)).astype(BF16)
    own_in = jnp.concatenate([own_in, riders[:HALF]], axis=1)
    other_in = jnp.concatenate([other_in, riders[HALF:]], axis=1)
    grad_in = reduce_rows(places, own_in, other_in)
    grad_vectors = grad_in[:, QKV : QKV + lanes].reshape(-1)[:vec_here]

    grad_query, grad_key, grad_value = (
        grad_in[:, :QW],
        grad_in[:, QW : QW + KW],
        grad_in[:, QW + KW : QKV],
    )
    grad_gate, grad_up, grad_down_t = (
        jnp.concatenate(
            [shard[:, m * w : (m + 1) * w] for shard, w in zip(feed_shards, CHUNKS)], axis=1
        )
        for m in range(3)
    )

    grads_all = jnp.concatenate([grad_in[:, :QKV], grad_out_t, grad_gate, grad_up, grad_down_t], axis=1)
    weights_all = jnp.concatenate(
        [query_weight, key_weight, value_weight, out_t, gate_weight, up_weight, down_t], axis=1
    )
    grad_blocks = column_blocks(grads_all.astype(BF16))
    weight_blocks = column_blocks(weights_all.astype(BF16))
    capacity = first_moment.shape[0]
    slot_count = n_dev * capacity
    slot_block = (
        jnp.full((slot_count,), -1, jnp.int32)
        .at[owner_slot]
        .set(jnp.arange(owner_slot.shape[0], dtype=jnp.int32))
    )
    slot_used = slot_block >= 0
    slot_index = jnp.maximum(slot_block, 0)
    owned_grads, owned_weights = (
        lax.all_to_all(
            jnp.take(blocks, slot_index, axis=0), BOTH, split_axis=0, concat_axis=1, tiled=True
        ).astype(F32)
        for blocks in (grad_blocks, weight_blocks)
    )
    local_used = lax.dynamic_slice_in_dim(
        slot_used, lax.axis_index(BOTH) * capacity, capacity, 0
    )
    new_first, new_second, new_blocks = rotated_adam(
        owned_grads, owned_weights, first_moment, second_moment, basis_left, basis_right, local_used
    )
    vector_second_new, vector_new = vector_adam(vectors, grad_vectors, vector_first, vector_second)
    return (
        output.reshape(inputs.shape),
        input_grad.reshape(inputs.shape),
        grad_query,
        grad_key,
        grad_value,
        grad_out_t.T,
        grad_gate,
        grad_up,
        grad_down_t.T,
        grad_vectors,
        new_first,
        new_second,
        new_blocks,
        vector_second_new,
        vector_new,
    )


def solution(mesh):
    rows = P(("dp", "seq"), None)
    columns = P(None, ("dp", "seq"))
    tokens = P(None, "dp", "seq", None)
    slots = P(("dp", "seq"), None, None)
    line = P(("dp", "seq"))
    places = Places(mesh.shape["dp"], mesh.shape["seq"])
    return jax.shard_map(
        functools.partial(on_device, places),
        mesh=mesh,
        in_specs=(
            tokens, tokens, P(None, "dp", None), rows, rows, rows, columns, rows, rows, columns,
            line, P(), slots, slots, slots, slots, line, line,
        ),
        out_specs=(
            tokens, tokens, rows, rows, rows, columns, rows, rows, columns, line,
            slots, slots, slots, line, line,
        ),
        check_vma=False,
    )
```

```python
import functools
import math

import jax
import jax.numpy as jnp
import numpy as np
from jax import lax
from jax.experimental import pallas as pl
from jax.experimental.pallas import tpu as pltpu
from jax.sharding import PartitionSpec as P

D = 896
QUERY_HEADS = 14
KEY_VALUE_HEADS = 2
HEAD_SIZE = 64
BW = 128
MICRO = 2
STEP = 10
QW = 896
KW = 128
QKV = QW + 2 * KW
FF = 4864

norm_epsilon = 1e-06
rope_theta = 1000000.0
beta_first = 0.9
beta_second = 0.999
adam_epsilon = 1e-08
weight_decay = 0.01
rate_matrix = 0.1
rate_vector = 0.5
masked_value = -1e30

F32 = jnp.float32
BF16 = jnp.bfloat16
BOTH = ("dp", "seq")

TILE = 256
CHUNKS = (1280, 1280, 1280, 1024)
OFFSETS = (0, 1280, 2560, 3840)
QUARTER = 112
HALF = 448
TOKEN_TILE = 256

HEAD_SETS = (
    ((0, 1, 2, 3), 0, 0),
    ((0, 1, 2), 1, 0),
    ((3, 4, 5, 6), 1, 1),
    ((4, 5, 6), 0, 1),
)
SET_ROWS = (0, 512, 896, 1408)
ALL_ROWS = 1792


def params(mib, **more):
    return pltpu.CompilerParams(vmem_limit_bytes=mib * 1024 * 1024, **more)


def dot_nn(a, b):
    return lax.dot_general(a, b, (((1,), (0,)), ((), ())), preferred_element_type=F32)


def dot_nt(a, b):
    return lax.dot_general(a, b, (((1,), (1,)), ((), ())), preferred_element_type=F32)


def dot_tn(a, b):
    return lax.dot_general(a, b, (((0,), (0,)), ((), ())), preferred_element_type=F32)


def following(kernel, n_in, after):
    def wrapped(*refs):
        return kernel(*refs[:n_in], *refs[n_in + len(after) :])

    return wrapped


TINY = pl.CostEstimate(flops=1, bytes_accessed=1, transcendentals=0)
ANYWHERE = pl.BlockSpec(memory_space=pl.ANY)


class Places:
    def __init__(self, n_dp, n_seq):
        self.line = n_dp // 4
        self.rows = D // (n_dp * n_seq)
        self.n_dev = n_dp * n_seq

        def pairs(move):
            found = []
            for z in range(self.line):
                for x in range(2):
                    for c in range(2):
                        for y in range(2):
                            tz, tx, tc, ty = move(z, x, c, y)
                            found.append(
                                (((z * 2 + x) * 2 + c) * 2 + y, ((tz * 2 + tx) * 2 + tc) * 2 + ty)
                            )
            return found

        self.sibling = pairs(lambda z, x, c, y: (z, x, 1 - c, y))
        self.long = pairs(lambda z, x, c, y: (z, 1 - x, c, y) if c == 0 else (z, x, c, 1 - y))
        self.short = pairs(lambda z, x, c, y: (z, 1 - x, c, y) if c == 1 else (z, x, c, 1 - y))
        self.ahead = [
            pairs(lambda z, x, c, y, k=k: ((z + k) % self.line, x, c, y)) for k in range(self.line)
        ]

    def natural_rows(self):
        dp = lax.axis_index("dp")
        y = lax.axis_index("seq")
        z, x, c = dp // 4, (dp // 2) % 2, dp % 2
        place = jnp.arange(D, dtype=jnp.int32)
        dc, da, db = place // HALF, (place // (2 * QUARTER)) % 2, (place // QUARTER) % 2
        dz, inner = (place % QUARTER) // self.rows, place % self.rows
        c_own = c ^ dc
        x_own = x ^ jnp.where(c_own == 0, da, db)
        y_own = y ^ jnp.where(c_own == 0, db, da)
        z_own = (z + dz) % self.line
        return self.rows * (((z_own * 2 + x_own) * 2 + c_own) * 2 + y_own) + inner


def send(array, pairs):
    return lax.ppermute(array, BOTH, pairs)


def line_parts(places, shard):
    return [shard] + [send(shard, places.ahead[-k % places.line]) for k in range(1, places.line)]


def stack_kernel(count, *refs):
    ins, (out, scr) = refs[:count], refs[count:]
    rows = ins[0].shape[1]
    for k, ref in enumerate(ins):
        scr[rows * k : rows * (k + 1), :] = ref[0].astype(F32)
    out[0] = scr[...].astype(BF16)


def stacked_rows(parts, after=()):
    pages, rows, width = parts[0].shape
    return pl.pallas_call(
        following(functools.partial(stack_kernel, len(parts)), len(parts), after),
        grid=(pages,),
        in_specs=[pl.BlockSpec((1, rows, width), lambda m: (m, 0, 0))] * len(parts)
        + [ANYWHERE] * len(after),
        out_specs=pl.BlockSpec((1, QUARTER, width), lambda m: (m, 0, 0)),
        out_shape=jax.ShapeDtypeStruct((pages, QUARTER, width), BF16),
        scratch_shapes=[pltpu.VMEM((QUARTER, width), F32)],
        compiler_params=params(32),
        cost_estimate=TINY,
        name="stacked_rows",
    )(*parts, *after)


def neighbours():
    dp, seq = lax.axis_index("dp"), lax.axis_index("seq")
    core = lax.rem(dp, 2)
    first = dp + 2 - 4 * lax.rem(dp // 2, 2)
    sibling = (dp + 1 - 2 * core, seq)
    long = (jnp.where(core == 0, first, dp), jnp.where(core == 0, seq, 1 - seq))
    short = (jnp.where(core == 0, dp, first), jnp.where(core == 0, 1 - seq, seq))
    return sibling, long, short


def greet(devices):
    barrier = pltpu.get_barrier_semaphore()
    for device in devices:
        pl.semaphore_signal(barrier, inc=1, device_id=device, device_id_type=pl.DeviceIdType.MESH)
    pl.semaphore_wait(barrier, len(devices))


def push(src, dst, sems, n, device):
    return pltpu.make_async_remote_copy(
        src_ref=src,
        dst_ref=dst,
        send_sem=sems.at[0, n],
        recv_sem=sems.at[1, n],
        device_id=device,
        device_id_type=pl.DeviceIdType.MESH,
    )


def quarter(ref, k):
    return ref.at[:, pl.ds(QUARTER * k, QUARTER), :]


def spread_kernel(own, out, sems, here_sem):
    sibling, long, short = neighbours()
    greet((sibling, long, short))
    here = pltpu.make_async_copy(own, quarter(out, 0), here_sem)
    moves = [
        push(own, quarter(out, 1), sems, 0, short),
        push(own, quarter(out, 2), sems, 1, long),
        push(own, quarter(out, 4), sems, 2, sibling),
    ]
    here.start()
    for move in moves:
        move.start()
    for k, first in ((1, 3), (2, None), (3, None)):
        moves[{1: 0, 2: 1, 3: 3}[k]].wait_recv()
        if first is not None:
            moves.append(push(quarter(out, 1), quarter(out, 3), sems, 3, long))
            moves[-1].start()
        moves.append(push(quarter(out, k), quarter(out, 4 + k), sems, 3 + k, sibling))
        moves[-1].start()
    here.wait()
    for n, move in enumerate(moves):
        move.wait_send()
        if n not in (0, 1, 3):
            move.wait_recv()


def spread(own, after=()):
    return pl.pallas_call(
        following(spread_kernel, 1, after),
        in_specs=[ANYWHERE] * (1 + len(after)),
        out_specs=ANYWHERE,
        out_shape=jax.ShapeDtypeStruct((1, D, own.shape[2]), BF16),
        scratch_shapes=[pltpu.SemaphoreType.DMA((2, 7)), pltpu.SemaphoreType.DMA],
        compiler_params=params(60, collective_id=8, has_side_effects=True),
        cost_estimate=TINY,
        name="spread",
    )(own, *after)


def fold_kernel(count, *refs):
    total = refs[0][...].astype(F32)
    for ref in refs[1:count]:
        total = total + ref[...].astype(F32)
    refs[count][...] = total.astype(BF16)


def fold(terms, rows, after=()):
    pages, _, width = terms[0][0].shape

    def spec(block):
        return pl.BlockSpec((1, rows, width), lambda m: (m, block, 0))

    return pl.pallas_call(
        following(functools.partial(fold_kernel, len(terms)), len(terms), after),
        grid=(pages,),
        in_specs=[spec(block) for _, block in terms] + [ANYWHERE] * len(after),
        out_specs=spec(0),
        out_shape=jax.ShapeDtypeStruct((pages, rows, width), BF16),
        compiler_params=params(32),
        cost_estimate=TINY,
        name="fold",
    )(*[array for array, _ in terms], *after)


def share_kernel(count, rows, *refs):
    scr = refs[-1]
    outs = refs[count:-1]
    total = refs[0][0].astype(F32)
    for ref in refs[1:count]:
        total = total + ref[0].astype(F32)
    scr[...] = total
    for k, ref in enumerate(outs):
        ref[0] = scr[rows * k : rows * (k + 1), :].astype(ref.dtype)


def share(terms, rows, line, after=()):
    pages, _, width = terms[0].shape
    part = pl.BlockSpec((1, rows, width), lambda m: (m, 0, 0))
    return pl.pallas_call(
        following(functools.partial(share_kernel, len(terms), rows), len(terms), after),
        grid=(pages,),
        in_specs=[pl.BlockSpec((1, QUARTER, width), lambda m: (m, 0, 0))] * len(terms)
        + [ANYWHERE] * len(after),
        out_specs=[part] * line,
        out_shape=[
            jax.ShapeDtypeStruct((pages, rows, width), F32 if k == 0 else BF16) for k in range(line)
        ],
        scratch_shapes=[pltpu.VMEM((QUARTER, width), F32)],
        compiler_params=params(32),
        cost_estimate=TINY,
        name="share",
    )(*terms, *after)


class Reduce:
    def __init__(self, places, terms, passed=None):
        self.places, self.terms, self.passed = places, terms, passed

    def second_step(self, after=()):
        operand = self.passed
        if operand is None:
            operand = fold([(t, 1) for t in self.terms], 2 * QUARTER, after)
        self.terms = self.terms + [send(operand, self.places.long)]
        return operand

    def third_step(self, after=()):
        operand = fold([(t, 1) for t in self.terms], QUARTER, after)
        self.terms = self.terms + [send(operand, self.places.short)]
        return operand

    def last_step(self, after=()):
        mine, *parts = share(self.terms, self.places.rows, self.places.line, after)
        self.parts = [mine] + [
            send(part, self.places.ahead[k + 1]) for k, part in enumerate(parts)
        ]
        return mine


def round_kernel(spans, *refs):
    ins, out = refs[:-1], refs[-1]
    at = [0] * out.shape[0]
    for page, which, offset, width in spans:
        out[page, :, at[page] : at[page] + width] = ins[which][:, offset : offset + width].astype(BF16)
        at[page] += width


def rounded(parts, spans, after=()):
    rows, pages = parts[0].shape[0], 1 + max(page for page, _, _, _ in spans)
    width = sum(width for page, _, _, width in spans if page == 0)
    return pl.pallas_call(
        following(functools.partial(round_kernel, spans), len(parts), after),
        in_specs=[pl.BlockSpec(memory_space=pltpu.VMEM)] * len(parts) + [ANYWHERE] * len(after),
        out_specs=pl.BlockSpec(memory_space=pltpu.VMEM),
        out_shape=jax.ShapeDtypeStruct((pages, rows, width), BF16),
        compiler_params=params(32),
        cost_estimate=TINY,
        name="rounded",
    )(*parts, *after)


def swap_halves(tile, low_half):
    return jnp.where(low_half, pltpu.roll(tile, 96, 1), pltpu.roll(tile, 32, 1))


def project_kernel(x_ref, pi_ref, *refs):
    w_ref, gain_ref, bias_ref, cos_ref, sin_ref, xp_ref, nl_ref, q_ref, k_ref, v_ref = refs
    xp = dot_nn(x_ref[...], pi_ref[...])
    inv = lax.rsqrt(jnp.sum(xp * xp, axis=1, keepdims=True) * (1.0 / D) + norm_epsilon)
    nl = (xp * inv * gain_ref[...]).astype(BF16)
    xp_ref[...] = xp.astype(BF16)
    nl_ref[...] = nl
    lin = dot_nn(nl, w_ref[:, :QKV]) + bias_ref[...]
    cos, sin = cos_ref[...], sin_ref[...]
    low = lax.broadcasted_iota(jnp.int32, cos.shape, 1) % HEAD_SIZE < HEAD_SIZE // 2
    for t in range(8):
        piece = lin[:, 128 * t : 128 * (t + 1)]
        turned = (piece * cos + swap_halves(piece, low) * sin).astype(BF16)
        if t < 7:
            q_ref[:, 128 * t : 128 * (t + 1)] = (turned.astype(F32) * 0.125).astype(BF16)
        else:
            k_ref[...] = turned
    v_ref[...] = lin[:, QW + KW :].astype(BF16)


def project(x, pi, weights, gain, bias, cos, sin, after=()):
    rows = x.shape[0]
    width = weights.shape[1]

    def tile(cols):
        return pl.BlockSpec((TOKEN_TILE, cols), lambda t: (t, 0))

    def whole(r, c):
        return pl.BlockSpec((r, c), lambda t: (0, 0))

    shapes = [(D, BF16), (D, BF16), (QW, BF16), (KW, BF16), (KW, BF16)]
    return pl.pallas_call(
        following(project_kernel, 7, after),
        grid=(rows // TOKEN_TILE,),
        in_specs=[tile(D), whole(D, D)]
        + [whole(D, width)]
        + [whole(1, D), whole(1, QKV), tile(128), tile(128)]
        + [ANYWHERE] * len(after),
        out_specs=[tile(c) for c, _ in shapes],
        out_shape=[jax.ShapeDtypeStruct((rows, c), t) for c, t in shapes],
        compiler_params=params(56),
        cost_estimate=TINY,
        name="project",
    )(x, pi, weights, gain, bias, cos, sin, *after)


def padded_heads(recv, own, out):
    lane = lax.broadcasted_iota(jnp.int32, (512, 128), 1)
    for part, ref in enumerate((recv, own)):
        if ref is None:
            continue
        natural = ref[0].astype(F32)
        crossed = pltpu.roll(natural, 64, 1)
        rows = pl.ds(512 * part, 512)
        for s, (_, half, head) in enumerate(HEAD_SETS):
            source = natural if half == head else crossed
            keep = (lane >= 64) if half else (lane < 64)
            out[s, rows, :] = jnp.where(keep, source, 0.0).astype(BF16)


def block_bias(kb, i, begin):
    shape = (128, 128)
    key = kb * 128 + lax.broadcasted_iota(jnp.int32, shape, 1)
    query = 512 + i * 128 + lax.broadcasted_iota(jnp.int32, shape, 0)
    return jnp.where((key >= begin) & (key <= query), 0.0, masked_value)


def stacked(tile_of, pairs):
    return jnp.concatenate([tile_of(p) for p in pairs], axis=0)


def attend_kernel(
    lo_ref, q_ref, kr_ref, ko_ref, vr_ref, vo_ref, ds_ref, o_ref, lse_ref, kp, vp, s_scr, m_scr, l_scr, acc
):
    b, i = pl.program_id(0), pl.program_id(1)

    @pl.when(i == 0)
    def _():
        padded_heads(kr_ref, ko_ref, kp)
        padded_heads(vr_ref, vo_ref, vp)

    lo, hi = lo_ref[b, i], i + 5
    begin = ds_ref[0]
    m_scr[...] = jnp.full(m_scr.shape, masked_value, F32)
    l_scr[...] = jnp.zeros(l_scr.shape, F32)
    acc[...] = jnp.zeros(acc.shape, F32)

    def scores(kb, carry):
        bias = block_bias(kb, i, begin)
        keys = pl.ds(pl.multiple_of(kb * 128, 128), 128)
        for s, (pairs, _, _) in enumerate(HEAD_SETS):
            x = stacked(lambda p: q_ref[0, :, 128 * p : 128 * (p + 1)], pairs)
            raw = dot_nt(x, kp[s, keys, :])
            for n in range(len(pairs)):
                rows = slice(SET_ROWS[s] + 128 * n, SET_ROWS[s] + 128 * (n + 1))
                value = raw[128 * n : 128 * (n + 1)] + bias
                s_scr[kb, rows, :] = value
                m_scr[rows, :] = jnp.maximum(m_scr[rows, :], value)
        return carry

    lax.fori_loop(lo, hi, scores, 0)
    top = jnp.max(m_scr[...], axis=1, keepdims=True)
    m_scr[...] = jnp.broadcast_to(top, m_scr.shape)

    def weigh(kb, carry):
        keys = pl.ds(pl.multiple_of(kb * 128, 128), 128)
        for s, (pairs, _, _) in enumerate(HEAD_SETS):
            rows = slice(SET_ROWS[s], SET_ROWS[s] + 128 * len(pairs))
            p = jnp.exp(s_scr[kb, rows, :] - m_scr[rows, :])
            l_scr[rows, :] += p
            acc[rows, :] += dot_nn(p.astype(BF16), vp[s, keys, :])
        return carry

    lax.fori_loop(lo, hi, weigh, 0)
    total = jnp.sum(l_scr[...], axis=1, keepdims=True)
    lse = m_scr[:, :1] + jnp.log(total)
    share = 1.0 / total
    lane = lax.broadcasted_iota(jnp.int32, (128, 128), 1)
    lanes = jnp.zeros((128, 128), F32)
    outs = [None] * 7
    for s, (pairs, half, _) in enumerate(HEAD_SETS):
        for n, p in enumerate(pairs):
            rows = slice(SET_ROWS[s] + 128 * n, SET_ROWS[s] + 128 * (n + 1))
            part = acc[rows, :] * share[rows]
            outs[p] = part if outs[p] is None else outs[p] + part
            lanes = jnp.where(lane == 2 * p + half, lse[rows], lanes)
    for p in range(7):
        o_ref[0, :, 128 * p : 128 * (p + 1)] = outs[p].astype(BF16)
    lse_ref[0] = lanes


def attend_specs():
    def block(cols):
        return pl.BlockSpec((1, 128, cols), lambda b, i, lo: (b, i, 0))

    def stream(cols):
        return pl.BlockSpec((1, 512, cols), lambda b, i, lo: (b, 0, 0))

    return block, stream


def attend(lo, q, k_recv, k_own, v_recv, v_own, begin, after=()):
    block, stream = attend_specs()
    return pl.pallas_call(
        following(attend_kernel, 7, after),
        grid_spec=pltpu.PrefetchScalarGridSpec(
            num_scalar_prefetch=1,
            grid=(MICRO, 4),
            in_specs=[block(QW)] + [stream(KW)] * 4 + [block(1)] + [ANYWHERE] * len(after),
            out_specs=[block(QW), block(128)],
            scratch_shapes=[
                pltpu.VMEM((4, 1024, 128), BF16),
                pltpu.VMEM((4, 1024, 128), BF16),
                pltpu.VMEM((8, ALL_ROWS, 128), F32),
                pltpu.VMEM((ALL_ROWS, 128), F32),
                pltpu.VMEM((ALL_ROWS, 128), F32),
                pltpu.VMEM((ALL_ROWS, 128), F32),
            ],
        ),
        out_shape=[
            jax.ShapeDtypeStruct((MICRO, 512, QW), BF16),
            jax.ShapeDtypeStruct((MICRO, 512, 128), F32),
        ],
        compiler_params=params(56),
        cost_estimate=TINY,
        name="attend",
    )(lo, q, k_recv, k_own, v_recv, v_own, begin, *after)


def attend_back_kernel(
    lo_ref, q_ref, kr_ref, ko_ref, vr_ref, vo_ref, ds_ref, o_ref, do_ref, lse_ref,
    dq_ref, own_ref, recv_ref, kp, vp, dk, dv, dq_acc,
):
    b, i = pl.program_id(0), pl.program_id(1)

    @pl.when(i == 0)
    def _():
        padded_heads(kr_ref, ko_ref, kp)
        padded_heads(vr_ref, vo_ref, vp)
        dk[...] = jnp.zeros(dk.shape, F32)
        dv[...] = jnp.zeros(dv.shape, F32)

    lo, hi = lo_ref[b, i], i + 5
    begin = ds_ref[0]
    lane = lax.broadcasted_iota(jnp.int32, (128, 128), 1)
    dq_acc[...] = jnp.zeros(dq_acc.shape, F32)
    lse_all = lse_ref[0]
    lse, dots = [], []
    for s, (pairs, half, _) in enumerate(HEAD_SETS):
        for p in pairs:
            cols = slice(128 * p, 128 * (p + 1))
            product = o_ref[0, :, cols].astype(F32) * do_ref[0, :, cols].astype(F32)
            keep = (lane >= 64) if half else (lane < 64)
            dots.append(jnp.sum(jnp.where(keep, product, 0.0), axis=1, keepdims=True))
            head = 2 * p + half
            lse.append(lse_all[:, head : head + 1])

    def one_block(kb, carry):
        bias = block_bias(kb, i, begin)
        keys = pl.ds(pl.multiple_of(kb * 128, 128), 128)
        at = 0
        for s, (pairs, _, _) in enumerate(HEAD_SETS):
            x = stacked(lambda p: q_ref[0, :, 128 * p : 128 * (p + 1)], pairs)
            y = stacked(lambda p: do_ref[0, :, 128 * p : 128 * (p + 1)], pairs)
            raw = dot_nt(x, kp[s, keys, :])
            d_prob = dot_nt(y, vp[s, keys, :])
            probs, d_scores = [], []
            for n in range(len(pairs)):
                rows = slice(128 * n, 128 * (n + 1))
                p = jnp.exp(raw[rows] + bias - lse[at + n])
                probs.append(p.astype(BF16))
                d_scores.append((p * (d_prob[rows] - dots[at + n])).astype(BF16))
            at += len(pairs)
            prob = jnp.concatenate(probs, axis=0)
            d_score = jnp.concatenate(d_scores, axis=0)
            d_query = dot_nn(d_score, kp[s, keys, :])
            for n, p in enumerate(pairs):
                dq_acc[p] += d_query[128 * n : 128 * (n + 1)]
            dk[s, keys, :] += dot_tn(d_score, x)
            dv[s, keys, :] += dot_tn(prob, y)
        return carry

    lax.fori_loop(lo, hi, one_block, 0)
    for p in range(7):
        dq_ref[0, :, 128 * p : 128 * (p + 1)] = (dq_acc[p] * 0.125).astype(BF16)

    @pl.when(i == 3)
    def _():
        wide = lax.broadcasted_iota(jnp.int32, (512, 128), 1) < 64
        for part, ref in enumerate((recv_ref, own_ref)):
            rows = pl.ds(512 * part, 512)
            for n, grads in enumerate((dk, dv)):
                low = grads[0, rows, :] + pltpu.roll(grads[1, rows, :], 64, 1)
                high = grads[2, rows, :] + pltpu.roll(grads[3, rows, :], 64, 1)
                value = jnp.where(wide, low, high)
                ref[0, :, 128 * n : 128 * (n + 1)] = value.astype(ref.dtype)


def attend_back(lo, q, k_recv, k_own, v_recv, v_own, begin, out, d_out, lse, after=()):
    block, stream = attend_specs()
    return pl.pallas_call(
        following(attend_back_kernel, 10, after),
        grid_spec=pltpu.PrefetchScalarGridSpec(
            num_scalar_prefetch=1,
            grid=(MICRO, 4),
            in_specs=[block(QW)]
            + [stream(KW)] * 4
            + [block(1), block(QW), block(QW), block(128)]
            + [ANYWHERE] * len(after),
            out_specs=[block(QW), stream(256), stream(256)],
            scratch_shapes=[
                pltpu.VMEM((4, 1024, 128), BF16),
                pltpu.VMEM((4, 1024, 128), BF16),
                pltpu.VMEM((4, 1024, 128), F32),
                pltpu.VMEM((4, 1024, 128), F32),
                pltpu.VMEM((7, 128, 128), F32),
            ],
        ),
        out_shape=[
            jax.ShapeDtypeStruct((MICRO, 512, QW), BF16),
            jax.ShapeDtypeStruct((MICRO, 512, 256), F32),
            jax.ShapeDtypeStruct((MICRO, 512, 256), BF16),
        ],
        compiler_params=params(56),
        cost_estimate=TINY,
        name="attend_back",
    )(lo, q, k_recv, k_own, v_recv, v_own, begin, out, d_out, lse, *after)


def middle_kernel(att_ref, xp_ref, *refs):
    w_ref, gain_ref, res_ref, n_ref, nt_ref = refs
    residual = xp_ref[...].astype(F32) + dot_nt(att_ref[...], w_ref[:, QKV : QKV + QW])
    inv = lax.rsqrt(jnp.sum(residual * residual, axis=1, keepdims=True) * (1.0 / D) + norm_epsilon)
    normed = residual * inv * gain_ref[...]
    res_ref[...] = residual
    n_ref[...] = normed.astype(BF16)
    nt_ref[...] = normed.T.astype(BF16)


def middle(attended, xp, weights, gain, after=()):
    rows = xp.shape[0]
    width = weights.shape[1]

    def tile(cols):
        return pl.BlockSpec((TOKEN_TILE, cols), lambda t: (t, 0))

    def whole(r, c):
        return pl.BlockSpec((r, c), lambda t: (0, 0))

    return pl.pallas_call(
        following(middle_kernel, 4, after),
        grid=(rows // TOKEN_TILE,),
        in_specs=[tile(QW), tile(D)]
        + [whole(D, width)]
        + [whole(1, D)]
        + [ANYWHERE] * len(after),
        out_specs=[tile(D), tile(D), pl.BlockSpec((D, TOKEN_TILE), lambda t: (0, t))],
        out_shape=[
            jax.ShapeDtypeStruct((rows, D), F32),
            jax.ShapeDtypeStruct((rows, D), BF16),
            jax.ShapeDtypeStruct((D, rows), BF16),
        ],
        compiler_params=params(56),
        cost_estimate=TINY,
        name="middle",
    )(attended, xp, weights, gain, *after)


def middle_back_kernel(res_ref, mlp_ref, dn_ref, cot_ref, att_ref, pi_ref, *refs):
    w_ref, gain_ref, out_ref, dres_ref, datt_ref, own_ref, sib_ref, dgain_ref, g_scr = refs
    t = pl.program_id(0)

    @pl.when(t == 0)
    def _():
        g_scr[...] = jnp.zeros(g_scr.shape, F32)
        dgain_ref[...] = jnp.zeros(dgain_ref.shape, F32)

    residual = res_ref[...]
    inv = lax.rsqrt(jnp.sum(residual * residual, axis=1, keepdims=True) * (1.0 / D) + norm_epsilon)
    out_low = (residual + mlp_ref[...]).astype(BF16)
    out_ref[...] = dot_nt(out_low, pi_ref[...]).astype(BF16)
    d_normed = dn_ref[...]
    hat = residual * inv
    scaled = d_normed * gain_ref[...]
    dgain_ref[...] += jnp.sum(d_normed * hat, axis=0, keepdims=True)
    mean = jnp.sum(scaled * hat, axis=1, keepdims=True) * (1.0 / D)
    d_res = cot_ref[...].astype(F32) + inv * (scaled - hat * mean)
    dres_ref[...] = d_res
    low = d_res.astype(BF16)
    datt_ref[...] = dot_nn(low, w_ref[:, QKV : QKV + QW]).astype(BF16)
    g_scr[...] += dot_tn(low, att_ref[...])

    @pl.when(t == pl.num_programs(0) - 1)
    def _():
        own_ref[...] = g_scr[:HALF].astype(BF16)
        sib_ref[...] = g_scr[HALF:].astype(BF16)


def middle_back(residual, mlp, d_normed, cot, attended, pi, weights, gain, after=()):
    rows = residual.shape[0]
    width = weights.shape[1]

    def tile(cols):
        return pl.BlockSpec((TOKEN_TILE, cols), lambda t: (t, 0))

    def whole(r, c):
        return pl.BlockSpec((r, c), lambda t: (0, 0))

    return pl.pallas_call(
        following(middle_back_kernel, 8, after),
        grid=(rows // TOKEN_TILE,),
        in_specs=[tile(D)] * 4
        + [tile(QW), whole(D, D)]
        + [whole(D, width)]
        + [whole(1, D)]
        + [ANYWHERE] * len(after),
        out_specs=[tile(D), tile(D), tile(QW), whole(HALF, QW), whole(HALF, QW), whole(1, D)],
        out_shape=[
            jax.ShapeDtypeStruct((rows, D), BF16),
            jax.ShapeDtypeStruct((rows, D), F32),
            jax.ShapeDtypeStruct((rows, QW), BF16),
            jax.ShapeDtypeStruct((HALF, QW), BF16),
            jax.ShapeDtypeStruct((HALF, QW), BF16),
            jax.ShapeDtypeStruct((1, D), F32),
        ],
        scratch_shapes=[pltpu.VMEM((D, QW), F32)],
        compiler_params=params(56),
        cost_estimate=TINY,
        name="middle_back",
    )(residual, mlp, d_normed, cot, attended, pi, weights, gain, *after)


def feed_kernel(wide, started, n_pieces, coming, *refs):
    n_in = 4 + (2 if started else 0)
    n_hbm, nt_hbm, cot_hbm, cott_hbm = refs[:4]
    sums_in = refs[4:n_in]
    pieces = refs[n_in : n_in + n_pieces]
    n_in += n_pieces
    if coming:
        line_hbm = refs[n_in]
        n_in += 1
    mlp_hbm, dn_hbm, keep_hbm, pass_hbm, far_hbm = refs[n_in : n_in + 5]
    n_in += 5
    if coming:
        next_hbm = refs[n_in]
        n_in += 1
    (
        n_v, nt_v, cot_v, cott_v, w_v, mlp_v, dn_v, act_v, grad_v, came_v,
        in_sem, w_sem, w_send, w_recv, out_sem, g_sem, g_send, g_recv, next_sem, next_here,
    ) = refs[n_in:]
    rows_all = n_v.shape[0]
    steps = wide // TILE
    span = 512
    parts = rows_all // span
    sibling, long, short = neighbours()
    mesh_id = pl.DeviceIdType.MESH
    share_rows = HALF // n_pieces

    def tile_of(j):
        return pl.ds(pl.multiple_of(j * TILE, TILE), TILE)

    def weight_copy(k, j):
        return pltpu.make_async_copy(
            pieces[k].at[:, :, tile_of(j)],
            w_v.at[:, pl.ds(share_rows * k, share_rows), tile_of(j)],
            w_sem.at[k, j],
        )

    def weight_push(k, j):
        return pltpu.make_async_remote_copy(
            src_ref=pieces[k].at[:, :, tile_of(j)],
            dst_ref=w_v.at[:, pl.ds(HALF + share_rows * k, share_rows), tile_of(j)],
            send_sem=w_send.at[k, j],
            recv_sem=w_recv.at[k, j],
            device_id=sibling,
            device_id_type=mesh_id,
        )

    def gradient_push(j):
        return pltpu.make_async_remote_copy(
            src_ref=grad_v.at[:, pl.ds(HALF, HALF), tile_of(j)],
            dst_ref=came_v.at[:, :, tile_of(j)],
            send_sem=g_send.at[j],
            recv_sem=g_recv.at[j],
            device_id=sibling,
            device_id_type=mesh_id,
        )

    def sum_copies(j):
        return [
            pltpu.make_async_copy(
                grad_v.at[:, pl.ds(2 * QUARTER * h, 2 * QUARTER), tile_of(j)],
                hbm.at[:, :, tile_of(j)],
                g_sem.at[j, h],
            )
            for h, hbm in enumerate((keep_hbm, pass_hbm))
        ]

    def add_sibling(j):
        cols = tile_of(j)
        gradient_push(j).wait_recv()
        for m in range(3):
            total = grad_v[m, :HALF, cols].astype(F32) + came_v[m, :, cols].astype(F32)
            grad_v[m, :HALF, cols] = total.astype(BF16)
        for copy in sum_copies(j):
            copy.start()

    def span_of(part):
        return pl.ds(part * span, span)

    loads = [
        pltpu.make_async_copy(src, dst, in_sem.at[n])
        for n, (src, dst) in enumerate(
            [(n_hbm, n_v), (cot_hbm, cot_v), (nt_hbm, nt_v), (cott_hbm, cott_v)]
            + ([(sums_in[0], mlp_v), (sums_in[1], dn_v)] if started else [])
        )
    ]
    loads[0].start()
    greet((sibling, long, short) if coming else (sibling,))

    def fetch(j, carry):
        for k in range(n_pieces):
            weight_copy(k, j).start()
            weight_push(k, j).start()
        return carry

    fetch(0, 0)
    for copy in loads[1:4]:
        copy.start()
    lax.fori_loop(1, steps, fetch, 0)
    for copy in loads[4:]:
        copy.start()
    if coming:
        at, width = coming
        line = line_hbm.at[:, :, pl.ds(at, width)]
        line_copy = pltpu.make_async_copy(line, quarter(next_hbm, 0), next_here)
        moves = [
            push(line, quarter(next_hbm, 1), next_sem, 0, short),
            push(line, quarter(next_hbm, 2), next_sem, 1, long),
            push(quarter(next_hbm, 1), quarter(next_hbm, 3), next_sem, 2, long),
        ]
        line_copy.start()
        moves[0].start()
        moves[1].start()

    for copy in loads[:4]:
        copy.wait()

    def columns(j, carry):
        for k in range(n_pieces):
            weight_copy(k, j).wait()
            weight_push(k, j).wait_recv()
        cols = tile_of(j)
        for part in range(parts):
            rows = span_of(part)
            normed = n_v[rows, :]
            gate = dot_nn(normed, w_v[0, :, cols])
            up = dot_nn(normed, w_v[1, :, cols])
            d_hidden = dot_nn(cot_v[rows, :], w_v[2, :, cols])
            s = 1.0 / (1.0 + jnp.exp(-gate))
            silu = gate * s
            act_v[2, rows, cols] = (silu * up).astype(BF16)
            act_v[0, rows, cols] = (d_hidden * up * s * (1.0 + gate * (1.0 - s))).astype(BF16)
            act_v[1, rows, cols] = (d_hidden * silu).astype(BF16)
        for m, left in ((2, cott_v), (0, nt_v), (1, nt_v)):
            grad_v[m, :, cols] = dot_nn(left[...], act_v[m, :, cols]).astype(BF16)
        gradient_push(j).start()

        @pl.when(j > 0)
        def _():
            add_sibling(j - 1)

        return carry

    lax.fori_loop(0, steps, columns, 0)
    stores = [pltpu.make_async_copy(w_v.at[:, pl.ds(HALF, HALF), :], far_hbm, out_sem.at[parts, 0])]
    stores[0].start()
    if coming:
        moves[0].wait_recv()
        moves[2].start()
    for copy in loads[4:]:
        copy.wait()
    for part in range(parts):
        rows = span_of(part)
        for k in range(2):
            if k == 0:
                total, ref, hbm = dot_nt(act_v[2, rows, :], w_v[2]), mlp_v, mlp_hbm
            else:
                total = dot_nt(act_v[0, rows, :], w_v[0]) + dot_nt(act_v[1, rows, :], w_v[1])
                ref, hbm = dn_v, dn_hbm
            ref[rows, :] = total + ref[rows, :] if started else total
            if part == 0 and k == 0:
                add_sibling(steps - 1)
            stores.append(
                pltpu.make_async_copy(ref.at[rows, :], hbm.at[rows, :], out_sem.at[part, k])
            )
            stores[-1].start()

    def settle(j, carry):
        for k in range(n_pieces):
            weight_push(k, j).wait_send()
        gradient_push(j).wait_send()
        for copy in sum_copies(j):
            copy.wait()
        return carry

    lax.fori_loop(0, steps, settle, 0)
    for copy in stores:
        copy.wait()
    if coming:
        line_copy.wait()
        moves[0].wait_send()
        moves[1].wait()
        moves[2].wait()


def feed(number, wide, normed, normed_t, cot, cot_t, sums, pieces, line=None, coming=None, after=()):
    rows = normed.shape[0]
    started = sums is not None
    extra = (list(sums) if started else []) + list(pieces) + ([line] if coming else [])
    n_in = 4 + len(extra)
    steps = wide // TILE
    half = jax.ShapeDtypeStruct((3, HALF, wide), BF16)
    two_quarters = jax.ShapeDtypeStruct((3, 2 * QUARTER, wide), BF16)
    return pl.pallas_call(
        following(functools.partial(feed_kernel, wide, started, len(pieces), coming), n_in, after),
        in_specs=[ANYWHERE] * (n_in + len(after)),
        out_specs=[ANYWHERE] * (6 if coming else 5),
        out_shape=[
            jax.ShapeDtypeStruct((rows, D), F32),
            jax.ShapeDtypeStruct((rows, D), F32),
            two_quarters,
            two_quarters,
            half,
        ]
        + ([jax.ShapeDtypeStruct((3, HALF, coming[1]), BF16)] if coming else []),
        scratch_shapes=[
            pltpu.VMEM((rows, D), BF16),
            pltpu.VMEM((D, rows), BF16),
            pltpu.VMEM((rows, D), BF16),
            pltpu.VMEM((D, rows), BF16),
            pltpu.VMEM((3, D, wide), BF16),
            pltpu.VMEM((rows, D), F32),
            pltpu.VMEM((rows, D), F32),
            pltpu.VMEM((3, rows, wide), BF16),
            pltpu.VMEM((3, D, wide), BF16),
            pltpu.VMEM((3, HALF, wide), BF16),
            pltpu.SemaphoreType.DMA((6,)),
            pltpu.SemaphoreType.DMA((len(pieces), steps)),
            pltpu.SemaphoreType.DMA((len(pieces), steps)),
            pltpu.SemaphoreType.DMA((len(pieces), steps)),
            pltpu.SemaphoreType.DMA((3, 2)),
            pltpu.SemaphoreType.DMA((steps, 2)),
            pltpu.SemaphoreType.DMA((steps,)),
            pltpu.SemaphoreType.DMA((steps,)),
            pltpu.SemaphoreType.DMA((2, 3)),
            pltpu.SemaphoreType.DMA,
        ],
        compiler_params=params(56, collective_id=number, has_side_effects=True),
        cost_estimate=TINY,
        name="feed",
    )(normed, normed_t, cot, cot_t, *extra, *after)


def project_back_kernel(dq_ref, own_kv_ref, recv_kv_ref, cos_ref, sin_ref, nl_ref, xp_ref, dres_ref, pi_ref, *refs):
    w_ref, gain_ref, ig_ref, own_ref, sib_ref, dgain_ref, dbias_ref, g_scr = refs
    t = pl.program_id(0)

    @pl.when(t == 0)
    def _():
        g_scr[...] = jnp.zeros(g_scr.shape, F32)
        dgain_ref[...] = jnp.zeros(dgain_ref.shape, F32)
        dbias_ref[...] = jnp.zeros(dbias_ref.shape, F32)

    cos, sin = cos_ref[...], sin_ref[...]
    low = lax.broadcasted_iota(jnp.int32, cos.shape, 1) % HEAD_SIZE < HEAD_SIZE // 2
    parts = []
    dkv = (own_kv_ref[...] + recv_kv_ref[...].astype(F32)).astype(BF16)
    for n in range(8):
        piece = (dq_ref[:, 128 * n : 128 * (n + 1)] if n < 7 else dkv[:, :KW]).astype(F32)
        parts.append((piece * cos - swap_halves(piece, low) * sin).astype(BF16))
    parts.append(dkv[:, KW:])
    d_lin = jnp.concatenate(parts, axis=1)
    dbias_ref[...] += jnp.sum(d_lin.astype(F32), axis=0, keepdims=True)
    d_normed = dot_nt(d_lin, w_ref[:, :QKV])
    xp = xp_ref[...].astype(F32)
    inv = lax.rsqrt(jnp.sum(xp * xp, axis=1, keepdims=True) * (1.0 / D) + norm_epsilon)
    hat = xp * inv
    scaled = d_normed * gain_ref[...]
    dgain_ref[...] += jnp.sum(d_normed * hat, axis=0, keepdims=True)
    mean = jnp.sum(scaled * hat, axis=1, keepdims=True) * (1.0 / D)
    grad = dres_ref[...] + inv * (scaled - hat * mean)
    high = grad.astype(BF16)
    rest = (grad - high.astype(F32)).astype(BF16)
    ig_ref[...] = dot_nt(high, pi_ref[...]) + dot_nt(rest, pi_ref[...])
    g_scr[...] += dot_tn(nl_ref[...], d_lin)

    @pl.when(t == pl.num_programs(0) - 1)
    def _():
        own_ref[...] = g_scr[:HALF].astype(BF16)
        sib_ref[...] = g_scr[HALF:].astype(BF16)


def project_back(dq, own_kv, recv_kv, cos, sin, nl, xp, d_res, pi, weights, gain, after=()):
    rows = xp.shape[0]
    width = weights.shape[1]

    def tile(cols):
        return pl.BlockSpec((TOKEN_TILE, cols), lambda t: (t, 0))

    def whole(r, c):
        return pl.BlockSpec((r, c), lambda t: (0, 0))

    return pl.pallas_call(
        following(project_back_kernel, 11, after),
        grid=(rows // TOKEN_TILE,),
        in_specs=[tile(QW), tile(256), tile(256), tile(128), tile(128), tile(D), tile(D), tile(D)]
        + [whole(D, D)]
        + [whole(D, width)]
        + [whole(1, D)]
        + [ANYWHERE] * len(after),
        out_specs=[tile(D), whole(HALF, QKV), whole(HALF, QKV), whole(1, D), whole(1, QKV)],
        out_shape=[
            jax.ShapeDtypeStruct((rows, D), F32),
            jax.ShapeDtypeStruct((HALF, QKV), BF16),
            jax.ShapeDtypeStruct((HALF, QKV), BF16),
            jax.ShapeDtypeStruct((1, D), F32),
            jax.ShapeDtypeStruct((1, QKV), F32),
        ],
        scratch_shapes=[pltpu.VMEM((D, QKV), F32)],
        compiler_params=params(56),
        cost_estimate=TINY,
        name="project_back",
    )(dq, own_kv, recv_kv, cos, sin, nl, xp, d_res, pi, weights, gain, *after)


def step_of(first_new, second_new):
    return (
        first_new
        / (1.0 - beta_first**STEP)
        / (jnp.sqrt(second_new / (1.0 - beta_second**STEP)) + adam_epsilon)
    )


def split_two(value):
    high = value.astype(BF16)
    return high, (value - high.astype(F32)).astype(BF16)


def product(dot, a, b):
    return dot(a[0], b[0]) + (dot(a[0], b[1]) + dot(a[1], b[0]))


def side_by_side(value):
    return jnp.concatenate([value[BW * t : BW * (t + 1)] for t in range(D // BW)], axis=1)


def one_above_other(value):
    return jnp.concatenate([value[:, BW * t : BW * (t + 1)] for t in range(D // BW)], axis=0)


def adam_kernel(spans, n_arrays, block_ref, grad_ref, pi_ref, first_ref, second_ref, left_ref, right_ref, *refs):
    arrays, at = [], 0
    for count in n_arrays:
        arrays.append(refs[at : at + count])
        at += count
    first_out, second_out, block_out, w_scr, sem = refs[at:]
    block = block_ref[pl.program_id(0)]
    used = block >= 0
    places = []
    for n, pieces in enumerate(arrays):
        for page, (low, high) in enumerate(spans[n]):
            inside = used & (block >= low) & (block < high)
            column = pl.multiple_of((block - low) * BW, BW)
            places.append((inside, pieces, page, column))

    def copies(pieces, page, column):
        found, row = [], 0
        for k, piece in enumerate(pieces):
            count = piece.shape[1]
            found.append(
                pltpu.make_async_copy(
                    piece.at[page, :, pl.ds(column, BW)], w_scr.at[pl.ds(row, count), :], sem.at[k]
                )
            )
            row += count
        return found

    for inside, pieces, page, column in places:

        @pl.when(inside)
        def _(pieces=pieces, page=page, column=column):
            found = copies(pieces, page, column)
            for copy in found:
                copy.start()
            for copy in found:
                copy.wait()

    @pl.when(used)
    def _():
        grad = grad_ref[0]
        left, right = split_two(left_ref[0]), split_two(right_ref[0])
        turned = split_two(side_by_side(dot_nn(grad, right[0]) + dot_nn(grad, right[1])))
        rotated = one_above_other(product(dot_tn, left, turned))
        first_new = beta_first * first_ref[0] + (1.0 - beta_first) * rotated
        second_new = beta_second * second_ref[0] + (1.0 - beta_second) * rotated * rotated
        first_out[0] = first_new
        second_out[0] = second_new
        step = split_two(step_of(first_new, second_new))
        back = split_two(side_by_side(product(dot_nt, step, right)))
        back = one_above_other(product(dot_nn, left, back))
        weights = dot_nn(pi_ref[...], w_scr[...])
        block_out[0] = weights - rate_matrix * (back + weight_decay * weights)

    @pl.when(jnp.logical_not(used))
    def _():
        for ref in (first_out, second_out, block_out):
            ref[...] = jnp.zeros(ref.shape, F32)


def pack_kernel(spots, targets, counts, block_ref, *refs):
    n_in = sum(counts)
    ins, outs, (slots_ref, all_scr) = refs[:n_in], refs[n_in:-2], refs[-2:]
    at = 0
    for count, found in zip(counts, spots):
        for page, (width, target) in enumerate(found):
            total = ins[at][page, :, :width]
            for ref in ins[at + 1 : at + count]:
                total = total + ref[page, :, :width].astype(F32)
            all_scr[:, target : target + width] = total
        at += count
    for ref, start in zip(outs, targets):
        ref[...] = all_scr[:, start : start + ref.shape[1]]

    def one(slot, carry):
        block = jnp.maximum(block_ref[slot], 0)
        column = pl.multiple_of(block * BW, BW)
        slots_ref[slot] = all_scr[:, pl.ds(column, BW)].astype(BF16)
        return carry

    lax.fori_loop(0, slots_ref.shape[0], one, 0)


def packed(slot_block, groups, spots, targets):
    rows = groups[0][0].shape[1]
    vmem = pl.BlockSpec(memory_space=pltpu.VMEM)
    parts = [part for group in groups for part in group]
    total = (130 + 1) * BW
    return pl.pallas_call(
        functools.partial(
            pack_kernel, spots, [start for start, _ in targets], [len(g) for g in groups]
        ),
        in_specs=[pl.BlockSpec(memory_space=pltpu.SMEM)] + [vmem] * len(parts),
        out_specs=[vmem] * (len(targets) + 1),
        out_shape=[jax.ShapeDtypeStruct((rows, width), F32) for _, width in targets]
        + [jax.ShapeDtypeStruct((slot_block.shape[0], rows, BW), BF16)],
        scratch_shapes=[pltpu.VMEM((rows, total), F32)],
        compiler_params=params(48),
        cost_estimate=TINY,
        name="packed",
    )(slot_block, *parts)


def rotated_adam(slot_block, grads, pi, first_moment, second_moment, left, right, arrays, spans):
    capacity = first_moment.shape[0]
    slab = pl.BlockSpec((1, D, BW), lambda s, b: (s, 0, 0))
    basis = pl.BlockSpec((1, BW, BW), lambda s, b: (s, 0, 0))
    return pl.pallas_call(
        functools.partial(adam_kernel, spans, [len(a) for a in arrays]),
        grid_spec=pltpu.PrefetchScalarGridSpec(
            num_scalar_prefetch=1,
            grid=(capacity,),
            in_specs=[slab, pl.BlockSpec((D, D), lambda s, b: (0, 0)), slab, slab, basis, basis]
            + [ANYWHERE] * sum(len(a) for a in arrays),
            out_specs=[slab] * 3,
            scratch_shapes=[pltpu.VMEM((D, BW), BF16), pltpu.SemaphoreType.DMA((8,))],
        ),
        out_shape=[jax.ShapeDtypeStruct((capacity, D, BW), F32)] * 3,
        compiler_params=params(60),
        cost_estimate=TINY,
        name="rotated_adam",
    )(slot_block, grads, pi, first_moment, second_moment, left, right, *[p for a in arrays for p in a])


def vector_adam(vectors, grad_vectors, vector_first, vector_second):
    first_new = beta_first * vector_first + (1.0 - beta_first) * grad_vectors
    second_new = beta_second * vector_second + (1.0 - beta_second) * grad_vectors * grad_vectors
    return (second_new, vectors - rate_vector * step_of(first_new, second_new))


def on_device(
    places,
    inputs,
    cotangent,
    starts,
    query_weight,
    key_weight,
    value_weight,
    out_weight,
    gate_weight,
    up_weight,
    down_weight,
    vectors,
    owner_slot,
    first_moment,
    second_moment,
    basis_left,
    basis_right,
    vector_first,
    vector_second,
):
    n_dev, shard_rows = places.n_dev, places.rows
    here = inputs.shape[2]
    seq_index = lax.axis_index("seq")
    vec_here = vectors.shape[0]

    out_t, down_t = out_weight.T, down_weight.T
    natural = places.natural_rows()
    pi = (jnp.arange(D, dtype=jnp.int32)[:, None] == natural[None, :]).astype(BF16)
    riding = (
        jnp.arange(n_dev, dtype=jnp.int32)[:, None] * shard_rows == natural[None, :]
    ).astype(BF16)
    vector_rows = jnp.pad(vectors.reshape(1, vec_here), ((0, shard_rows - 1), (0, 128 - vec_here)))
    attention_line = stacked_rows(
        line_parts(
            places,
            rounded(
                [query_weight, key_weight, value_weight, out_t, vector_rows],
                [(0, 0, 0, QW), (0, 1, 0, KW), (0, 2, 0, KW), (0, 3, 0, QW), (0, 4, 0, 128)],
            ),
        )
    )
    feed_parts = [gate_weight, up_weight, down_t]

    def shard_of(chunks, after):
        spans = [(m, m, OFFSETS[n], CHUNKS[n]) for n in chunks for m in range(3)]
        return rounded(feed_parts, spans, after=after)

    shard_a = shard_of((0,), (attention_line,))
    attention = spread(attention_line, after=(shard_a,))
    line_a = stacked_rows(line_parts(places, shard_a), after=(attention,))
    shard_b = shard_of((1,), (attention,))
    short_a, long_a = send(line_a, places.short), send(line_a, places.long)
    attention_pages, attention = attention, attention[0]
    riders = attention[:, QKV + QW :]
    vectors_full = dot_nn(riding, riders)[:, :vec_here].reshape(-1)
    gains = jnp.pad(vectors_full[: 2 * D].reshape(2, D), ((0, 6), (0, 0))).astype(BF16)
    gains = dot_nn(gains, pi)
    gain_attn, gain_mlp = gains[0:1], gains[1:2]
    bias = vectors_full[2 * D :].reshape(1, QKV)

    spots = seq_index * here + jnp.arange(here, dtype=jnp.int32)
    own_starts = starts[:, 0]
    before = own_starts[:, None, :] <= spots[None, :, None]
    doc_begin = jnp.max(jnp.where(before, own_starts[:, None, :], 0), axis=2)
    relative = (spots[None, :] - doc_begin).astype(F32).reshape(-1)
    frequency = jnp.power(
        rope_theta, -jnp.arange(0, HEAD_SIZE, 2, dtype=F32) / HEAD_SIZE
    )
    angles = relative[:, None] * frequency[None, :]
    cos, sin = jnp.cos(angles), jnp.sin(angles)
    cos = jnp.concatenate([cos] * 4, axis=1)
    sin = jnp.concatenate([-sin, sin, -sin, sin], axis=1)
    begin = doc_begin + here - seq_index * here
    lo = begin[:, ::128] // 128
    begin = begin[:, :, None]

    x = inputs[:, 0].reshape(-1, D)
    cot = cotangent[:, 0].reshape(-1, D)
    cot_p = dot_nn(cot, pi).astype(BF16)
    cot_t = lax.dot_general(
        pi, cot, (((0,), (1,)), ((), ())), preferred_element_type=F32
    ).astype(BF16)

    xp, nl, q, k, v = project(
        x, pi, attention, gain_attn, bias, cos, sin, after=(line_a, shard_b)
    )
    line_b = stacked_rows(line_parts(places, shard_b), after=(q,))
    far_a = send(short_a, places.long)
    short_b, long_b = send(line_b, places.short), send(line_b, places.long)
    shard_c = shard_of((2, 3), (line_b,))

    forth = [(2 * n, 2 * n + 1) for n in range(n_dev // 2)]
    back = [(2 * n + 1, 2 * n) for n in range(n_dev // 2)]
    kv = send(jnp.concatenate([k, v], axis=1), forth)

    def streams(array):
        return array.reshape(MICRO, here, array.shape[-1])

    heads = (
        lo,
        streams(q),
        streams(kv[:, :KW]),
        streams(k),
        streams(kv[:, KW:]),
        streams(v),
        begin,
    )
    attended, lse = attend(*heads, after=(line_b, short_a, shard_c))
    attended_flat = attended.reshape(-1, QW)
    residual, normed, normed_t = middle(
        attended_flat, xp, attention, gain_mlp, after=(short_b,)
    )
    far_b = send(short_b, places.long)
    line_c = stacked_rows(line_parts(places, shard_c), after=(normed,))

    sums = None
    reductions, feed_pieces = [], []

    def advance(*steps, after=()):
        return tuple(getattr(reductions[n], step)(after) for n, step in steps)

    waits = [
        lambda: (),
        lambda: (),
        lambda: advance((0, "third_step"), after=sums),
        lambda: advance((0, "last_step"), (1, "third_step"), after=sums),
    ]
    pieces = [[line_a, short_a, long_a, far_a], [line_b, short_b, long_b, far_b]]
    at = 0
    for n, (wide, wait) in enumerate(zip(CHUNKS, waits)):
        coming = (at, CHUNKS[n + 2]) if n + 2 < len(CHUNKS) else None
        mlp, d_normed, kept, passed, far, *arrived = feed(
            n, wide, normed, normed_t, cot_p, cot_t, sums, pieces[n], line_c, coming, after=wait()
        )
        sums = (mlp, d_normed)
        feed_pieces.append(list(pieces[n]) + [far])
        if coming:
            pieces.append(arrived)
            at += coming[1]
        reductions.append(Reduce(places, [kept], passed))
        advance((n, "second_step"))

    output, d_res, d_att, own_out, other_out, d_gain_mlp = middle_back(
        residual, sums[0], sums[1], cot_p, attended_flat, pi, attention, gain_mlp,
        after=advance((1, "last_step"), (2, "third_step"), after=sums[:1]),
    )
    reductions.append(Reduce(places, [own_out[None], send(other_out[None], places.sibling)]))
    dq, dkv, dkv_recv = attend_back(
        *heads, attended, streams(d_att), lse,
        after=advance((2, "last_step"), (3, "third_step"), (4, "second_step"), after=(d_res,)),
    )
    dkv_recv = send(dkv_recv, back)
    input_grad, own_in, other_in, d_gain_attn, d_bias = project_back(
        dq.reshape(-1, QW), dkv.reshape(-1, 2 * KW), dkv_recv.reshape(-1, 2 * KW),
        cos, sin, nl, xp, d_res, pi,
        attention, gain_attn,
        after=advance((3, "last_step"), (4, "third_step"), after=(dq,)),
    )

    d_gains = jnp.concatenate([d_gain_attn, d_gain_mlp, jnp.zeros((6, D), F32)], axis=0)
    high, rest = split_two(d_gains)
    d_gains = dot_nt(high, pi) + dot_nt(rest, pi)
    d_vectors = jnp.concatenate([d_gains[0], d_gains[1], d_bias[0]])
    d_vectors = jnp.pad(d_vectors.reshape(n_dev, vec_here), ((0, 0), (0, 128 - vec_here)))
    riders = dot_tn(riding, d_vectors.astype(BF16)).astype(BF16)
    own_in = jnp.concatenate([own_in, riders[:HALF]], axis=1)[None]
    other_in = jnp.concatenate([other_in, riders[HALF:]], axis=1)[None]
    reductions.append(Reduce(places, [own_in, send(other_in, places.sibling)]))
    advance((4, "last_step"), after=(own_in,))
    advance((5, "second_step"), (5, "third_step"), (5, "last_step"))

    capacity = first_moment.shape[0]
    slot_count = n_dev * capacity
    slot_block = (
        jnp.full((slot_count,), -1, jnp.int32)
        .at[owner_slot]
        .set(jnp.arange(owner_slot.shape[0], dtype=jnp.int32))
    )
    spots = [
        [(w, 2048 + m * FF + o) for m in range(3)] for o, w in zip(OFFSETS, CHUNKS)
    ] + [[(QW, QKV)], [(QKV, 0)]]
    groups = [r.parts for r in reductions]
    rider_parts = [part[:, :, QKV:] for part in groups[-1]]
    groups.append(rider_parts)
    spots.append([(BW, 130 * BW)])
    targets = [
        (0, QW), (QW, KW), (QW + KW, KW), (QKV, QW),
        (2048, FF), (2048 + FF, FF), (2048 + 2 * FF, FF), (130 * BW, BW),
    ]
    (
        grad_query, grad_key, grad_value, grad_out_t, grad_gate, grad_up, grad_down_t, rider_sums, slots,
    ) = packed(slot_block, groups, spots, targets)
    grad_vectors = rider_sums[0, :vec_here]
    owned_grads = lax.all_to_all(
        slots,
        BOTH,
        split_axis=0,
        concat_axis=1,
        tiled=True,
    )
    local_block = lax.dynamic_slice_in_dim(
        slot_block, lax.axis_index(BOTH) * capacity, capacity, 0
    )
    spans = [[(0, 16)]]
    for o, w in zip(OFFSETS, CHUNKS):
        first, count = o // BW, w // BW
        spans.append(
            [(16 + 38 * m + first, 16 + 38 * m + first + count) for m in range(3)]
        )
    new_first, new_second, new_blocks = rotated_adam(
        local_block, owned_grads, pi, first_moment, second_moment, basis_left, basis_right,
        [[attention_pages]] + feed_pieces, spans,
    )
    vector_second_new, vector_new = vector_adam(vectors, grad_vectors, vector_first, vector_second)
    return (
        output.reshape(inputs.shape),
        input_grad.reshape(inputs.shape),
        grad_query,
        grad_key,
        grad_value,
        grad_out_t.T,
        grad_gate,
        grad_up,
        grad_down_t.T,
        grad_vectors,
        new_first,
        new_second,
        new_blocks,
        vector_second_new,
        vector_new,
    )


def solution(mesh):
    rows = P(("dp", "seq"), None)
    columns = P(None, ("dp", "seq"))
    tokens = P(None, "dp", "seq", None)
    slots = P(("dp", "seq"), None, None)
    line = P(("dp", "seq"))
    places = Places(mesh.shape["dp"], mesh.shape["seq"])
    return jax.shard_map(
        functools.partial(on_device, places),
        mesh=mesh,
        in_specs=(
            tokens, tokens, P(None, "dp", None), rows, rows, rows, columns, rows, rows, columns,
            line, P(), slots, slots, slots, slots, line, line,
        ),
        out_specs=(
            tokens, tokens, rows, rows, rows, columns, rows, rows, columns, line,
            slots, slots, slots, line, line,
        ),
        check_vma=False,
    )
```

```python
import functools
import math

import jax
import jax.numpy as jnp
import numpy as np
from jax import lax
from jax.experimental import pallas as pl
from jax.experimental.pallas import tpu as pltpu
from jax.sharding import PartitionSpec as P

D = 896
QUERY_HEADS = 14
KEY_VALUE_HEADS = 2
HEAD_SIZE = 64
BW = 128
MICRO = 2
STEP = 10
QW = 896
KW = 128
QKV = QW + 2 * KW
FF = 4864

norm_epsilon = 1e-06
rope_theta = 1000000.0
beta_first = 0.9
beta_second = 0.999
adam_epsilon = 1e-08
weight_decay = 0.01
rate_matrix = 0.1
rate_vector = 0.5
masked_value = -1e30

F32 = jnp.float32
BF16 = jnp.bfloat16
BOTH = ("dp", "seq")

TILE = 256
CHUNKS = (1280, 1280, 1280, 1024)
OFFSETS = (0, 1280, 2560, 3840)
QUARTER = 112
HALF = 448
TOKEN_TILE = 256

HEAD_SETS = (
    ((0, 1, 2, 3), 0, 0),
    ((0, 1, 2), 1, 0),
    ((3, 4, 5, 6), 1, 1),
    ((4, 5, 6), 0, 1),
)
SET_ROWS = (0, 512, 896, 1408)
ALL_ROWS = 1792


def params(mib, **more):
    return pltpu.CompilerParams(vmem_limit_bytes=mib * 1024 * 1024, **more)


def dot_nn(a, b):
    return lax.dot_general(a, b, (((1,), (0,)), ((), ())), preferred_element_type=F32)


def dot_nt(a, b):
    return lax.dot_general(a, b, (((1,), (1,)), ((), ())), preferred_element_type=F32)


def dot_tn(a, b):
    return lax.dot_general(a, b, (((0,), (0,)), ((), ())), preferred_element_type=F32)


def following(kernel, n_in, after):
    def wrapped(*refs):
        return kernel(*refs[:n_in], *refs[n_in + len(after) :])

    return wrapped


TINY = pl.CostEstimate(flops=1, bytes_accessed=1, transcendentals=0)
ANYWHERE = pl.BlockSpec(memory_space=pl.ANY)


class Places:
    def __init__(self, n_dp, n_seq):
        self.line = n_dp // 4
        self.rows = D // (n_dp * n_seq)
        self.n_dev = n_dp * n_seq
        self.padded = -(-self.rows // 16) * 16

        def pairs(move):
            found = []
            for z in range(self.line):
                for x in range(2):
                    for c in range(2):
                        for y in range(2):
                            tz, tx, tc, ty = move(z, x, c, y)
                            found.append(
                                (((z * 2 + x) * 2 + c) * 2 + y, ((tz * 2 + tx) * 2 + tc) * 2 + ty)
                            )
            return found

        self.sibling = pairs(lambda z, x, c, y: (z, x, 1 - c, y))
        self.long = pairs(lambda z, x, c, y: (z, 1 - x, c, y) if c == 0 else (z, x, c, 1 - y))
        self.short = pairs(lambda z, x, c, y: (z, 1 - x, c, y) if c == 1 else (z, x, c, 1 - y))
        self.ahead = [
            pairs(lambda z, x, c, y, k=k: ((z + k) % self.line, x, c, y)) for k in range(self.line)
        ]

    def natural_rows(self):
        dp = lax.axis_index("dp")
        y = lax.axis_index("seq")
        z, x, c = dp // 4, (dp // 2) % 2, dp % 2
        place = jnp.arange(D, dtype=jnp.int32)
        dc, da, db = place // HALF, (place // (2 * QUARTER)) % 2, (place // QUARTER) % 2
        dz, inner = (place % QUARTER) // self.rows, place % self.rows
        c_own = c ^ dc
        x_own = x ^ jnp.where(c_own == 0, da, db)
        y_own = y ^ jnp.where(c_own == 0, db, da)
        z_own = (z + dz) % self.line
        return self.rows * (((z_own * 2 + x_own) * 2 + c_own) * 2 + y_own) + inner


def send(array, pairs):
    return lax.ppermute(array, BOTH, pairs)


def line_parts(places, shard):
    return [shard] + [send(shard, places.ahead[-k % places.line]) for k in range(1, places.line)]


def stack_kernel(count, *refs):
    ins, (out, scr) = refs[:count], refs[count:]
    rows = QUARTER // count
    for k, ref in enumerate(ins):
        scr[rows * k : rows * (k + 1), :] = ref[0, :rows].astype(F32)
    out[0] = scr[...].astype(BF16)


def stacked_rows(parts, after=()):
    pages, rows, width = parts[0].shape
    return pl.pallas_call(
        following(functools.partial(stack_kernel, len(parts)), len(parts), after),
        grid=(pages,),
        in_specs=[pl.BlockSpec((1, rows, width), lambda m: (m, 0, 0))] * len(parts)
        + [ANYWHERE] * len(after),
        out_specs=pl.BlockSpec((1, QUARTER, width), lambda m: (m, 0, 0)),
        out_shape=jax.ShapeDtypeStruct((pages, QUARTER, width), BF16),
        scratch_shapes=[pltpu.VMEM((QUARTER, width), F32)],
        compiler_params=params(32),
        cost_estimate=TINY,
        name="stacked_rows",
    )(*parts, *after)


def neighbours():
    dp, seq = lax.axis_index("dp"), lax.axis_index("seq")
    core = lax.rem(dp, 2)
    first = dp + 2 - 4 * lax.rem(dp // 2, 2)
    sibling = (dp + 1 - 2 * core, seq)
    long = (jnp.where(core == 0, first, dp), jnp.where(core == 0, seq, 1 - seq))
    short = (jnp.where(core == 0, dp, first), jnp.where(core == 0, 1 - seq, seq))
    return sibling, long, short


def greet(devices):
    barrier = pltpu.get_barrier_semaphore()
    for device in devices:
        pl.semaphore_signal(barrier, inc=1, device_id=device, device_id_type=pl.DeviceIdType.MESH)
    pl.semaphore_wait(barrier, len(devices))


def push(src, dst, sems, n, device):
    return pltpu.make_async_remote_copy(
        src_ref=src,
        dst_ref=dst,
        send_sem=sems.at[0, n],
        recv_sem=sems.at[1, n],
        device_id=device,
        device_id_type=pl.DeviceIdType.MESH,
    )


def quarter(ref, k):
    return ref.at[:, pl.ds(QUARTER * k, QUARTER), :]


def device_of(kind):
    if isinstance(kind, str):
        return dict(zip(("sibling", "long", "short"), neighbours()))[kind]
    ahead, line = kind
    dp = lax.axis_index("dp")
    return (lax.rem(dp // 4 + ahead, line) * 4 + lax.rem(dp, 4), lax.axis_index("seq"))


def greet_kinds(kinds):
    found = []
    for kind in kinds:
        if kind not in found:
            found.append(kind)
    greet([device_of(kind) for kind in found])


def carried(kinds, srcs, dsts, sems):
    return [
        push(src, dst, sems, n, device_of(kind))
        for n, (kind, src, dst) in enumerate(zip(kinds, srcs, dsts))
    ]


def carrying(kernel, kinds, n_in, n_out):
    count = len(kinds)

    def wrapped(*refs):
        ins, srcs = refs[:n_in], refs[n_in : n_in + count]
        at = n_in + count
        outs, dsts = refs[at : at + n_out], refs[at + n_out : at + n_out + count]
        scratch, sems = refs[at + n_out + count : -1], refs[-1]

        @pl.when(pl.program_id(0) == 0)
        def _():
            greet_kinds(kinds)
            for move in carried(kinds, srcs, dsts, sems):
                move.start()

        kernel(*ins, *outs, *scratch)

        @pl.when(pl.program_id(0) == pl.num_programs(0) - 1)
        def _():
            for move in carried(kinds, srcs, dsts, sems):
                move.wait()

    return wrapped


def like(array):
    return jax.ShapeDtypeStruct(array.shape, array.dtype)


def spread_kernel(kinds, own, *refs):
    count = len(kinds)
    srcs, out, dsts, (sems, here_sem, more_sems) = (
        refs[:count], refs[count], refs[count + 1 : 2 * count + 1], refs[2 * count + 1 :],
    )
    sibling, long, short = neighbours()
    greet_kinds(("sibling", "long", "short") + tuple(kinds))
    for move in carried(kinds, srcs, dsts, more_sems):
        move.start()
    here = pltpu.make_async_copy(own, quarter(out, 0), here_sem)
    moves = [
        push(own, quarter(out, 1), sems, 0, short),
        push(own, quarter(out, 2), sems, 1, long),
        push(own, quarter(out, 4), sems, 2, sibling),
    ]
    here.start()
    for move in moves:
        move.start()
    for k, first in ((1, 3), (2, None), (3, None)):
        moves[{1: 0, 2: 1, 3: 3}[k]].wait_recv()
        if first is not None:
            moves.append(push(quarter(out, 1), quarter(out, 3), sems, 3, long))
            moves[-1].start()
        moves.append(push(quarter(out, k), quarter(out, 4 + k), sems, 3 + k, sibling))
        moves[-1].start()
    here.wait()
    for n, move in enumerate(moves):
        move.wait_send()
        if n not in (0, 1, 3):
            move.wait_recv()
    for move in carried(kinds, srcs, dsts, more_sems):
        move.wait()


def spread(own, loads):
    kinds = tuple(kind for kind, _ in loads)
    return pl.pallas_call(
        functools.partial(spread_kernel, kinds),
        in_specs=[ANYWHERE] * (1 + len(loads)),
        out_specs=[ANYWHERE] * (1 + len(loads)),
        out_shape=[jax.ShapeDtypeStruct((1, D, own.shape[2]), BF16)] + [like(a) for _, a in loads],
        scratch_shapes=[
            pltpu.SemaphoreType.DMA((2, 7)),
            pltpu.SemaphoreType.DMA,
            pltpu.SemaphoreType.DMA((2, max(1, len(loads)))),
        ],
        compiler_params=params(60, collective_id=8, has_side_effects=True),
        cost_estimate=TINY,
        name="spread",
    )(own, *[array for _, array in loads])


def fold_kernel(count, *refs):
    total = refs[0][...].astype(F32)
    for ref in refs[1:count]:
        total = total + ref[...].astype(F32)
    refs[count][...] = total.astype(BF16)


def fold(terms, rows, after=()):
    pages, _, width = terms[0][0].shape

    def spec(block):
        return pl.BlockSpec((1, rows, width), lambda m: (m, block, 0))

    return pl.pallas_call(
        following(functools.partial(fold_kernel, len(terms)), len(terms), after),
        grid=(pages,),
        in_specs=[spec(block) for _, block in terms] + [ANYWHERE] * len(after),
        out_specs=spec(0),
        out_shape=jax.ShapeDtypeStruct((pages, rows, width), BF16),
        compiler_params=params(32),
        cost_estimate=TINY,
        name="fold",
    )(*[array for array, _ in terms], *after)


def share_kernel(count, rows, *refs):
    scr = refs[-1]
    outs = refs[count:-1]
    total = refs[0][0].astype(F32)
    for ref in refs[1:count]:
        total = total + ref[0].astype(F32)
    scr[...] = total
    for k, ref in enumerate(outs):
        ref[0, :rows] = scr[rows * k : rows * (k + 1), :].astype(ref.dtype)


def share(terms, rows, padded, line, after=()):
    pages, _, width = terms[0].shape
    part = [
        pl.BlockSpec((1, padded if k else rows, width), lambda m: (m, 0, 0)) for k in range(line)
    ]
    return pl.pallas_call(
        following(functools.partial(share_kernel, len(terms), rows), len(terms), after),
        grid=(pages,),
        in_specs=[pl.BlockSpec((1, QUARTER, width), lambda m: (m, 0, 0))] * len(terms)
        + [ANYWHERE] * len(after),
        out_specs=part,
        out_shape=[
            jax.ShapeDtypeStruct((pages, padded if k else rows, width), BF16 if k else F32)
            for k in range(line)
        ],
        scratch_shapes=[pltpu.VMEM((QUARTER, width), F32)],
        compiler_params=params(32),
        cost_estimate=TINY,
        name="share",
    )(*terms, *after)


class Reduce:
    def __init__(self, places, kept, passed):
        self.places, self.terms = places, [kept]
        self.next = [("long", passed)]

    def fold(self, arrived, after):
        self.terms.append(arrived[0])
        self.next = [("short", fold([(t, 1) for t in self.terms], QUARTER, after))]

    def share(self, arrived, after):
        self.terms.append(arrived[0])
        line = self.places.line
        mine, *parts = share(self.terms, self.places.rows, self.places.padded, line, after)
        self.parts = [mine]
        self.next = [((k + 1, line), part) for k, part in enumerate(parts)]

    def end(self, arrived):
        self.parts += list(arrived)


def tail_kernel(line, rows, load_kinds, own, other, *refs):
    count = len(load_kinds)
    srcs, out, dsts = refs[:count], refs[count], refs[count + 1 : 2 * count + 1]
    came, half, came_half, quart, came_quart, keep, parts, came_parts, sems, load_sems = refs[
        2 * count + 1 :
    ]
    kinds = ["sibling", "long", "short"] + [(k, line) for k in range(1, line)]
    greet_kinds(kinds)
    for move in carried(load_kinds, srcs, dsts, load_sems):
        move.start()
    first = push(other, came, sems, 0, device_of("sibling"))
    first.start()
    first.wait_recv()
    two = 2 * QUARTER
    half[...] = (own[two:].astype(F32) + came[two:].astype(F32)).astype(BF16)
    second = push(half, came_half, sems, 1, device_of("long"))
    second.start()
    keep[...] = own[:two].astype(F32) + came[:two].astype(F32)
    second.wait_recv()
    quart[...] = (keep[QUARTER:] + came_half[QUARTER:].astype(F32)).astype(BF16)
    third = push(quart, came_quart, sems, 2, device_of("short"))
    third.start()
    keep[:QUARTER] = keep[:QUARTER] + came_half[:QUARTER].astype(F32)
    third.wait_recv()
    keep[:QUARTER] = keep[:QUARTER] + came_quart[...].astype(F32)
    moves = [first, second, third]
    for k in range(1, line):
        parts[k - 1, :rows] = keep[rows * k : rows * (k + 1), :].astype(BF16)
        moves.append(
            push(parts.at[k - 1], came_parts.at[k - 1], sems, 2 + k, device_of((k, line)))
        )
        moves[-1].start()
    total = keep[:rows]
    for k in range(1, line):
        moves[2 + k].wait_recv()
        total = total + came_parts[k - 1, :rows].astype(F32)
    out[0] = total
    for move in moves:
        move.wait_send()
    for move in carried(load_kinds, srcs, dsts, load_sems):
        move.wait()


def reduce_tail(places, own, other, loads):
    width, line, padded = own.shape[1], places.line, places.padded
    vmem = pl.BlockSpec(memory_space=pltpu.VMEM)
    return pl.pallas_call(
        functools.partial(tail_kernel, line, places.rows, tuple(kind for kind, _ in loads)),
        in_specs=[vmem, vmem] + [ANYWHERE] * len(loads),
        out_specs=[vmem] + [ANYWHERE] * len(loads),
        out_shape=[jax.ShapeDtypeStruct((1, places.rows, width), F32)] + [like(a) for _, a in loads],
        scratch_shapes=[
            pltpu.VMEM((HALF, width), BF16),
            pltpu.VMEM((2 * QUARTER, width), BF16),
            pltpu.VMEM((2 * QUARTER, width), BF16),
            pltpu.VMEM((QUARTER, width), BF16),
            pltpu.VMEM((QUARTER, width), BF16),
            pltpu.VMEM((2 * QUARTER, width), F32),
            pltpu.VMEM((line - 1, padded, width), BF16),
            pltpu.VMEM((line - 1, padded, width), BF16),
            pltpu.SemaphoreType.DMA((2, 2 + line)),
            pltpu.SemaphoreType.DMA((2, max(1, len(loads)))),
        ],
        compiler_params=params(56, collective_id=11, has_side_effects=True),
        cost_estimate=TINY,
        name="reduce_tail",
    )(own, other, *[array for _, array in loads])


def round_kernel(spans, *refs):
    ins, out = refs[:-1], refs[-1]
    at = [0] * out.shape[0]
    for page, which, offset, width in spans:
        piece = ins[which][:, offset : offset + width]
        out[page, : piece.shape[0], at[page] : at[page] + width] = piece.astype(BF16)
        at[page] += width


def rounded(parts, padded, spans, after=()):
    pages = 1 + max(page for page, _, _, _ in spans)
    width = sum(width for page, _, _, width in spans if page == 0)
    return pl.pallas_call(
        following(functools.partial(round_kernel, spans), len(parts), after),
        in_specs=[pl.BlockSpec(memory_space=pltpu.VMEM)] * len(parts) + [ANYWHERE] * len(after),
        out_specs=pl.BlockSpec(memory_space=pltpu.VMEM),
        out_shape=jax.ShapeDtypeStruct((pages, padded, width), BF16),
        compiler_params=params(32),
        cost_estimate=TINY,
        name="rounded",
    )(*parts, *after)


def swap_halves(tile, low_half):
    return jnp.where(low_half, pltpu.roll(tile, 96, 1), pltpu.roll(tile, 32, 1))


def project_kernel(x_ref, pi_ref, *refs):
    w_ref, gain_ref, bias_ref, cos_ref, sin_ref, xp_ref, nl_ref, q_ref, k_ref, v_ref = refs
    xp = dot_nn(x_ref[...], pi_ref[...])
    inv = lax.rsqrt(jnp.sum(xp * xp, axis=1, keepdims=True) * (1.0 / D) + norm_epsilon)
    nl = (xp * inv * gain_ref[...]).astype(BF16)
    xp_ref[...] = xp.astype(BF16)
    nl_ref[...] = nl
    lin = dot_nn(nl, w_ref[:, :QKV]) + bias_ref[...]
    cos, sin = cos_ref[...], sin_ref[...]
    low = lax.broadcasted_iota(jnp.int32, cos.shape, 1) % HEAD_SIZE < HEAD_SIZE // 2
    for t in range(8):
        piece = lin[:, 128 * t : 128 * (t + 1)]
        turned = (piece * cos + swap_halves(piece, low) * sin).astype(BF16)
        if t < 7:
            q_ref[:, 128 * t : 128 * (t + 1)] = (turned.astype(F32) * 0.125).astype(BF16)
        else:
            k_ref[...] = turned
    v_ref[...] = lin[:, QW + KW :].astype(BF16)


def project(x, pi, weights, gain, bias, cos, sin, after=()):
    rows = x.shape[0]
    width = weights.shape[1]

    def tile(cols):
        return pl.BlockSpec((TOKEN_TILE, cols), lambda t: (t, 0))

    def whole(r, c):
        return pl.BlockSpec((r, c), lambda t: (0, 0))

    shapes = [(D, BF16), (D, BF16), (QW, BF16), (KW, BF16), (KW, BF16)]
    return pl.pallas_call(
        following(project_kernel, 7, after),
        grid=(rows // TOKEN_TILE,),
        in_specs=[tile(D), whole(D, D)]
        + [whole(D, width)]
        + [whole(1, D), whole(1, QKV), tile(128), tile(128)]
        + [ANYWHERE] * len(after),
        out_specs=[tile(c) for c, _ in shapes],
        out_shape=[jax.ShapeDtypeStruct((rows, c), t) for c, t in shapes],
        compiler_params=params(56),
        cost_estimate=TINY,
        name="project",
    )(x, pi, weights, gain, bias, cos, sin, *after)


def padded_heads(recv, own, out):
    lane = lax.broadcasted_iota(jnp.int32, (512, 128), 1)
    for part, ref in enumerate((recv, own)):
        if ref is None:
            continue
        natural = ref[0].astype(F32)
        crossed = pltpu.roll(natural, 64, 1)
        rows = pl.ds(512 * part, 512)
        for s, (_, half, head) in enumerate(HEAD_SETS):
            source = natural if half == head else crossed
            keep = (lane >= 64) if half else (lane < 64)
            out[s, rows, :] = jnp.where(keep, source, 0.0).astype(BF16)


def block_bias(kb, i, begin):
    shape = (128, 128)
    key = kb * 128 + lax.broadcasted_iota(jnp.int32, shape, 1)
    query = 512 + i * 128 + lax.broadcasted_iota(jnp.int32, shape, 0)
    return jnp.where((key >= begin) & (key <= query), 0.0, masked_value)


def stacked(tile_of, pairs):
    return jnp.concatenate([tile_of(p) for p in pairs], axis=0)


def attend_kernel(
    lo_ref, q_ref, kr_ref, ko_ref, vr_ref, vo_ref, ds_ref, o_ref, lse_ref, kp, vp, s_scr, m_scr, l_scr, acc
):
    b, i = pl.program_id(0), pl.program_id(1)

    @pl.when(i == 0)
    def _():
        padded_heads(kr_ref, ko_ref, kp)
        padded_heads(vr_ref, vo_ref, vp)

    lo, hi = lo_ref[b, i], i + 5
    begin = ds_ref[0]
    m_scr[...] = jnp.full(m_scr.shape, masked_value, F32)
    l_scr[...] = jnp.zeros(l_scr.shape, F32)
    acc[...] = jnp.zeros(acc.shape, F32)

    def scores(kb, carry):
        bias = block_bias(kb, i, begin)
        keys = pl.ds(pl.multiple_of(kb * 128, 128), 128)
        for s, (pairs, _, _) in enumerate(HEAD_SETS):
            x = stacked(lambda p: q_ref[0, :, 128 * p : 128 * (p + 1)], pairs)
            raw = dot_nt(x, kp[s, keys, :])
            for n in range(len(pairs)):
                rows = slice(SET_ROWS[s] + 128 * n, SET_ROWS[s] + 128 * (n + 1))
                value = raw[128 * n : 128 * (n + 1)] + bias
                s_scr[kb, rows, :] = value
                m_scr[rows, :] = jnp.maximum(m_scr[rows, :], value)
        return carry

    lax.fori_loop(lo, hi, scores, 0)
    top = jnp.max(m_scr[...], axis=1, keepdims=True)
    m_scr[...] = jnp.broadcast_to(top, m_scr.shape)

    def weigh(kb, carry):
        keys = pl.ds(pl.multiple_of(kb * 128, 128), 128)
        for s, (pairs, _, _) in enumerate(HEAD_SETS):
            rows = slice(SET_ROWS[s], SET_ROWS[s] + 128 * len(pairs))
            p = jnp.exp(s_scr[kb, rows, :] - m_scr[rows, :])
            l_scr[rows, :] += p
            acc[rows, :] += dot_nn(p.astype(BF16), vp[s, keys, :])
        return carry

    lax.fori_loop(lo, hi, weigh, 0)
    total = jnp.sum(l_scr[...], axis=1, keepdims=True)
    lse = m_scr[:, :1] + jnp.log(total)
    share = 1.0 / total
    lane = lax.broadcasted_iota(jnp.int32, (128, 128), 1)
    lanes = jnp.zeros((128, 128), F32)
    outs = [None] * 7
    for s, (pairs, half, _) in enumerate(HEAD_SETS):
        for n, p in enumerate(pairs):
            rows = slice(SET_ROWS[s] + 128 * n, SET_ROWS[s] + 128 * (n + 1))
            part = acc[rows, :] * share[rows]
            outs[p] = part if outs[p] is None else outs[p] + part
            lanes = jnp.where(lane == 2 * p + half, lse[rows], lanes)
    for p in range(7):
        o_ref[0, :, 128 * p : 128 * (p + 1)] = outs[p].astype(BF16)
    lse_ref[0] = lanes


def attend_specs():
    def block(cols):
        return pl.BlockSpec((1, 128, cols), lambda b, i, lo: (b, i, 0))

    def stream(cols):
        return pl.BlockSpec((1, 512, cols), lambda b, i, lo: (b, 0, 0))

    return block, stream


def attend(lo, q, k_recv, k_own, v_recv, v_own, begin, after=()):
    block, stream = attend_specs()
    return pl.pallas_call(
        following(attend_kernel, 7, after),
        grid_spec=pltpu.PrefetchScalarGridSpec(
            num_scalar_prefetch=1,
            grid=(MICRO, 4),
            in_specs=[block(QW)] + [stream(KW)] * 4 + [block(1)] + [ANYWHERE] * len(after),
            out_specs=[block(QW), block(128)],
            scratch_shapes=[
                pltpu.VMEM((4, 1024, 128), BF16),
                pltpu.VMEM((4, 1024, 128), BF16),
                pltpu.VMEM((8, ALL_ROWS, 128), F32),
                pltpu.VMEM((ALL_ROWS, 128), F32),
                pltpu.VMEM((ALL_ROWS, 128), F32),
                pltpu.VMEM((ALL_ROWS, 128), F32),
            ],
        ),
        out_shape=[
            jax.ShapeDtypeStruct((MICRO, 512, QW), BF16),
            jax.ShapeDtypeStruct((MICRO, 512, 128), F32),
        ],
        compiler_params=params(56),
        cost_estimate=TINY,
        name="attend",
    )(lo, q, k_recv, k_own, v_recv, v_own, begin, *after)


def attend_back_kernel(
    lo_ref, q_ref, kr_ref, ko_ref, vr_ref, vo_ref, ds_ref, o_ref, do_ref, lse_ref,
    dq_ref, own_ref, recv_ref, kp, vp, dk, dv, dq_acc,
):
    b, i = pl.program_id(0), pl.program_id(1)

    @pl.when(i == 0)
    def _():
        padded_heads(kr_ref, ko_ref, kp)
        padded_heads(vr_ref, vo_ref, vp)
        dk[...] = jnp.zeros(dk.shape, F32)
        dv[...] = jnp.zeros(dv.shape, F32)

    lo, hi = lo_ref[b, i], i + 5
    begin = ds_ref[0]
    lane = lax.broadcasted_iota(jnp.int32, (128, 128), 1)
    dq_acc[...] = jnp.zeros(dq_acc.shape, F32)
    lse_all = lse_ref[0]
    lse, dots = [], []
    for s, (pairs, half, _) in enumerate(HEAD_SETS):
        for p in pairs:
            cols = slice(128 * p, 128 * (p + 1))
            product = o_ref[0, :, cols].astype(F32) * do_ref[0, :, cols].astype(F32)
            keep = (lane >= 64) if half else (lane < 64)
            dots.append(jnp.sum(jnp.where(keep, product, 0.0), axis=1, keepdims=True))
            head = 2 * p + half
            lse.append(lse_all[:, head : head + 1])

    def one_block(kb, carry):
        bias = block_bias(kb, i, begin)
        keys = pl.ds(pl.multiple_of(kb * 128, 128), 128)
        at = 0
        for s, (pairs, _, _) in enumerate(HEAD_SETS):
            x = stacked(lambda p: q_ref[0, :, 128 * p : 128 * (p + 1)], pairs)
            y = stacked(lambda p: do_ref[0, :, 128 * p : 128 * (p + 1)], pairs)
            raw = dot_nt(x, kp[s, keys, :])
            d_prob = dot_nt(y, vp[s, keys, :])
            probs, d_scores = [], []
            for n in range(len(pairs)):
                rows = slice(128 * n, 128 * (n + 1))
                p = jnp.exp(raw[rows] + bias - lse[at + n])
                probs.append(p.astype(BF16))
                d_scores.append((p * (d_prob[rows] - dots[at + n])).astype(BF16))
            at += len(pairs)
            prob = jnp.concatenate(probs, axis=0)
            d_score = jnp.concatenate(d_scores, axis=0)
            d_query = dot_nn(d_score, kp[s, keys, :])
            for n, p in enumerate(pairs):
                dq_acc[p] += d_query[128 * n : 128 * (n + 1)]
            dk[s, keys, :] += dot_tn(d_score, x)
            dv[s, keys, :] += dot_tn(prob, y)
        return carry

    lax.fori_loop(lo, hi, one_block, 0)
    for p in range(7):
        dq_ref[0, :, 128 * p : 128 * (p + 1)] = (dq_acc[p] * 0.125).astype(BF16)

    @pl.when(i == 3)
    def _():
        wide = lax.broadcasted_iota(jnp.int32, (512, 128), 1) < 64
        for part, ref in enumerate((recv_ref, own_ref)):
            rows = pl.ds(512 * part, 512)
            for n, grads in enumerate((dk, dv)):
                low = grads[0, rows, :] + pltpu.roll(grads[1, rows, :], 64, 1)
                high = grads[2, rows, :] + pltpu.roll(grads[3, rows, :], 64, 1)
                value = jnp.where(wide, low, high)
                ref[0, :, 128 * n : 128 * (n + 1)] = value.astype(ref.dtype)


def attend_back(lo, q, k_recv, k_own, v_recv, v_own, begin, out, d_out, lse, after=()):
    block, stream = attend_specs()
    return pl.pallas_call(
        following(attend_back_kernel, 10, after),
        grid_spec=pltpu.PrefetchScalarGridSpec(
            num_scalar_prefetch=1,
            grid=(MICRO, 4),
            in_specs=[block(QW)]
            + [stream(KW)] * 4
            + [block(1), block(QW), block(QW), block(128)]
            + [ANYWHERE] * len(after),
            out_specs=[block(QW), stream(256), stream(256)],
            scratch_shapes=[
                pltpu.VMEM((4, 1024, 128), BF16),
                pltpu.VMEM((4, 1024, 128), BF16),
                pltpu.VMEM((4, 1024, 128), F32),
                pltpu.VMEM((4, 1024, 128), F32),
                pltpu.VMEM((7, 128, 128), F32),
            ],
        ),
        out_shape=[
            jax.ShapeDtypeStruct((MICRO, 512, QW), BF16),
            jax.ShapeDtypeStruct((MICRO, 512, 256), F32),
            jax.ShapeDtypeStruct((MICRO, 512, 256), BF16),
        ],
        compiler_params=params(56),
        cost_estimate=TINY,
        name="attend_back",
    )(lo, q, k_recv, k_own, v_recv, v_own, begin, out, d_out, lse, *after)


def middle_kernel(att_ref, xp_ref, *refs):
    w_ref, gain_ref, res_ref, n_ref, nt_ref = refs
    residual = xp_ref[...].astype(F32) + dot_nt(att_ref[...], w_ref[:, QKV : QKV + QW])
    inv = lax.rsqrt(jnp.sum(residual * residual, axis=1, keepdims=True) * (1.0 / D) + norm_epsilon)
    normed = residual * inv * gain_ref[...]
    res_ref[...] = residual
    n_ref[...] = normed.astype(BF16)
    nt_ref[...] = normed.T.astype(BF16)


def middle(attended, xp, weights, gain, after=()):
    rows = xp.shape[0]
    width = weights.shape[1]

    def tile(cols):
        return pl.BlockSpec((TOKEN_TILE, cols), lambda t: (t, 0))

    def whole(r, c):
        return pl.BlockSpec((r, c), lambda t: (0, 0))

    return pl.pallas_call(
        following(middle_kernel, 4, after),
        grid=(rows // TOKEN_TILE,),
        in_specs=[tile(QW), tile(D)]
        + [whole(D, width)]
        + [whole(1, D)]
        + [ANYWHERE] * len(after),
        out_specs=[tile(D), tile(D), pl.BlockSpec((D, TOKEN_TILE), lambda t: (0, t))],
        out_shape=[
            jax.ShapeDtypeStruct((rows, D), F32),
            jax.ShapeDtypeStruct((rows, D), BF16),
            jax.ShapeDtypeStruct((D, rows), BF16),
        ],
        compiler_params=params(56),
        cost_estimate=TINY,
        name="middle",
    )(attended, xp, weights, gain, *after)


def middle_back_kernel(res_ref, mlp_ref, dn_ref, cot_ref, att_ref, pi_ref, *refs):
    w_ref, gain_ref, out_ref, dres_ref, datt_ref, own_ref, sib_ref, dgain_ref, g_scr = refs
    t = pl.program_id(0)

    @pl.when(t == 0)
    def _():
        g_scr[...] = jnp.zeros(g_scr.shape, F32)
        dgain_ref[...] = jnp.zeros(dgain_ref.shape, F32)

    residual = res_ref[...]
    inv = lax.rsqrt(jnp.sum(residual * residual, axis=1, keepdims=True) * (1.0 / D) + norm_epsilon)
    out_low = (residual + mlp_ref[...]).astype(BF16)
    out_ref[...] = dot_nt(out_low, pi_ref[...]).astype(BF16)
    d_normed = dn_ref[...]
    hat = residual * inv
    scaled = d_normed * gain_ref[...]
    dgain_ref[...] += jnp.sum(d_normed * hat, axis=0, keepdims=True)
    mean = jnp.sum(scaled * hat, axis=1, keepdims=True) * (1.0 / D)
    d_res = cot_ref[...].astype(F32) + inv * (scaled - hat * mean)
    dres_ref[...] = d_res
    low = d_res.astype(BF16)
    datt_ref[...] = dot_nn(low, w_ref[:, QKV : QKV + QW]).astype(BF16)
    g_scr[...] += dot_tn(low, att_ref[...])

    @pl.when(t == pl.num_programs(0) - 1)
    def _():
        own_ref[...] = g_scr[:HALF].astype(BF16)
        sib_ref[...] = g_scr[HALF:].astype(BF16)


def middle_back(residual, mlp, d_normed, cot, attended, pi, weights, gain, loads):
    rows = residual.shape[0]
    width = weights.shape[1]

    def tile(cols):
        return pl.BlockSpec((TOKEN_TILE, cols), lambda t: (t, 0))

    def whole(r, c):
        return pl.BlockSpec((r, c), lambda t: (0, 0))

    return pl.pallas_call(
        carrying(middle_back_kernel, tuple(kind for kind, _ in loads), 8, 6),
        grid=(rows // TOKEN_TILE,),
        in_specs=[tile(D)] * 4
        + [tile(QW), whole(D, D)]
        + [whole(D, width)]
        + [whole(1, D)]
        + [ANYWHERE] * len(loads),
        out_specs=[tile(D), tile(D), tile(QW), whole(HALF, QW), whole(HALF, QW), whole(1, D)]
        + [ANYWHERE] * len(loads),
        out_shape=[
            jax.ShapeDtypeStruct((rows, D), BF16),
            jax.ShapeDtypeStruct((rows, D), F32),
            jax.ShapeDtypeStruct((rows, QW), BF16),
            jax.ShapeDtypeStruct((HALF, QW), BF16),
            jax.ShapeDtypeStruct((HALF, QW), BF16),
            jax.ShapeDtypeStruct((1, D), F32),
        ]
        + [like(array) for _, array in loads],
        scratch_shapes=[pltpu.VMEM((D, QW), F32), pltpu.SemaphoreType.DMA((2, len(loads)))],
        compiler_params=params(56, collective_id=9, has_side_effects=True),
        cost_estimate=TINY,
        name="middle_back",
    )(residual, mlp, d_normed, cot, attended, pi, weights, gain, *[array for _, array in loads])


def feed_kernel(wide, started, n_pieces, coming, kinds, *refs):
    n_in = 4 + (2 if started else 0)
    n_hbm, nt_hbm, cot_hbm, cott_hbm = refs[:4]
    sums_in = refs[4:n_in]
    pieces = refs[n_in : n_in + n_pieces]
    n_in += n_pieces
    if coming:
        line_hbm = refs[n_in]
        n_in += 1
    srcs = refs[n_in : n_in + len(kinds)]
    n_in += len(kinds)
    mlp_hbm, dn_hbm, keep_hbm, pass_hbm, far_hbm = refs[n_in : n_in + 5]
    n_in += 5
    if coming:
        next_hbm = refs[n_in]
        n_in += 1
    dsts = refs[n_in : n_in + len(kinds)]
    n_in += len(kinds)
    (
        n_v, nt_v, cot_v, cott_v, w_v, mlp_v, dn_v, act_v, grad_v, came_v,
        in_sem, w_sem, w_send, w_recv, out_sem, g_sem, g_send, g_recv, next_sem, next_here,
        carry_sem,
    ) = refs[n_in:]
    rows_all = n_v.shape[0]
    steps = wide // TILE
    span = 512
    parts = rows_all // span
    sibling, long, short = neighbours()
    mesh_id = pl.DeviceIdType.MESH
    share_rows = HALF // n_pieces

    def tile_of(j):
        return pl.ds(pl.multiple_of(j * TILE, TILE), TILE)

    def weight_copy(k, j):
        return pltpu.make_async_copy(
            pieces[k].at[:, :, tile_of(j)],
            w_v.at[:, pl.ds(share_rows * k, share_rows), tile_of(j)],
            w_sem.at[k, j],
        )

    def weight_push(k, j):
        return pltpu.make_async_remote_copy(
            src_ref=pieces[k].at[:, :, tile_of(j)],
            dst_ref=w_v.at[:, pl.ds(HALF + share_rows * k, share_rows), tile_of(j)],
            send_sem=w_send.at[k, j],
            recv_sem=w_recv.at[k, j],
            device_id=sibling,
            device_id_type=mesh_id,
        )

    def gradient_push(j):
        return pltpu.make_async_remote_copy(
            src_ref=grad_v.at[:, pl.ds(HALF, HALF), tile_of(j)],
            dst_ref=came_v.at[:, :, tile_of(j)],
            send_sem=g_send.at[j],
            recv_sem=g_recv.at[j],
            device_id=sibling,
            device_id_type=mesh_id,
        )

    def sum_copies(j):
        return [
            pltpu.make_async_copy(
                grad_v.at[:, pl.ds(2 * QUARTER * h, 2 * QUARTER), tile_of(j)],
                hbm.at[:, :, tile_of(j)],
                g_sem.at[j, h],
            )
            for h, hbm in enumerate((keep_hbm, pass_hbm))
        ]

    def add_sibling(j):
        cols = tile_of(j)
        gradient_push(j).wait_recv()
        for m in range(3):
            total = grad_v[m, :HALF, cols].astype(F32) + came_v[m, :, cols].astype(F32)
            grad_v[m, :HALF, cols] = total.astype(BF16)
        for copy in sum_copies(j):
            copy.start()

    def span_of(part):
        return pl.ds(part * span, span)

    loads = [
        pltpu.make_async_copy(src, dst, in_sem.at[n])
        for n, (src, dst) in enumerate(
            [(n_hbm, n_v), (cot_hbm, cot_v), (nt_hbm, nt_v), (cott_hbm, cott_v)]
            + ([(sums_in[0], mlp_v), (sums_in[1], dn_v)] if started else [])
        )
    ]
    loads[0].start()
    greet_kinds(("sibling",) + (("long", "short") if coming else ()) + kinds)

    def fetch(j, carry):
        for k in range(n_pieces):
            weight_copy(k, j).start()
            weight_push(k, j).start()
        return carry

    fetch(0, 0)
    for copy in loads[1:4]:
        copy.start()
    lax.fori_loop(1, steps, fetch, 0)
    for copy in loads[4:]:
        copy.start()
    if coming:
        at, width = coming
        line = line_hbm.at[:, :, pl.ds(at, width)]
        line_copy = pltpu.make_async_copy(line, quarter(next_hbm, 0), next_here)
        moves = [
            push(line, quarter(next_hbm, 1), next_sem, 0, short),
            push(line, quarter(next_hbm, 2), next_sem, 1, long),
            push(quarter(next_hbm, 1), quarter(next_hbm, 3), next_sem, 2, long),
        ]
        line_copy.start()
        moves[0].start()
        moves[1].start()

    for move in carried(kinds, srcs, dsts, carry_sem):
        move.start()

    for copy in loads[:4]:
        copy.wait()

    def columns(j, carry):
        for k in range(n_pieces):
            weight_copy(k, j).wait()
            weight_push(k, j).wait_recv()
        cols = tile_of(j)
        for part in range(parts):
            rows = span_of(part)
            normed = n_v[rows, :]
            gate = dot_nn(normed, w_v[0, :, cols])
            up = dot_nn(normed, w_v[1, :, cols])
            d_hidden = dot_nn(cot_v[rows, :], w_v[2, :, cols])
            s = 1.0 / (1.0 + jnp.exp(-gate))
            silu = gate * s
            act_v[2, rows, cols] = (silu * up).astype(BF16)
            act_v[0, rows, cols] = (d_hidden * up * s * (1.0 + gate * (1.0 - s))).astype(BF16)
            act_v[1, rows, cols] = (d_hidden * silu).astype(BF16)
        for m, left in ((2, cott_v), (0, nt_v), (1, nt_v)):
            grad_v[m, :, cols] = dot_nn(left[...], act_v[m, :, cols]).astype(BF16)
        gradient_push(j).start()

        @pl.when(j > 0)
        def _():
            add_sibling(j - 1)

        return carry

    lax.fori_loop(0, steps, columns, 0)
    stores = [pltpu.make_async_copy(w_v.at[:, pl.ds(HALF, HALF), :], far_hbm, out_sem.at[parts, 0])]
    stores[0].start()
    if coming:
        moves[0].wait_recv()
        moves[2].start()
    for copy in loads[4:]:
        copy.wait()
    for part in range(parts):
        rows = span_of(part)
        for k in range(2):
            if k == 0:
                total, ref, hbm = dot_nt(act_v[2, rows, :], w_v[2]), mlp_v, mlp_hbm
            else:
                total = dot_nt(act_v[0, rows, :], w_v[0]) + dot_nt(act_v[1, rows, :], w_v[1])
                ref, hbm = dn_v, dn_hbm
            ref[rows, :] = total + ref[rows, :] if started else total
            if part == 0 and k == 0:
                add_sibling(steps - 1)
            stores.append(
                pltpu.make_async_copy(ref.at[rows, :], hbm.at[rows, :], out_sem.at[part, k])
            )
            stores[-1].start()

    def settle(j, carry):
        for k in range(n_pieces):
            weight_push(k, j).wait_send()
        gradient_push(j).wait_send()
        for copy in sum_copies(j):
            copy.wait()
        return carry

    lax.fori_loop(0, steps, settle, 0)
    for copy in stores:
        copy.wait()
    if coming:
        line_copy.wait()
        moves[0].wait_send()
        moves[1].wait()
        moves[2].wait()
    for move in carried(kinds, srcs, dsts, carry_sem):
        move.wait()


def feed(number, wide, normed, normed_t, cot, cot_t, sums, pieces, line, coming, loads):
    rows = normed.shape[0]
    started = sums is not None
    kinds = tuple(kind for kind, _ in loads)
    extra = (list(sums) if started else []) + list(pieces) + ([line] if coming else [])
    extra += [array for _, array in loads]
    n_in = 4 + len(extra)
    steps = wide // TILE
    half = jax.ShapeDtypeStruct((3, HALF, wide), BF16)
    two_quarters = jax.ShapeDtypeStruct((3, 2 * QUARTER, wide), BF16)
    return pl.pallas_call(
        functools.partial(feed_kernel, wide, started, len(pieces), coming, kinds),
        in_specs=[ANYWHERE] * n_in,
        out_specs=[ANYWHERE] * ((6 if coming else 5) + len(loads)),
        out_shape=[
            jax.ShapeDtypeStruct((rows, D), F32),
            jax.ShapeDtypeStruct((rows, D), F32),
            two_quarters,
            two_quarters,
            half,
        ]
        + ([jax.ShapeDtypeStruct((3, HALF, coming[1]), BF16)] if coming else [])
        + [like(array) for _, array in loads],
        scratch_shapes=[
            pltpu.VMEM((rows, D), BF16),
            pltpu.VMEM((D, rows), BF16),
            pltpu.VMEM((rows, D), BF16),
            pltpu.VMEM((D, rows), BF16),
            pltpu.VMEM((3, D, wide), BF16),
            pltpu.VMEM((rows, D), F32),
            pltpu.VMEM((rows, D), F32),
            pltpu.VMEM((3, rows, wide), BF16),
            pltpu.VMEM((3, D, wide), BF16),
            pltpu.VMEM((3, HALF, wide), BF16),
            pltpu.SemaphoreType.DMA((6,)),
            pltpu.SemaphoreType.DMA((len(pieces), steps)),
            pltpu.SemaphoreType.DMA((len(pieces), steps)),
            pltpu.SemaphoreType.DMA((len(pieces), steps)),
            pltpu.SemaphoreType.DMA((3, 2)),
            pltpu.SemaphoreType.DMA((steps, 2)),
            pltpu.SemaphoreType.DMA((steps,)),
            pltpu.SemaphoreType.DMA((steps,)),
            pltpu.SemaphoreType.DMA((2, 3)),
            pltpu.SemaphoreType.DMA,
            pltpu.SemaphoreType.DMA((2, max(1, len(loads)))),
        ],
        compiler_params=params(56, collective_id=number, has_side_effects=True),
        cost_estimate=TINY,
        name="feed",
    )(normed, normed_t, cot, cot_t, *extra)


def project_back_kernel(dq_ref, own_kv_ref, recv_kv_ref, cos_ref, sin_ref, nl_ref, xp_ref, dres_ref, pi_ref, *refs):
    w_ref, gain_ref, ig_ref, own_ref, sib_ref, dgain_ref, dbias_ref, g_scr = refs
    t = pl.program_id(0)

    @pl.when(t == 0)
    def _():
        g_scr[...] = jnp.zeros(g_scr.shape, F32)
        dgain_ref[...] = jnp.zeros(dgain_ref.shape, F32)
        dbias_ref[...] = jnp.zeros(dbias_ref.shape, F32)

    cos, sin = cos_ref[...], sin_ref[...]
    low = lax.broadcasted_iota(jnp.int32, cos.shape, 1) % HEAD_SIZE < HEAD_SIZE // 2
    parts = []
    dkv = (own_kv_ref[...] + recv_kv_ref[...].astype(F32)).astype(BF16)
    for n in range(8):
        piece = (dq_ref[:, 128 * n : 128 * (n + 1)] if n < 7 else dkv[:, :KW]).astype(F32)
        parts.append((piece * cos - swap_halves(piece, low) * sin).astype(BF16))
    parts.append(dkv[:, KW:])
    d_lin = jnp.concatenate(parts, axis=1)
    dbias_ref[...] += jnp.sum(d_lin.astype(F32), axis=0, keepdims=True)
    d_normed = dot_nt(d_lin, w_ref[:, :QKV])
    xp = xp_ref[...].astype(F32)
    inv = lax.rsqrt(jnp.sum(xp * xp, axis=1, keepdims=True) * (1.0 / D) + norm_epsilon)
    hat = xp * inv
    scaled = d_normed * gain_ref[...]
    dgain_ref[...] += jnp.sum(d_normed * hat, axis=0, keepdims=True)
    mean = jnp.sum(scaled * hat, axis=1, keepdims=True) * (1.0 / D)
    grad = dres_ref[...] + inv * (scaled - hat * mean)
    high = grad.astype(BF16)
    rest = (grad - high.astype(F32)).astype(BF16)
    ig_ref[...] = dot_nt(high, pi_ref[...]) + dot_nt(rest, pi_ref[...])
    g_scr[...] += dot_tn(nl_ref[...], d_lin)

    @pl.when(t == pl.num_programs(0) - 1)
    def _():
        own_ref[...] = g_scr[:HALF].astype(BF16)
        sib_ref[...] = g_scr[HALF:].astype(BF16)


def project_back(dq, own_kv, recv_kv, cos, sin, nl, xp, d_res, pi, weights, gain, loads):
    rows = xp.shape[0]
    width = weights.shape[1]

    def tile(cols):
        return pl.BlockSpec((TOKEN_TILE, cols), lambda t: (t, 0))

    def whole(r, c):
        return pl.BlockSpec((r, c), lambda t: (0, 0))

    return pl.pallas_call(
        carrying(project_back_kernel, tuple(kind for kind, _ in loads), 11, 5),
        grid=(rows // TOKEN_TILE,),
        in_specs=[tile(QW), tile(256), tile(256), tile(128), tile(128), tile(D), tile(D), tile(D)]
        + [whole(D, D)]
        + [whole(D, width)]
        + [whole(1, D)]
        + [ANYWHERE] * len(loads),
        out_specs=[tile(D), whole(HALF, QKV), whole(HALF, QKV), whole(1, D), whole(1, QKV)]
        + [ANYWHERE] * len(loads),
        out_shape=[
            jax.ShapeDtypeStruct((rows, D), F32),
            jax.ShapeDtypeStruct((HALF, QKV), BF16),
            jax.ShapeDtypeStruct((HALF, QKV), BF16),
            jax.ShapeDtypeStruct((1, D), F32),
            jax.ShapeDtypeStruct((1, QKV), F32),
        ]
        + [like(array) for _, array in loads],
        scratch_shapes=[pltpu.VMEM((D, QKV), F32), pltpu.SemaphoreType.DMA((2, len(loads)))],
        compiler_params=params(56, collective_id=10, has_side_effects=True),
        cost_estimate=TINY,
        name="project_back",
    )(dq, own_kv, recv_kv, cos, sin, nl, xp, d_res, pi, weights, gain,
      *[array for _, array in loads])


def step_of(first_new, second_new):
    return (
        first_new
        / (1.0 - beta_first**STEP)
        / (jnp.sqrt(second_new / (1.0 - beta_second**STEP)) + adam_epsilon)
    )


def split_two(value):
    high = value.astype(BF16)
    return high, (value - high.astype(F32)).astype(BF16)


def product(dot, a, b):
    return dot(a[0], b[0]) + (dot(a[0], b[1]) + dot(a[1], b[0]))


def side_by_side(value):
    return jnp.concatenate([value[BW * t : BW * (t + 1)] for t in range(D // BW)], axis=1)


def one_above_other(value):
    return jnp.concatenate([value[:, BW * t : BW * (t + 1)] for t in range(D // BW)], axis=0)


def pick_kernel(spans, counts, block_ref, pi_ref, *refs):
    arrays, at = [], 0
    for count in counts:
        arrays.append(refs[at : at + count])
        at += count
    out_ref, w_scr, sem = refs[at:]
    slots = out_ref.shape[0]

    def each(slot, act):
        block = block_ref[slot]
        for n, pieces in enumerate(arrays):
            for page, (low, high) in enumerate(spans[n]):

                @pl.when((block >= low) & (block < high))
                def _(pieces=pieces, page=page, low=low):
                    column = pl.multiple_of((block - low) * BW, BW)
                    row = 0
                    for k, piece in enumerate(pieces):
                        count = piece.shape[1]
                        act(
                            pltpu.make_async_copy(
                                piece.at[page, :, pl.ds(column, BW)],
                                w_scr.at[slot, pl.ds(row, count), :],
                                sem.at[slot, k],
                            )
                        )
                        row += count

    for slot in range(slots):
        each(slot, lambda copy: copy.start())
    for slot in range(slots):
        each(slot, lambda copy: copy.wait())
        out_ref[slot] = dot_nn(pi_ref[...], w_scr[slot])


def picked(slot_block, pi, arrays, spans, after=()):
    capacity = slot_block.shape[0]
    vmem = pl.BlockSpec(memory_space=pltpu.VMEM)
    flat = [p for a in arrays for p in a]
    return pl.pallas_call(
        following(
            functools.partial(pick_kernel, spans, [len(a) for a in arrays]), 2 + len(flat), after
        ),
        in_specs=[pl.BlockSpec(memory_space=pltpu.SMEM), vmem]
        + [ANYWHERE] * (len(flat) + len(after)),
        out_specs=vmem,
        out_shape=jax.ShapeDtypeStruct((capacity, D, BW), F32),
        scratch_shapes=[pltpu.VMEM((capacity, D, BW), BF16), pltpu.SemaphoreType.DMA((capacity, 8))],
        compiler_params=params(60),
        cost_estimate=TINY,
        name="picked",
    )(slot_block, pi, *flat, *after)


def adam_kernel(block_ref, grad_ref, weight_ref, first_ref, second_ref, left_ref, right_ref, first_out, second_out, block_out):
    used = block_ref[pl.program_id(0)] >= 0

    @pl.when(used)
    def _():
        grad = grad_ref[0]
        left, right = split_two(left_ref[0]), split_two(right_ref[0])
        turned = split_two(side_by_side(dot_nn(grad, right[0]) + dot_nn(grad, right[1])))
        rotated = one_above_other(product(dot_tn, left, turned))
        first_new = beta_first * first_ref[0] + (1.0 - beta_first) * rotated
        second_new = beta_second * second_ref[0] + (1.0 - beta_second) * rotated * rotated
        first_out[0] = first_new
        second_out[0] = second_new
        step = split_two(step_of(first_new, second_new))
        back = split_two(side_by_side(product(dot_nt, step, right)))
        back = one_above_other(product(dot_nn, left, back))
        weights = weight_ref[0]
        block_out[0] = weights - rate_matrix * (back + weight_decay * weights)

    @pl.when(jnp.logical_not(used))
    def _():
        for ref in (first_out, second_out, block_out):
            ref[...] = jnp.zeros(ref.shape, F32)


def pack_kernel(spots, targets, counts, block_ref, *refs):
    n_in = sum(counts)
    ins, outs, (slots_ref, all_scr) = refs[:n_in], refs[n_in:-2], refs[-2:]
    at = 0
    for count, found in zip(counts, spots):
        for page, (width, target) in enumerate(found):
            total = ins[at][page, :, :width]
            for ref in ins[at + 1 : at + count]:
                total = total + ref[page, : total.shape[0], :width].astype(F32)
            all_scr[:, target : target + width] = total
        at += count
    for ref, start in zip(outs, targets):
        ref[...] = all_scr[:, start : start + ref.shape[1]]

    def one(slot, carry):
        block = jnp.maximum(block_ref[slot], 0)
        column = pl.multiple_of(block * BW, BW)
        slots_ref[slot] = all_scr[:, pl.ds(column, BW)].astype(BF16)
        return carry

    lax.fori_loop(0, slots_ref.shape[0], one, 0)


def packed(slot_block, groups, spots, targets):
    rows = groups[0][0].shape[1]
    vmem = pl.BlockSpec(memory_space=pltpu.VMEM)
    parts = [part for group in groups for part in group]
    total = (130 + 1) * BW
    return pl.pallas_call(
        functools.partial(
            pack_kernel, spots, [start for start, _ in targets], [len(g) for g in groups]
        ),
        in_specs=[pl.BlockSpec(memory_space=pltpu.SMEM)] + [vmem] * len(parts),
        out_specs=[vmem] * (len(targets) + 1),
        out_shape=[jax.ShapeDtypeStruct((rows, width), F32) for _, width in targets]
        + [jax.ShapeDtypeStruct((slot_block.shape[0], rows, BW), BF16)],
        scratch_shapes=[pltpu.VMEM((rows, total), F32)],
        compiler_params=params(48),
        cost_estimate=TINY,
        name="packed",
    )(slot_block, *parts)


def rotated_adam(slot_block, grads, weights, first_moment, second_moment, left, right):
    capacity = first_moment.shape[0]
    slab = pl.BlockSpec((1, D, BW), lambda s, b: (s, 0, 0))
    basis = pl.BlockSpec((1, BW, BW), lambda s, b: (s, 0, 0))
    return pl.pallas_call(
        adam_kernel,
        grid_spec=pltpu.PrefetchScalarGridSpec(
            num_scalar_prefetch=1,
            grid=(capacity,),
            in_specs=[slab, slab, slab, slab, basis, basis],
            out_specs=[slab] * 3,
        ),
        out_shape=[jax.ShapeDtypeStruct((capacity, D, BW), F32)] * 3,
        compiler_params=params(40),
        cost_estimate=TINY,
        name="rotated_adam",
    )(slot_block, grads, weights, first_moment, second_moment, left, right)


def vector_adam(vectors, grad_vectors, vector_first, vector_second):
    first_new = beta_first * vector_first + (1.0 - beta_first) * grad_vectors
    second_new = beta_second * vector_second + (1.0 - beta_second) * grad_vectors * grad_vectors
    return (second_new, vectors - rate_vector * step_of(first_new, second_new))


def hand_out(moving, arrived, after=()):
    at = 0
    for r in moving:
        came = arrived[at : at + len(r.next)]
        at += len(r.next)
        kind = r.next[0][0]
        if kind == "long":
            r.fold(came, after)
        elif kind == "short":
            r.share(came, after)
        else:
            r.end(came)
            r.next = []


def on_device(
    places,
    inputs,
    cotangent,
    starts,
    query_weight,
    key_weight,
    value_weight,
    out_weight,
    gate_weight,
    up_weight,
    down_weight,
    vectors,
    owner_slot,
    first_moment,
    second_moment,
    basis_left,
    basis_right,
    vector_first,
    vector_second,
):
    n_dev, shard_rows = places.n_dev, places.rows
    here = inputs.shape[2]
    seq_index = lax.axis_index("seq")
    vec_here = vectors.shape[0]

    out_t, down_t = out_weight.T, down_weight.T
    natural = places.natural_rows()
    pi = (jnp.arange(D, dtype=jnp.int32)[:, None] == natural[None, :]).astype(BF16)
    riding = (
        jnp.arange(n_dev, dtype=jnp.int32)[:, None] * shard_rows == natural[None, :]
    ).astype(BF16)
    vector_rows = jnp.pad(vectors.reshape(1, vec_here), ((0, shard_rows - 1), (0, 128 - vec_here)))
    attention_line = stacked_rows(
        line_parts(
            places,
            rounded(
                [query_weight, key_weight, value_weight, out_t, vector_rows],
                places.padded,
                [(0, 0, 0, QW), (0, 1, 0, KW), (0, 2, 0, KW), (0, 3, 0, QW), (0, 4, 0, 128)],
            ),
        )
    )
    feed_parts = [gate_weight, up_weight, down_t]

    def shard_of(chunks, after):
        spans = [(m, m, OFFSETS[n], CHUNKS[n]) for n in chunks for m in range(3)]
        return rounded(feed_parts, places.padded, spans, after=after)

    shard_a = shard_of((0,), ())
    backwards = [(-k % places.line, places.line) for k in range(1, places.line)]
    attention, *arrived = spread(attention_line, [(kind, shard_a) for kind in backwards])
    line_a = stacked_rows([shard_a] + arrived)
    shard_b = shard_of((1,), (attention,))
    short_a, long_a = send(line_a, places.short), send(line_a, places.long)
    attention_pages, attention = attention, attention[0]
    riders = attention[:, QKV + QW :]
    vectors_full = dot_nn(riding, riders)[:, :vec_here].reshape(-1)
    gains = jnp.pad(vectors_full[: 2 * D].reshape(2, D), ((0, 6), (0, 0))).astype(BF16)
    gains = dot_nn(gains, pi)
    gain_attn, gain_mlp = gains[0:1], gains[1:2]
    bias = vectors_full[2 * D :].reshape(1, QKV)

    spots = seq_index * here + jnp.arange(here, dtype=jnp.int32)
    own_starts = starts[:, 0]
    before = own_starts[:, None, :] <= spots[None, :, None]
    doc_begin = jnp.max(jnp.where(before, own_starts[:, None, :], 0), axis=2)
    relative = (spots[None, :] - doc_begin).astype(F32).reshape(-1)
    frequency = jnp.power(
        rope_theta, -jnp.arange(0, HEAD_SIZE, 2, dtype=F32) / HEAD_SIZE
    )
    angles = relative[:, None] * frequency[None, :]
    cos, sin = jnp.cos(angles), jnp.sin(angles)
    cos = jnp.concatenate([cos] * 4, axis=1)
    sin = jnp.concatenate([-sin, sin, -sin, sin], axis=1)
    begin = doc_begin + here - seq_index * here
    lo = begin[:, ::128] // 128
    begin = begin[:, :, None]

    x = inputs[:, 0].reshape(-1, D)
    cot = cotangent[:, 0].reshape(-1, D)
    cot_p = dot_nn(cot, pi).astype(BF16)
    cot_t = lax.dot_general(
        pi, cot, (((0,), (1,)), ((), ())), preferred_element_type=F32
    ).astype(BF16)

    xp, nl, q, k, v = project(
        x, pi, attention, gain_attn, bias, cos, sin, after=(line_a, shard_b)
    )
    line_b = stacked_rows(line_parts(places, shard_b), after=(q,))
    far_a = send(short_a, places.long)
    short_b, long_b = send(line_b, places.short), send(line_b, places.long)
    shard_c = shard_of((2, 3), (line_b,))

    forth = [(2 * n, 2 * n + 1) for n in range(n_dev // 2)]
    back = [(2 * n + 1, 2 * n) for n in range(n_dev // 2)]
    kv = send(jnp.concatenate([k, v], axis=1), forth)

    def streams(array):
        return array.reshape(MICRO, here, array.shape[-1])

    heads = (
        lo,
        streams(q),
        streams(kv[:, :KW]),
        streams(k),
        streams(kv[:, KW:]),
        streams(v),
        begin,
    )
    attended, lse = attend(*heads, after=(line_b, short_a, shard_c))
    attended_flat = attended.reshape(-1, QW)
    residual, normed, normed_t = middle(
        attended_flat, xp, attention, gain_mlp, after=(short_b,)
    )
    far_b = send(short_b, places.long)
    line_c = stacked_rows(line_parts(places, shard_c), after=(normed,))

    sums = None
    reductions, feed_pieces = [], []

    pieces = [[line_a, short_a, long_a, far_a], [line_b, short_b, long_b, far_b]]
    at = 0
    loads = []
    for n, wide in enumerate(CHUNKS):
        coming = (at, CHUNKS[n + 2]) if n + 2 < len(CHUNKS) else None
        moving = [r for r in reductions if r.next]
        loads = [load for r in moving for load in r.next]
        mlp, d_normed, kept, passed, far, *arrived = feed(
            n, wide, normed, normed_t, cot_p, cot_t, sums, pieces[n], line_c, coming, loads
        )
        sums = (mlp, d_normed)
        feed_pieces.append(list(pieces[n]) + [far])
        if coming:
            pieces.append([arrived.pop(0)])
            at += coming[1]
        hand_out(moving, arrived)
        reductions.append(Reduce(places, kept, passed))

    moving = [r for r in reductions if r.next]
    output, d_res, d_att, own_out, other_out, d_gain_mlp, *arrived = middle_back(
        residual, sums[0], sums[1], cot_p, attended_flat, pi, attention, gain_mlp,
        [load for r in moving for load in r.next],
    )
    hand_out(moving, arrived)
    moving = [r for r in reductions if r.next]
    along = {"long": places.long, "short": places.short}
    arrived = [
        send(array, along[kind] if kind in along else places.ahead[kind[0]])
        for r in moving
        for kind, array in r.next
    ]
    dq, dkv, dkv_recv = attend_back(
        *heads, attended, streams(d_att), lse,
        after=tuple(array for r in moving for _, array in r.next),
    )
    dkv_recv = send(dkv_recv, back)
    hand_out(moving, arrived, (dq,))
    moving = [r for r in reductions if r.next]
    input_grad, own_in, other_in, d_gain_attn, d_bias, *arrived = project_back(
        dq.reshape(-1, QW), dkv.reshape(-1, 2 * KW), dkv_recv.reshape(-1, 2 * KW),
        cos, sin, nl, xp, d_res, pi, attention, gain_attn,
        [load for r in moving for load in r.next],
    )
    hand_out(moving, arrived)

    d_gains = jnp.concatenate([d_gain_attn, d_gain_mlp, jnp.zeros((6, D), F32)], axis=0)
    high, rest = split_two(d_gains)
    d_gains = dot_nt(high, pi) + dot_nt(rest, pi)
    d_vectors = jnp.concatenate([d_gains[0], d_gains[1], d_bias[0]])
    d_vectors = jnp.pad(d_vectors.reshape(n_dev, vec_here), ((0, 0), (0, 128 - vec_here)))
    riders = dot_tn(riding, d_vectors.astype(BF16)).astype(BF16)
    moving = [r for r in reductions if r.next]
    grad_in, *arrived = reduce_tail(
        places,
        jnp.concatenate([own_in, riders[:HALF], own_out], axis=1),
        jnp.concatenate([other_in, riders[HALF:], other_out], axis=1),
        [load for r in moving for load in r.next],
    )
    hand_out(moving, arrived)

    capacity = first_moment.shape[0]
    slot_count = n_dev * capacity
    slot_block = (
        jnp.full((slot_count,), -1, jnp.int32)
        .at[owner_slot]
        .set(jnp.arange(owner_slot.shape[0], dtype=jnp.int32))
    )
    spots = [
        [(w, 2048 + m * FF + o) for m in range(3)] for o, w in zip(OFFSETS, CHUNKS)
    ]
    groups = [r.parts for r in reductions]
    for start, width, target in ((0, QKV, 0), (QKV, BW, 130 * BW), (QKV + BW, QW, QKV)):
        groups.append([grad_in[:, :, start : start + width]])
        spots.append([(width, target)])
    targets = [
        (0, QW), (QW, KW), (QW + KW, KW), (QKV, QW),
        (2048, FF), (2048 + FF, FF), (2048 + 2 * FF, FF), (130 * BW, BW),
    ]
    (
        grad_query, grad_key, grad_value, grad_out_t, grad_gate, grad_up, grad_down_t, rider_sums, slots,
    ) = packed(slot_block, groups, spots, targets)
    grad_vectors = rider_sums[0, :vec_here]
    owned_grads = lax.all_to_all(
        slots,
        BOTH,
        split_axis=0,
        concat_axis=1,
        tiled=True,
    )
    local_block = lax.dynamic_slice_in_dim(
        slot_block, lax.axis_index(BOTH) * capacity, capacity, 0
    )
    spans = [[(0, 16)]]
    for o, w in zip(OFFSETS, CHUNKS):
        first, count = o // BW, w // BW
        spans.append(
            [(16 + 38 * m + first, 16 + 38 * m + first + count) for m in range(3)]
        )
    owned_weights = picked(
        local_block, pi, [[attention_pages]] + feed_pieces, spans, after=(slots,)
    )
    new_first, new_second, new_blocks = rotated_adam(
        local_block, owned_grads, owned_weights, first_moment, second_moment, basis_left, basis_right
    )
    vector_second_new, vector_new = vector_adam(vectors, grad_vectors, vector_first, vector_second)
    return (
        output.reshape(inputs.shape),
        input_grad.reshape(inputs.shape),
        grad_query,
        grad_key,
        grad_value,
        grad_out_t.T,
        grad_gate,
        grad_up,
        grad_down_t.T,
        grad_vectors,
        new_first,
        new_second,
        new_blocks,
        vector_second_new,
        vector_new,
    )


def solution(mesh):
    rows = P(("dp", "seq"), None)
    columns = P(None, ("dp", "seq"))
    tokens = P(None, "dp", "seq", None)
    slots = P(("dp", "seq"), None, None)
    line = P(("dp", "seq"))
    places = Places(mesh.shape["dp"], mesh.shape["seq"])
    return jax.shard_map(
        functools.partial(on_device, places),
        mesh=mesh,
        in_specs=(
            tokens, tokens, P(None, "dp", None), rows, rows, rows, columns, rows, rows, columns,
            line, P(), slots, slots, slots, slots, line, line,
        ),
        out_specs=(
            tokens, tokens, rows, rows, rows, columns, rows, rows, columns, line,
            slots, slots, slots, line, line,
        ),
        check_vma=False,
    )
```

```python
import functools
import math

import jax
import jax.numpy as jnp
import numpy as np
from jax import lax
from jax.experimental import pallas as pl
from jax.experimental.pallas import tpu as pltpu
from jax.sharding import PartitionSpec as P

D = 896
QUERY_HEADS = 14
KEY_VALUE_HEADS = 2
HEAD_SIZE = 64
BW = 128
MICRO = 2
STEP = 10
QW = 896
KW = 128
QKV = QW + 2 * KW
FF = 4864

norm_epsilon = 1e-06
rope_theta = 1000000.0
beta_first = 0.9
beta_second = 0.999
adam_epsilon = 1e-08
weight_decay = 0.01
rate_matrix = 0.1
rate_vector = 0.5
masked_value = -1e30

F32 = jnp.float32
BF16 = jnp.bfloat16
BOTH = ("dp", "seq")

TILE = 256
CHUNKS = (1280, 1280, 1280, 1024)
OFFSETS = (0, 1280, 2560, 3840)
QUARTER = 112
HALF = 448
TOKEN_TILE = 256

HEAD_SETS = (
    ((0, 1, 2, 3), 0, 0),
    ((0, 1, 2), 1, 0),
    ((3, 4, 5, 6), 1, 1),
    ((4, 5, 6), 0, 1),
)
SET_ROWS = (0, 512, 896, 1408)
ALL_ROWS = 1792


def params(mib, **more):
    return pltpu.CompilerParams(vmem_limit_bytes=mib * 1024 * 1024, **more)


def dot_nn(a, b):
    return lax.dot_general(a, b, (((1,), (0,)), ((), ())), preferred_element_type=F32)


def dot_nt(a, b):
    return lax.dot_general(a, b, (((1,), (1,)), ((), ())), preferred_element_type=F32)


def dot_tn(a, b):
    return lax.dot_general(a, b, (((0,), (0,)), ((), ())), preferred_element_type=F32)


def following(kernel, n_in, after):
    def wrapped(*refs):
        return kernel(*refs[:n_in], *refs[n_in + len(after) :])

    return wrapped


TINY = pl.CostEstimate(flops=1, bytes_accessed=1, transcendentals=0)
ANYWHERE = pl.BlockSpec(memory_space=pl.ANY)


class Places:
    def __init__(self, n_dp, n_seq):
        self.line = n_dp // 4
        self.rows = D // (n_dp * n_seq)
        self.n_dev = n_dp * n_seq
        self.padded = -(-self.rows // 16) * 16

        def pairs(move):
            found = []
            for z in range(self.line):
                for x in range(2):
                    for c in range(2):
                        for y in range(2):
                            tz, tx, tc, ty = move(z, x, c, y)
                            found.append(
                                (((z * 2 + x) * 2 + c) * 2 + y, ((tz * 2 + tx) * 2 + tc) * 2 + ty)
                            )
            return found

        self.sibling = pairs(lambda z, x, c, y: (z, x, 1 - c, y))
        self.long = pairs(lambda z, x, c, y: (z, 1 - x, c, y) if c == 0 else (z, x, c, 1 - y))
        self.short = pairs(lambda z, x, c, y: (z, 1 - x, c, y) if c == 1 else (z, x, c, 1 - y))
        self.ahead = [
            pairs(lambda z, x, c, y, k=k: ((z + k) % self.line, x, c, y)) for k in range(self.line)
        ]

    def natural_rows(self):
        dp = lax.axis_index("dp")
        y = lax.axis_index("seq")
        z, x, c = dp // 4, (dp // 2) % 2, dp % 2
        place = jnp.arange(D, dtype=jnp.int32)
        dc, da, db = place // HALF, (place // (2 * QUARTER)) % 2, (place // QUARTER) % 2
        dz, inner = (place % QUARTER) // self.rows, place % self.rows
        c_own = c ^ dc
        x_own = x ^ jnp.where(c_own == 0, da, db)
        y_own = y ^ jnp.where(c_own == 0, db, da)
        z_own = (z + dz) % self.line
        return self.rows * (((z_own * 2 + x_own) * 2 + c_own) * 2 + y_own) + inner


def send(array, pairs):
    return lax.ppermute(array, BOTH, pairs)


def line_parts(places, shard, last=None):
    count = places.line
    return [shard] + [
        send(shard if last is None or k < count - 1 else last, places.ahead[-k % count])
        for k in range(1, count)
    ]


def stack_kernel(count, *refs):
    ins, (out, scr) = refs[:count], refs[count:]
    rows = QUARTER // count
    for k, ref in enumerate(ins):
        scr[rows * k : rows * (k + 1), :] = ref[0, :rows].astype(F32)
    out[0] = scr[...].astype(BF16)


def stacked_rows(parts, after=()):
    pages, rows, width = parts[0].shape
    return pl.pallas_call(
        following(functools.partial(stack_kernel, len(parts)), len(parts), after),
        grid=(pages,),
        in_specs=[pl.BlockSpec((1, rows, width), lambda m: (m, 0, 0))] * len(parts)
        + [ANYWHERE] * len(after),
        out_specs=pl.BlockSpec((1, QUARTER, width), lambda m: (m, 0, 0)),
        out_shape=jax.ShapeDtypeStruct((pages, QUARTER, width), BF16),
        scratch_shapes=[pltpu.VMEM((QUARTER, width), F32)],
        compiler_params=params(60),
        cost_estimate=TINY,
        name="stacked_rows",
    )(*parts, *after)


def neighbours():
    dp, seq = lax.axis_index("dp"), lax.axis_index("seq")
    core = lax.rem(dp, 2)
    first = dp + 2 - 4 * lax.rem(dp // 2, 2)
    sibling = (dp + 1 - 2 * core, seq)
    long = (jnp.where(core == 0, first, dp), jnp.where(core == 0, seq, 1 - seq))
    short = (jnp.where(core == 0, dp, first), jnp.where(core == 0, 1 - seq, seq))
    return sibling, long, short


def greet(devices):
    barrier = pltpu.get_barrier_semaphore()
    for device in devices:
        pl.semaphore_signal(barrier, inc=1, device_id=device, device_id_type=pl.DeviceIdType.MESH)
    pl.semaphore_wait(barrier, len(devices))


def push(src, dst, sems, n, device):
    return pltpu.make_async_remote_copy(
        src_ref=src,
        dst_ref=dst,
        send_sem=sems.at[0, n],
        recv_sem=sems.at[1, n],
        device_id=device,
        device_id_type=pl.DeviceIdType.MESH,
    )


def quarter(ref, k):
    return ref.at[:, pl.ds(QUARTER * k, QUARTER), :]


def device_of(kind):
    if isinstance(kind, str):
        return dict(zip(("sibling", "long", "short"), neighbours()))[kind]
    ahead, line = kind
    dp = lax.axis_index("dp")
    return (lax.rem(dp // 4 + ahead, line) * 4 + lax.rem(dp, 4), lax.axis_index("seq"))


def greet_kinds(kinds):
    found = []
    for kind in kinds:
        if kind not in found:
            found.append(kind)
    greet([device_of(kind) for kind in found])


def carried(kinds, srcs, dsts, sems):
    return [
        push(src, dst, sems, n, device_of(kind))
        for n, (kind, src, dst) in enumerate(zip(kinds, srcs, dsts))
    ]


def carrying(kernel, kinds, n_in, n_out):
    count = len(kinds)

    def wrapped(*refs):
        ins, srcs = refs[:n_in], refs[n_in : n_in + count]
        at = n_in + count
        outs, dsts = refs[at : at + n_out], refs[at + n_out : at + n_out + count]
        scratch, sems = refs[at + n_out + count : -1], refs[-1]

        @pl.when(pl.program_id(0) == 0)
        def _():
            greet_kinds(kinds)
            for move in carried(kinds, srcs, dsts, sems):
                move.start()

        kernel(*ins, *outs, *scratch)

        @pl.when(pl.program_id(0) == pl.num_programs(0) - 1)
        def _():
            for move in carried(kinds, srcs, dsts, sems):
                move.wait()

    return wrapped


def like(array):
    return jax.ShapeDtypeStruct(array.shape, array.dtype)


def spread_kernel(kinds, own, *refs):
    count = len(kinds)
    srcs, out, dsts, (sems, here_sem, more_sems) = (
        refs[:count], refs[count], refs[count + 1 : 2 * count + 1], refs[2 * count + 1 :],
    )
    sibling, long, short = neighbours()
    greet_kinds(("sibling", "long", "short") + tuple(kinds))
    for move in carried(kinds, srcs, dsts, more_sems):
        move.start()
    here = pltpu.make_async_copy(own, quarter(out, 0), here_sem)
    moves = [
        push(own, quarter(out, 1), sems, 0, short),
        push(own, quarter(out, 2), sems, 1, long),
        push(own, quarter(out, 4), sems, 2, sibling),
    ]
    here.start()
    for move in moves:
        move.start()
    for k, first in ((1, 3), (2, None), (3, None)):
        moves[{1: 0, 2: 1, 3: 3}[k]].wait_recv()
        if first is not None:
            moves.append(push(quarter(out, 1), quarter(out, 3), sems, 3, long))
            moves[-1].start()
        moves.append(push(quarter(out, k), quarter(out, 4 + k), sems, 3 + k, sibling))
        moves[-1].start()
    here.wait()
    for n, move in enumerate(moves):
        move.wait_send()
        if n not in (0, 1, 3):
            move.wait_recv()
    for move in carried(kinds, srcs, dsts, more_sems):
        move.wait()


def spread(own, loads):
    kinds = tuple(kind for kind, _ in loads)
    return pl.pallas_call(
        functools.partial(spread_kernel, kinds),
        in_specs=[ANYWHERE] * (1 + len(loads)),
        out_specs=[ANYWHERE] * (1 + len(loads)),
        out_shape=[jax.ShapeDtypeStruct((1, D, own.shape[2]), BF16)] + [like(a) for _, a in loads],
        scratch_shapes=[
            pltpu.SemaphoreType.DMA((2, 7)),
            pltpu.SemaphoreType.DMA,
            pltpu.SemaphoreType.DMA((2, max(1, len(loads)))),
        ],
        compiler_params=params(60, collective_id=8, has_side_effects=True),
        cost_estimate=TINY,
        name="spread",
    )(own, *[array for _, array in loads])


def fold_kernel(count, *refs):
    total = refs[0][...].astype(F32)
    for ref in refs[1:count]:
        total = total + ref[...].astype(F32)
    refs[count][...] = total.astype(BF16)


def fold(terms, rows, after=()):
    pages, _, width = terms[0][0].shape

    def spec(block):
        return pl.BlockSpec((1, rows, width), lambda m: (m, block, 0))

    return pl.pallas_call(
        following(functools.partial(fold_kernel, len(terms)), len(terms), after),
        grid=(pages,),
        in_specs=[spec(block) for _, block in terms] + [ANYWHERE] * len(after),
        out_specs=spec(0),
        out_shape=jax.ShapeDtypeStruct((pages, rows, width), BF16),
        compiler_params=params(60),
        cost_estimate=TINY,
        name="fold",
    )(*[array for array, _ in terms], *after)


def share_kernel(count, rows, *refs):
    scr = refs[-1]
    outs = refs[count:-1]
    total = refs[0][0].astype(F32)
    for ref in refs[1:count]:
        total = total + ref[0].astype(F32)
    scr[...] = total
    for k, ref in enumerate(outs):
        ref[0, :rows] = scr[rows * k : rows * (k + 1), :].astype(ref.dtype)


def share(terms, rows, padded, line, after=()):
    pages, _, width = terms[0].shape
    part = [
        pl.BlockSpec((1, padded if k else rows, width), lambda m: (m, 0, 0)) for k in range(line)
    ]
    return pl.pallas_call(
        following(functools.partial(share_kernel, len(terms), rows), len(terms), after),
        grid=(pages,),
        in_specs=[pl.BlockSpec((1, QUARTER, width), lambda m: (m, 0, 0))] * len(terms)
        + [ANYWHERE] * len(after),
        out_specs=part,
        out_shape=[
            jax.ShapeDtypeStruct((pages, padded if k else rows, width), BF16 if k else F32)
            for k in range(line)
        ],
        scratch_shapes=[pltpu.VMEM((QUARTER, width), F32)],
        compiler_params=params(60),
        cost_estimate=TINY,
        name="share",
    )(*terms, *after)


class Reduce:
    def __init__(self, places, kept, passed):
        self.places, self.terms = places, [kept]
        self.next = [("long", passed)]

    def fold(self, arrived, after):
        self.terms.append(arrived[0])
        self.next = [("short", fold([(t, 1) for t in self.terms], QUARTER, after))]

    def share(self, arrived, after):
        self.terms.append(arrived[0])
        line = self.places.line
        mine, *parts = share(self.terms, self.places.rows, self.places.padded, line, after)
        self.parts = [mine]
        self.next = [((k + 1, line), part) for k, part in enumerate(parts)]

    def end(self, arrived):
        self.parts += list(arrived)


def tail_kernel(line, rows, widths, load_kinds, *refs):
    parts_n, count = len(widths), len(load_kinds)
    owns, others = refs[:parts_n], refs[parts_n : 2 * parts_n]
    at = 2 * parts_n
    srcs, out, dsts = refs[at : at + count], refs[at + count], refs[at + count + 1 : at + 2 * count + 1]
    came, half, came_half, quart, came_quart, keep, parts, came_parts, sems, load_sems = refs[
        at + 2 * count + 1 :
    ]
    starts = [sum(widths[:n]) for n in range(parts_n)]
    spans = [slice(start, start + width) for start, width in zip(starts, widths)]
    sibling, long, short = neighbours()
    greet_kinds(["sibling", "long", "short"] + [(k, line) for k in range(1, line)])
    moves = []

    def go(src, dst, device):
        moves.append(push(src, dst, sems, len(moves), device))
        moves[-1].start()
        return moves[-1]

    first = [go(others[n], came.at[:, span], sibling) for n, span in enumerate(spans)]
    for move in carried(load_kinds, srcs, dsts, load_sems):
        move.start()
    two = 2 * QUARTER
    second, third, last = [], [], []
    for n, span in enumerate(spans):
        first[n].wait_recv()
        half[:, span] = (owns[n][two:].astype(F32) + came[two:, span].astype(F32)).astype(BF16)
        second.append(go(half.at[:, span], came_half.at[:, span], long))
        keep[:, span] = owns[n][:two].astype(F32) + came[:two, span].astype(F32)
    for n, span in enumerate(spans):
        second[n].wait_recv()
        total = keep[QUARTER:, span] + came_half[QUARTER:, span].astype(F32)
        quart[:, span] = total.astype(BF16)
        third.append(go(quart.at[:, span], came_quart.at[:, span], short))
        keep[:QUARTER, span] = keep[:QUARTER, span] + came_half[:QUARTER, span].astype(F32)
    for n, span in enumerate(spans):
        third[n].wait_recv()
        keep[:QUARTER, span] = keep[:QUARTER, span] + came_quart[:, span].astype(F32)
        for k in range(1, line):
            parts[k - 1, :rows, span] = keep[rows * k : rows * (k + 1), span].astype(BF16)
            last.append(
                go(parts.at[k - 1, :, span], came_parts.at[k - 1, :, span], device_of((k, line)))
            )
    for n, span in enumerate(spans):
        total = keep[:rows, span]
        for k in range(1, line):
            last[n * (line - 1) + k - 1].wait_recv()
            total = total + came_parts[k - 1, :rows, span].astype(F32)
        out[0, :, span] = total
    for move in moves:
        move.wait_send()
    for move in carried(load_kinds, srcs, dsts, load_sems):
        move.wait()


def reduce_tail(places, owns, others, loads):
    widths, line, padded = [a.shape[1] for a in owns], places.line, places.padded
    width = sum(widths)
    vmem = pl.BlockSpec(memory_space=pltpu.VMEM)
    return pl.pallas_call(
        functools.partial(
            tail_kernel, line, places.rows, widths, tuple(kind for kind, _ in loads)
        ),
        in_specs=[vmem] * (2 * len(owns)) + [ANYWHERE] * len(loads),
        out_specs=[vmem] + [ANYWHERE] * len(loads),
        out_shape=[jax.ShapeDtypeStruct((1, places.rows, width), F32)] + [like(a) for _, a in loads],
        scratch_shapes=[
            pltpu.VMEM((HALF, width), BF16),
            pltpu.VMEM((2 * QUARTER, width), BF16),
            pltpu.VMEM((2 * QUARTER, width), BF16),
            pltpu.VMEM((QUARTER, width), BF16),
            pltpu.VMEM((QUARTER, width), BF16),
            pltpu.VMEM((2 * QUARTER, width), F32),
            pltpu.VMEM((line - 1, padded, width), BF16),
            pltpu.VMEM((line - 1, padded, width), BF16),
            pltpu.SemaphoreType.DMA((2, len(owns) * (2 + line))),
            pltpu.SemaphoreType.DMA((2, max(1, len(loads)))),
        ],
        compiler_params=params(56, collective_id=11, has_side_effects=True),
        cost_estimate=TINY,
        name="reduce_tail",
    )(*owns, *others, *[array for _, array in loads])


def round_kernel(spans, *refs):
    ins, out = refs[:-1], refs[-1]
    at = [0] * out.shape[0]
    for page, which, offset, width in spans:
        piece = ins[which][:, offset : offset + width]
        out[page, : piece.shape[0], at[page] : at[page] + width] = piece.astype(BF16)
        at[page] += width


def rounded(parts, padded, spans, after=()):
    pages = 1 + max(page for page, _, _, _ in spans)
    width = sum(width for page, _, _, width in spans if page == 0)
    return pl.pallas_call(
        following(functools.partial(round_kernel, spans), len(parts), after),
        in_specs=[pl.BlockSpec(memory_space=pltpu.VMEM)] * len(parts) + [ANYWHERE] * len(after),
        out_specs=pl.BlockSpec(memory_space=pltpu.VMEM),
        out_shape=jax.ShapeDtypeStruct((pages, padded, width), BF16),
        compiler_params=params(60),
        cost_estimate=TINY,
        name="rounded",
    )(*parts, *after)


def swap_halves(tile, low_half):
    return jnp.where(low_half, pltpu.roll(tile, 96, 1), pltpu.roll(tile, 32, 1))


def project_kernel(x_ref, pi_ref, *refs):
    (
        w_ref, gain_ref, bias_ref, cos_ref, sin_ref, xp_ref, nl_ref, q_ref, k_ref, v_ref, came_hbm,
        kv_scr, sems,
    ) = refs
    step, steps = pl.program_id(0), kv_scr.shape[0] // TOKEN_TILE
    seq = lax.axis_index("seq")
    other = (lax.axis_index("dp"), 1 - seq)

    def hand_on(n):
        rows = pl.ds(pl.multiple_of(n * TOKEN_TILE, TOKEN_TILE), TOKEN_TILE)
        return push(kv_scr.at[rows, :], came_hbm.at[rows, :], sems, n, other)

    @pl.when(step == 0)
    def _():
        greet([other])

    xp = dot_nn(x_ref[...], pi_ref[...])
    inv = lax.rsqrt(jnp.sum(xp * xp, axis=1, keepdims=True) * (1.0 / D) + norm_epsilon)
    nl = (xp * inv * gain_ref[...]).astype(BF16)
    xp_ref[...] = xp.astype(BF16)
    nl_ref[...] = nl
    lin = dot_nn(nl, w_ref[:, :QKV]) + bias_ref[...]
    cos, sin = cos_ref[...], sin_ref[...]
    low = lax.broadcasted_iota(jnp.int32, cos.shape, 1) % HEAD_SIZE < HEAD_SIZE // 2
    for t in range(8):
        piece = lin[:, 128 * t : 128 * (t + 1)]
        turned = (piece * cos + swap_halves(piece, low) * sin).astype(BF16)
        if t < 7:
            q_ref[:, 128 * t : 128 * (t + 1)] = (turned.astype(F32) * 0.125).astype(BF16)
        else:
            k_ref[...] = turned
            kv_scr[pl.ds(pl.multiple_of(step * TOKEN_TILE, TOKEN_TILE), TOKEN_TILE), :KW] = turned
    value = lin[:, QW + KW :].astype(BF16)
    v_ref[...] = value
    kv_scr[pl.ds(pl.multiple_of(step * TOKEN_TILE, TOKEN_TILE), TOKEN_TILE), KW:] = value

    @pl.when(seq == 0)
    def _():
        hand_on(step).start()

    @pl.when((step == steps - 1) & (seq == 0))
    def _():
        for n in range(steps):
            hand_on(n).wait_send()

    @pl.when((step == steps - 1) & (seq == 1))
    def _():
        for n in range(steps):
            hand_on(n).wait_recv()


def project(x, pi, weights, gain, bias, cos, sin, after=()):
    rows = x.shape[0]
    width = weights.shape[1]

    def tile(cols):
        return pl.BlockSpec((TOKEN_TILE, cols), lambda t: (t, 0))

    def whole(r, c):
        return pl.BlockSpec((r, c), lambda t: (0, 0))

    shapes = [(D, BF16), (D, BF16), (QW, BF16), (KW, BF16), (KW, BF16)]
    return pl.pallas_call(
        following(project_kernel, 7, after),
        grid=(rows // TOKEN_TILE,),
        in_specs=[tile(D), whole(D, D)]
        + [whole(D, width)]
        + [whole(1, D), whole(1, QKV), tile(128), tile(128)]
        + [ANYWHERE] * len(after),
        out_specs=[tile(c) for c, _ in shapes] + [ANYWHERE],
        out_shape=[jax.ShapeDtypeStruct((rows, c), t) for c, t in shapes + [(2 * KW, BF16)]],
        scratch_shapes=[
            pltpu.VMEM((rows, 2 * KW), BF16),
            pltpu.SemaphoreType.DMA((2, rows // TOKEN_TILE)),
        ],
        compiler_params=params(56, collective_id=12, has_side_effects=True),
        cost_estimate=TINY,
        name="project",
    )(x, pi, weights, gain, bias, cos, sin, *after)


def padded_heads(recv, own, out, turned):
    for part, ref in enumerate((recv, own)):
        natural = ref[0].astype(F32)
        span = pl.ds(512 * part, 512)
        if out is not None:
            lane = lax.broadcasted_iota(jnp.int32, (512, 128), 1)
            crossed = pltpu.roll(natural, 64, 1)
            for s, (_, half, head) in enumerate(HEAD_SETS):
                source = natural if half == head else crossed
                keep = (lane >= 64) if half else (lane < 64)
                out[s, span, :] = jnp.where(keep, source, 0.0).astype(BF16)
        if turned is not None:
            flat = natural.T
            other = jnp.concatenate([flat[64:], flat[:64]], axis=0)
            row = lax.broadcasted_iota(jnp.int32, (128, 512), 0)
            for s, (_, half, head) in enumerate(HEAD_SETS):
                source = flat if half == head else other
                keep = (row >= 64) if half else (row < 64)
                turned[s, :, span] = jnp.where(keep, source, 0.0).astype(BF16)


def block_bias(kb, i, begin):
    shape = (128, 128)
    key = kb * 128 + lax.broadcasted_iota(jnp.int32, shape, 0)
    query = 512 + i * 128 + lax.broadcasted_iota(jnp.int32, shape, 1)
    return jnp.where((key >= begin) & (key <= query), 0.0, masked_value)


def stacked(tile_of, pairs):
    return jnp.concatenate([tile_of(p) for p in pairs], axis=0)


def turned_block(ref, out):
    for p in range(7):
        cols = slice(128 * p, 128 * (p + 1))
        out[:, cols] = ref[0, :, cols].astype(F32).T.astype(BF16)


def pair_columns(s):
    pairs = HEAD_SETS[s][0]
    return slice(128 * pairs[0], 128 * (pairs[-1] + 1))


def columns_of(s, n=None):
    pairs = HEAD_SETS[s][0]
    if n is None:
        return slice(SET_ROWS[s], SET_ROWS[s] + 128 * len(pairs))
    return slice(SET_ROWS[s] + 128 * n, SET_ROWS[s] + 128 * (n + 1))


def eights(value):
    return value.reshape(value.shape[0] // 8, 8, value.shape[1])


def attend_kernel(
    lo_ref, q_ref, kr_ref, ko_ref, vr_ref, vo_ref, ds_ref, o_ref, lse_ref, kp, vt, qt, s_scr, m_scr, l_scr, acc
):
    b, i = pl.program_id(0), pl.program_id(1)

    @pl.when(i == 0)
    def _():
        padded_heads(kr_ref, ko_ref, kp, None)
        padded_heads(vr_ref, vo_ref, None, vt)

    lo, hi = lo_ref[b, i], i + 5
    begin = ds_ref[0]
    turned_block(q_ref, qt)
    m_scr[...] = jnp.full(m_scr.shape, masked_value, F32)
    l_scr[...] = jnp.zeros(l_scr.shape, F32)
    acc[...] = jnp.zeros(acc.shape, F32)

    def scores(kb, carry):
        bias = block_bias(kb, i, begin)
        keys = pl.ds(pl.multiple_of(kb * 128, 128), 128)
        raws = [dot_nn(kp[s, keys, :], qt[:, pair_columns(s)]) for s in range(4)]
        for s, (pairs, _, _) in enumerate(HEAD_SETS):
            cols = columns_of(s)
            value = raws[s] + jnp.concatenate([bias] * len(pairs), axis=1)
            s_scr[kb, :, cols] = value
            m_scr[:, cols] = jnp.maximum(m_scr[:, cols], jnp.max(eights(value), axis=0))
        return carry

    lax.fori_loop(lo, hi, scores, 0)
    top = jnp.max(m_scr[...], axis=0, keepdims=True)

    def weigh(kb, carry):
        keys = pl.ds(pl.multiple_of(kb * 128, 128), 128)
        probs = [jnp.exp(s_scr[kb, :, columns_of(s)] - top[:, columns_of(s)]) for s in range(4)]
        parts = [dot_nn(vt[s, :, keys], probs[s].astype(BF16)) for s in range(4)]
        for s in range(4):
            cols = columns_of(s)
            l_scr[:, cols] += jnp.sum(eights(probs[s]), axis=0)
            acc[:, cols] += parts[s]
        return carry

    lax.fori_loop(lo, hi, weigh, 0)
    total = jnp.sum(l_scr[...], axis=0, keepdims=True)
    lse = top + jnp.log(total)
    share = 1.0 / total
    outs = [None] * 7
    for s, (pairs, half, _) in enumerate(HEAD_SETS):
        for n, p in enumerate(pairs):
            cols = columns_of(s, n)
            part = acc[:, cols] * share[:, cols]
            outs[p] = part if outs[p] is None else outs[p] + part
            head = 2 * p + half
            lse_ref[0, head : head + 1, :] = lse[:, cols]
    for p in range(7):
        o_ref[0, :, 128 * p : 128 * (p + 1)] = outs[p].T.astype(BF16)


def attend_specs():
    def block(cols):
        return pl.BlockSpec((1, 128, cols), lambda b, i, lo: (b, i, 0))

    def lanes(rows):
        return pl.BlockSpec((1, rows, 128), lambda b, i, lo: (b, 0, i))

    def stream(cols):
        return pl.BlockSpec((1, 512, cols), lambda b, i, lo: (b, 0, 0))

    return block, lanes, stream


def attend(lo, q, k_recv, k_own, v_recv, v_own, begin, after=()):
    block, lanes, stream = attend_specs()
    return pl.pallas_call(
        following(attend_kernel, 7, after),
        grid_spec=pltpu.PrefetchScalarGridSpec(
            num_scalar_prefetch=1,
            grid=(MICRO, 4),
            in_specs=[block(QW)] + [stream(KW)] * 4 + [lanes(1)] + [ANYWHERE] * len(after),
            out_specs=[block(QW), lanes(16)],
            scratch_shapes=[
                pltpu.VMEM((4, 1024, 128), BF16),
                pltpu.VMEM((4, 128, 1024), BF16),
                pltpu.VMEM((128, QW), BF16),
                pltpu.VMEM((8, 128, ALL_ROWS), F32),
                pltpu.VMEM((8, ALL_ROWS), F32),
                pltpu.VMEM((8, ALL_ROWS), F32),
                pltpu.VMEM((128, ALL_ROWS), F32),
            ],
        ),
        out_shape=[
            jax.ShapeDtypeStruct((MICRO, 512, QW), BF16),
            jax.ShapeDtypeStruct((MICRO, 16, 512), F32),
        ],
        compiler_params=params(56),
        cost_estimate=TINY,
        name="attend",
    )(lo, q, k_recv, k_own, v_recv, v_own, begin, *after)


def attend_back_kernel(
    lo_ref, q_ref, kr_ref, ko_ref, vr_ref, vo_ref, ds_ref, o_ref, do_ref, lse_ref,
    dq_ref, own_ref, recv_ref, kp, vp, kt, qt, dot_t, dk, dv, dq_acc,
):
    b, i = pl.program_id(0), pl.program_id(1)

    @pl.when(i == 0)
    def _():
        padded_heads(kr_ref, ko_ref, kp, kt)
        padded_heads(vr_ref, vo_ref, vp, None)
        dk[...] = jnp.zeros(dk.shape, F32)
        dv[...] = jnp.zeros(dv.shape, F32)

    lo, hi = lo_ref[b, i], i + 5
    begin = ds_ref[0]
    dq_acc[...] = jnp.zeros(dq_acc.shape, F32)
    turned_block(q_ref, qt)
    turned_block(do_ref, dot_t)
    pick = lax.broadcasted_iota(jnp.int32, (8, 128), 1) // 64 == lax.broadcasted_iota(
        jnp.int32, (8, 128), 0
    )
    pick = pick.astype(F32).astype(BF16)
    halves = []
    for p in range(7):
        cols = slice(128 * p, 128 * (p + 1))
        high, rest = split_two(o_ref[0, :, cols].astype(F32) * do_ref[0, :, cols].astype(F32))
        halves.append(dot_nt(pick, high) + dot_nt(pick, rest))
    lse, dots = [], []
    for pairs, half, _ in HEAD_SETS:
        heads = [2 * p + half for p in pairs]
        lse.append(jnp.concatenate([lse_ref[0, h : h + 1, :] for h in heads], axis=1))
        dots.append(jnp.concatenate([halves[p][half : half + 1] for p in pairs], axis=1))

    def one_block(kb, carry):
        bias = block_bias(kb, i, begin)
        keys = pl.ds(pl.multiple_of(kb * 128, 128), 128)
        work = []
        for s, (pairs, _, _) in enumerate(HEAD_SETS):
            cols = columns_of(s)
            x = stacked(lambda p: q_ref[0, :, 128 * p : 128 * (p + 1)], pairs)
            y = stacked(lambda p: do_ref[0, :, 128 * p : 128 * (p + 1)], pairs)
            raw = dot_nn(kp[s, keys, :], qt[:, pair_columns(s)]) + jnp.concatenate([bias] * len(pairs), axis=1)
            d_prob = dot_nn(vp[s, keys, :], dot_t[:, pair_columns(s)])
            work.append((s, cols, x, y, raw, d_prob))
        parts = []
        for s, cols, x, y, raw, d_prob in work:
            p = jnp.exp(raw - lse[s])
            d_score = (p * (d_prob - dots[s])).astype(BF16)
            parts.append((s, cols, x, y, p.astype(BF16), d_score))
        sums = [
            (s, cols, dot_nn(kt[s, :, keys], d_score), dot_nn(d_score, x), dot_nn(p, y))
            for s, cols, x, y, p, d_score in parts
        ]
        for s, cols, d_query, d_key, d_value in sums:
            dq_acc[:, cols] += d_query
            dk[s, keys, :] += d_key
            dv[s, keys, :] += d_value
        return carry

    lax.fori_loop(lo, hi, one_block, 0)
    sums = [None] * 7
    for s, (pairs, _, _) in enumerate(HEAD_SETS):
        for n, p in enumerate(pairs):
            part = dq_acc[:, columns_of(s, n)]
            sums[p] = part if sums[p] is None else sums[p] + part
    for p in range(7):
        dq_ref[0, :, 128 * p : 128 * (p + 1)] = (sums[p] * 0.125).T.astype(BF16)

    @pl.when(i == 3)
    def _():
        wide = lax.broadcasted_iota(jnp.int32, (512, 128), 1) < 64
        for part, ref in enumerate((recv_ref, own_ref)):
            rows = pl.ds(512 * part, 512)
            for n, grads in enumerate((dk, dv)):
                low = grads[0, rows, :] + pltpu.roll(grads[1, rows, :], 64, 1)
                high = grads[2, rows, :] + pltpu.roll(grads[3, rows, :], 64, 1)
                value = jnp.where(wide, low, high)
                ref[0, :, 128 * n : 128 * (n + 1)] = value.astype(ref.dtype)


def attend_back(lo, q, k_recv, k_own, v_recv, v_own, begin, out, d_out, lse, after=()):
    block, lanes, stream = attend_specs()
    return pl.pallas_call(
        following(attend_back_kernel, 10, after),
        grid_spec=pltpu.PrefetchScalarGridSpec(
            num_scalar_prefetch=1,
            grid=(MICRO, 4),
            in_specs=[block(QW)]
            + [stream(KW)] * 4
            + [lanes(1), block(QW), block(QW), lanes(16)]
            + [ANYWHERE] * len(after),
            out_specs=[block(QW), stream(256), stream(256)],
            scratch_shapes=[
                pltpu.VMEM((4, 1024, 128), BF16),
                pltpu.VMEM((4, 1024, 128), BF16),
                pltpu.VMEM((4, 128, 1024), BF16),
                pltpu.VMEM((128, QW), BF16),
                pltpu.VMEM((128, QW), BF16),
                pltpu.VMEM((4, 1024, 128), F32),
                pltpu.VMEM((4, 1024, 128), F32),
                pltpu.VMEM((128, ALL_ROWS), F32),
            ],
        ),
        out_shape=[
            jax.ShapeDtypeStruct((MICRO, 512, QW), BF16),
            jax.ShapeDtypeStruct((MICRO, 512, 256), F32),
            jax.ShapeDtypeStruct((MICRO, 512, 256), BF16),
        ],
        compiler_params=params(56),
        cost_estimate=TINY,
        name="attend_back",
    )(lo, q, k_recv, k_own, v_recv, v_own, begin, out, d_out, lse, *after)


def middle_kernel(att_ref, xp_ref, *refs):
    w_ref, gain_ref, res_ref, n_ref, nt_ref = refs
    residual = xp_ref[...].astype(F32) + dot_nt(att_ref[...], w_ref[:, QKV : QKV + QW])
    inv = lax.rsqrt(jnp.sum(residual * residual, axis=1, keepdims=True) * (1.0 / D) + norm_epsilon)
    normed = residual * inv * gain_ref[...]
    res_ref[...] = residual
    n_ref[...] = normed.astype(BF16)
    nt_ref[...] = normed.T.astype(BF16)


def middle(attended, xp, weights, gain, after=()):
    rows = xp.shape[0]
    width = weights.shape[1]

    def tile(cols):
        return pl.BlockSpec((TOKEN_TILE, cols), lambda t: (t, 0))

    def whole(r, c):
        return pl.BlockSpec((r, c), lambda t: (0, 0))

    return pl.pallas_call(
        following(middle_kernel, 4, after),
        grid=(rows // TOKEN_TILE,),
        in_specs=[tile(QW), tile(D)]
        + [whole(D, width)]
        + [whole(1, D)]
        + [ANYWHERE] * len(after),
        out_specs=[tile(D), tile(D), pl.BlockSpec((D, TOKEN_TILE), lambda t: (0, t))],
        out_shape=[
            jax.ShapeDtypeStruct((rows, D), F32),
            jax.ShapeDtypeStruct((rows, D), BF16),
            jax.ShapeDtypeStruct((D, rows), BF16),
        ],
        compiler_params=params(56),
        cost_estimate=TINY,
        name="middle",
    )(attended, xp, weights, gain, *after)


def middle_back_kernel(res_ref, mlp_ref, dn_ref, cot_ref, att_ref, pi_ref, *refs):
    w_ref, gain_ref, out_ref, dres_ref, datt_ref, own_ref, sib_ref, dgain_ref, g_scr = refs
    t = pl.program_id(0)

    @pl.when(t == 0)
    def _():
        g_scr[...] = jnp.zeros(g_scr.shape, F32)
        dgain_ref[...] = jnp.zeros(dgain_ref.shape, F32)

    residual = res_ref[...]
    inv = lax.rsqrt(jnp.sum(residual * residual, axis=1, keepdims=True) * (1.0 / D) + norm_epsilon)
    out_low = (residual + mlp_ref[...]).astype(BF16)
    out_ref[...] = dot_nt(out_low, pi_ref[...]).astype(BF16)
    d_normed = dn_ref[...]
    hat = residual * inv
    scaled = d_normed * gain_ref[...]
    dgain_ref[...] += jnp.sum(d_normed * hat, axis=0, keepdims=True)
    mean = jnp.sum(scaled * hat, axis=1, keepdims=True) * (1.0 / D)
    d_res = cot_ref[...].astype(F32) + inv * (scaled - hat * mean)
    dres_ref[...] = d_res
    low = d_res.astype(BF16)
    datt_ref[...] = dot_nn(low, w_ref[:, QKV : QKV + QW]).astype(BF16)
    g_scr[...] += dot_tn(low, att_ref[...])

    @pl.when(t == pl.num_programs(0) - 1)
    def _():
        own_ref[...] = g_scr[:HALF].astype(BF16)
        sib_ref[...] = g_scr[HALF:].astype(BF16)


def middle_back(residual, mlp, d_normed, cot, attended, pi, weights, gain, after=()):
    rows = residual.shape[0]
    width = weights.shape[1]

    def tile(cols):
        return pl.BlockSpec((TOKEN_TILE, cols), lambda t: (t, 0))

    def whole(r, c):
        return pl.BlockSpec((r, c), lambda t: (0, 0))

    return pl.pallas_call(
        following(middle_back_kernel, 8, after),
        grid=(rows // TOKEN_TILE,),
        in_specs=[tile(D)] * 4
        + [tile(QW), whole(D, D)]
        + [whole(D, width)]
        + [whole(1, D)]
        + [ANYWHERE] * len(after),
        out_specs=[tile(D), tile(D), tile(QW), whole(HALF, QW), whole(HALF, QW), whole(1, D)],
        out_shape=[
            jax.ShapeDtypeStruct((rows, D), BF16),
            jax.ShapeDtypeStruct((rows, D), F32),
            jax.ShapeDtypeStruct((rows, QW), BF16),
            jax.ShapeDtypeStruct((HALF, QW), BF16),
            jax.ShapeDtypeStruct((HALF, QW), BF16),
            jax.ShapeDtypeStruct((1, D), F32),
        ],
        scratch_shapes=[pltpu.VMEM((D, QW), F32)],
        compiler_params=params(56),
        cost_estimate=TINY,
        name="middle_back",
    )(residual, mlp, d_normed, cot, attended, pi, weights, gain, *after)


def feed_kernel(wide, started, n_pieces, coming, kinds, *refs):
    n_in = 4 + (2 if started else 0)
    n_hbm, nt_hbm, cot_hbm, cott_hbm = refs[:4]
    sums_in = refs[4:n_in]
    pieces = refs[n_in : n_in + n_pieces]
    n_in += n_pieces
    if coming:
        line_hbm = refs[n_in]
        n_in += 1
    srcs = refs[n_in : n_in + len(kinds)]
    n_in += len(kinds)
    mlp_hbm, dn_hbm, keep_hbm, pass_hbm, far_hbm = refs[n_in : n_in + 5]
    n_in += 5
    if coming:
        next_hbm = refs[n_in]
        n_in += 1
    dsts = refs[n_in : n_in + len(kinds)]
    n_in += len(kinds)
    (
        n_v, nt_v, cot_v, cott_v, w_v, mlp_v, dn_v, act_v, grad_v, came_v,
        in_sem, w_sem, w_send, w_recv, out_sem, g_sem, g_send, g_recv, next_sem, next_here,
        carry_sem,
    ) = refs[n_in:]
    rows_all = n_v.shape[0]
    steps = wide // TILE
    span = 512
    parts = rows_all // span
    sibling, long, short = neighbours()
    mesh_id = pl.DeviceIdType.MESH
    share_rows = HALF // n_pieces

    def tile_of(j):
        return pl.ds(pl.multiple_of(j * TILE, TILE), TILE)

    def weight_copy(k, j):
        return pltpu.make_async_copy(
            pieces[k].at[:, :, tile_of(j)],
            w_v.at[:, pl.ds(share_rows * k, share_rows), tile_of(j)],
            w_sem.at[k, j],
        )

    def weight_push(k, j):
        return pltpu.make_async_remote_copy(
            src_ref=pieces[k].at[:, :, tile_of(j)],
            dst_ref=w_v.at[:, pl.ds(HALF + share_rows * k, share_rows), tile_of(j)],
            send_sem=w_send.at[k, j],
            recv_sem=w_recv.at[k, j],
            device_id=sibling,
            device_id_type=mesh_id,
        )

    def gradient_push(j):
        return pltpu.make_async_remote_copy(
            src_ref=grad_v.at[:, pl.ds(HALF, HALF), tile_of(j)],
            dst_ref=came_v.at[:, :, tile_of(j)],
            send_sem=g_send.at[j],
            recv_sem=g_recv.at[j],
            device_id=sibling,
            device_id_type=mesh_id,
        )

    def sum_copies(j):
        return [
            pltpu.make_async_copy(
                grad_v.at[:, pl.ds(2 * QUARTER * h, 2 * QUARTER), tile_of(j)],
                hbm.at[:, :, tile_of(j)],
                g_sem.at[j, h],
            )
            for h, hbm in enumerate((keep_hbm, pass_hbm))
        ]

    def add_sibling(j):
        cols = tile_of(j)
        gradient_push(j).wait_recv()
        for m in range(3):
            total = grad_v[m, :HALF, cols].astype(F32) + came_v[m, :, cols].astype(F32)
            grad_v[m, :HALF, cols] = total.astype(BF16)
        for copy in sum_copies(j):
            copy.start()

    def span_of(part):
        return pl.ds(part * span, span)

    loads = [
        pltpu.make_async_copy(src, dst, in_sem.at[n])
        for n, (src, dst) in enumerate(
            [(n_hbm, n_v), (cot_hbm, cot_v), (nt_hbm, nt_v), (cott_hbm, cott_v)]
            + ([(sums_in[0], mlp_v), (sums_in[1], dn_v)] if started else [])
        )
    ]
    loads[0].start()
    greet_kinds(("sibling",) + (("long", "short") if coming else ()) + kinds)

    def fetch(j, carry):
        for k in range(n_pieces):
            weight_copy(k, j).start()
            weight_push(k, j).start()
        return carry

    fetch(0, 0)
    for copy in loads[1:4]:
        copy.start()
    lax.fori_loop(1, steps, fetch, 0)
    for copy in loads[4:]:
        copy.start()
    if coming:
        at, width = coming
        line = line_hbm.at[:, :, pl.ds(at, width)]
        line_copy = pltpu.make_async_copy(line, quarter(next_hbm, 0), next_here)
        moves = [
            push(line, quarter(next_hbm, 1), next_sem, 0, short),
            push(line, quarter(next_hbm, 2), next_sem, 1, long),
            push(quarter(next_hbm, 1), quarter(next_hbm, 3), next_sem, 2, long),
        ]
        line_copy.start()
        moves[0].start()
        moves[1].start()

    for move in carried(kinds, srcs, dsts, carry_sem):
        move.start()

    for copy in loads[:4]:
        copy.wait()

    def columns(j, carry):
        for k in range(n_pieces):
            weight_copy(k, j).wait()
            weight_push(k, j).wait_recv()
        cols = tile_of(j)
        for part in range(parts):
            rows = span_of(part)
            normed = n_v[rows, :]
            gate = dot_nn(normed, w_v[0, :, cols])
            up = dot_nn(normed, w_v[1, :, cols])
            d_hidden = dot_nn(cot_v[rows, :], w_v[2, :, cols])
            s = 1.0 / (1.0 + jnp.exp(-gate))
            silu = gate * s
            act_v[2, rows, cols] = (silu * up).astype(BF16)
            act_v[0, rows, cols] = (d_hidden * up * s * (1.0 + gate * (1.0 - s))).astype(BF16)
            act_v[1, rows, cols] = (d_hidden * silu).astype(BF16)
        for m, left in ((2, cott_v), (0, nt_v), (1, nt_v)):
            grad_v[m, :, cols] = dot_nn(left[...], act_v[m, :, cols]).astype(BF16)
        gradient_push(j).start()

        @pl.when(j > 0)
        def _():
            add_sibling(j - 1)

        return carry

    lax.fori_loop(0, steps, columns, 0)
    stores = [pltpu.make_async_copy(w_v.at[:, pl.ds(HALF, HALF), :], far_hbm, out_sem.at[parts, 0])]
    stores[0].start()
    if coming:
        moves[0].wait_recv()
        moves[2].start()
    for copy in loads[4:]:
        copy.wait()
    for part in range(parts):
        rows = span_of(part)
        for k in range(2):
            if k == 0:
                total, ref, hbm = dot_nt(act_v[2, rows, :], w_v[2]), mlp_v, mlp_hbm
            else:
                total = dot_nt(act_v[0, rows, :], w_v[0]) + dot_nt(act_v[1, rows, :], w_v[1])
                ref, hbm = dn_v, dn_hbm
            ref[rows, :] = total + ref[rows, :] if started else total
            if part == 0 and k == 0:
                add_sibling(steps - 1)
            stores.append(
                pltpu.make_async_copy(ref.at[rows, :], hbm.at[rows, :], out_sem.at[part, k])
            )
            stores[-1].start()

    def settle(j, carry):
        for k in range(n_pieces):
            weight_push(k, j).wait_send()
        gradient_push(j).wait_send()
        for copy in sum_copies(j):
            copy.wait()
        return carry

    lax.fori_loop(0, steps, settle, 0)
    for copy in stores:
        copy.wait()
    if coming:
        line_copy.wait()
        moves[0].wait_send()
        moves[1].wait()
        moves[2].wait()
    for move in carried(kinds, srcs, dsts, carry_sem):
        move.wait()


def feed(number, wide, normed, normed_t, cot, cot_t, sums, pieces, line, coming, loads):
    rows = normed.shape[0]
    started = sums is not None
    kinds = tuple(kind for kind, _ in loads)
    extra = (list(sums) if started else []) + list(pieces) + ([line] if coming else [])
    extra += [array for _, array in loads]
    n_in = 4 + len(extra)
    steps = wide // TILE
    half = jax.ShapeDtypeStruct((3, HALF, wide), BF16)
    two_quarters = jax.ShapeDtypeStruct((3, 2 * QUARTER, wide), BF16)
    return pl.pallas_call(
        functools.partial(feed_kernel, wide, started, len(pieces), coming, kinds),
        in_specs=[ANYWHERE] * n_in,
        out_specs=[ANYWHERE] * ((6 if coming else 5) + len(loads)),
        out_shape=[
            jax.ShapeDtypeStruct((rows, D), F32),
            jax.ShapeDtypeStruct((rows, D), F32),
            two_quarters,
            two_quarters,
            half,
        ]
        + ([jax.ShapeDtypeStruct((3, HALF, coming[1]), BF16)] if coming else [])
        + [like(array) for _, array in loads],
        scratch_shapes=[
            pltpu.VMEM((rows, D), BF16),
            pltpu.VMEM((D, rows), BF16),
            pltpu.VMEM((rows, D), BF16),
            pltpu.VMEM((D, rows), BF16),
            pltpu.VMEM((3, D, wide), BF16),
            pltpu.VMEM((rows, D), F32),
            pltpu.VMEM((rows, D), F32),
            pltpu.VMEM((3, rows, wide), BF16),
            pltpu.VMEM((3, D, wide), BF16),
            pltpu.VMEM((3, HALF, wide), BF16),
            pltpu.SemaphoreType.DMA((6,)),
            pltpu.SemaphoreType.DMA((len(pieces), steps)),
            pltpu.SemaphoreType.DMA((len(pieces), steps)),
            pltpu.SemaphoreType.DMA((len(pieces), steps)),
            pltpu.SemaphoreType.DMA((3, 2)),
            pltpu.SemaphoreType.DMA((steps, 2)),
            pltpu.SemaphoreType.DMA((steps,)),
            pltpu.SemaphoreType.DMA((steps,)),
            pltpu.SemaphoreType.DMA((2, 3)),
            pltpu.SemaphoreType.DMA,
            pltpu.SemaphoreType.DMA((2, max(1, len(loads)))),
        ],
        compiler_params=params(56, collective_id=number, has_side_effects=True),
        cost_estimate=TINY,
        name="feed",
    )(normed, normed_t, cot, cot_t, *extra)


def project_back_kernel(dq_ref, own_kv_ref, recv_kv_ref, cos_ref, sin_ref, nl_ref, xp_ref, dres_ref, pi_ref, *refs):
    w_ref, gain_ref, ig_ref, own_ref, sib_ref, dgain_ref, dbias_ref, g_scr = refs
    t = pl.program_id(0)

    @pl.when(t == 0)
    def _():
        g_scr[...] = jnp.zeros(g_scr.shape, F32)
        dgain_ref[...] = jnp.zeros(dgain_ref.shape, F32)
        dbias_ref[...] = jnp.zeros(dbias_ref.shape, F32)

    cos, sin = cos_ref[...], sin_ref[...]
    low = lax.broadcasted_iota(jnp.int32, cos.shape, 1) % HEAD_SIZE < HEAD_SIZE // 2
    parts = []
    dkv = (own_kv_ref[...] + recv_kv_ref[...].astype(F32)).astype(BF16)
    for n in range(8):
        piece = (dq_ref[:, 128 * n : 128 * (n + 1)] if n < 7 else dkv[:, :KW]).astype(F32)
        parts.append((piece * cos - swap_halves(piece, low) * sin).astype(BF16))
    parts.append(dkv[:, KW:])
    d_lin = jnp.concatenate(parts, axis=1)
    dbias_ref[...] += jnp.sum(d_lin.astype(F32), axis=0, keepdims=True)
    d_normed = dot_nt(d_lin, w_ref[:, :QKV])
    xp = xp_ref[...].astype(F32)
    inv = lax.rsqrt(jnp.sum(xp * xp, axis=1, keepdims=True) * (1.0 / D) + norm_epsilon)
    hat = xp * inv
    scaled = d_normed * gain_ref[...]
    dgain_ref[...] += jnp.sum(d_normed * hat, axis=0, keepdims=True)
    mean = jnp.sum(scaled * hat, axis=1, keepdims=True) * (1.0 / D)
    grad = dres_ref[...] + inv * (scaled - hat * mean)
    high = grad.astype(BF16)
    rest = (grad - high.astype(F32)).astype(BF16)
    ig_ref[...] = dot_nt(high, pi_ref[...]) + dot_nt(rest, pi_ref[...])
    g_scr[...] += dot_tn(nl_ref[...], d_lin)

    @pl.when(t == pl.num_programs(0) - 1)
    def _():
        own_ref[...] = g_scr[:HALF].astype(BF16)
        sib_ref[...] = g_scr[HALF:].astype(BF16)


def project_back(dq, own_kv, recv_kv, cos, sin, nl, xp, d_res, pi, weights, gain, loads):
    rows = xp.shape[0]
    width = weights.shape[1]

    def tile(cols):
        return pl.BlockSpec((TOKEN_TILE, cols), lambda t: (t, 0))

    def whole(r, c):
        return pl.BlockSpec((r, c), lambda t: (0, 0))

    return pl.pallas_call(
        carrying(project_back_kernel, tuple(kind for kind, _ in loads), 11, 5),
        grid=(rows // TOKEN_TILE,),
        in_specs=[tile(QW), tile(256), tile(256), tile(128), tile(128), tile(D), tile(D), tile(D)]
        + [whole(D, D)]
        + [whole(D, width)]
        + [whole(1, D)]
        + [ANYWHERE] * len(loads),
        out_specs=[tile(D), whole(HALF, QKV), whole(HALF, QKV), whole(1, D), whole(1, QKV)]
        + [ANYWHERE] * len(loads),
        out_shape=[
            jax.ShapeDtypeStruct((rows, D), F32),
            jax.ShapeDtypeStruct((HALF, QKV), BF16),
            jax.ShapeDtypeStruct((HALF, QKV), BF16),
            jax.ShapeDtypeStruct((1, D), F32),
            jax.ShapeDtypeStruct((1, QKV), F32),
        ]
        + [like(array) for _, array in loads],
        scratch_shapes=[pltpu.VMEM((D, QKV), F32), pltpu.SemaphoreType.DMA((2, len(loads)))],
        compiler_params=params(56, collective_id=10, has_side_effects=True),
        cost_estimate=TINY,
        name="project_back",
    )(dq, own_kv, recv_kv, cos, sin, nl, xp, d_res, pi, weights, gain,
      *[array for _, array in loads])


def step_of(first_new, second_new):
    return (
        first_new
        / (1.0 - beta_first**STEP)
        / (jnp.sqrt(second_new / (1.0 - beta_second**STEP)) + adam_epsilon)
    )


def split_two(value):
    high = value.astype(BF16)
    return high, (value - high.astype(F32)).astype(BF16)


def product(dot, a, b):
    return dot(a[0], b[0]) + (dot(a[0], b[1]) + dot(a[1], b[0]))


def side_by_side(value):
    return jnp.concatenate([value[BW * t : BW * (t + 1)] for t in range(D // BW)], axis=1)


def one_above_other(value):
    return jnp.concatenate([value[:, BW * t : BW * (t + 1)] for t in range(D // BW)], axis=0)


def pick_kernel(spans, counts, block_ref, pi_ref, *refs):
    arrays, at = [], 0
    for count in counts:
        arrays.append(refs[at : at + count])
        at += count
    out_ref, w_scr, sem = refs[at:]
    slots = out_ref.shape[0]

    def each(slot, act):
        block = block_ref[slot]
        for n, pieces in enumerate(arrays):
            for page, (low, high) in enumerate(spans[n]):

                @pl.when((block >= low) & (block < high))
                def _(pieces=pieces, page=page, low=low):
                    column = pl.multiple_of((block - low) * BW, BW)
                    row = 0
                    for k, piece in enumerate(pieces):
                        count = piece.shape[1]
                        act(
                            pltpu.make_async_copy(
                                piece.at[page, :, pl.ds(column, BW)],
                                w_scr.at[slot, pl.ds(row, count), :],
                                sem.at[slot, k],
                            )
                        )
                        row += count

    for slot in range(slots):
        each(slot, lambda copy: copy.start())
    for slot in range(slots):
        each(slot, lambda copy: copy.wait())
        out_ref[slot] = dot_nn(pi_ref[...], w_scr[slot])


def picked(slot_block, pi, arrays, spans, after=()):
    capacity = slot_block.shape[0]
    vmem = pl.BlockSpec(memory_space=pltpu.VMEM)
    flat = [p for a in arrays for p in a]
    return pl.pallas_call(
        following(
            functools.partial(pick_kernel, spans, [len(a) for a in arrays]), 2 + len(flat), after
        ),
        in_specs=[pl.BlockSpec(memory_space=pltpu.SMEM), vmem]
        + [ANYWHERE] * (len(flat) + len(after)),
        out_specs=vmem,
        out_shape=jax.ShapeDtypeStruct((capacity, D, BW), F32),
        scratch_shapes=[pltpu.VMEM((capacity, D, BW), BF16), pltpu.SemaphoreType.DMA((capacity, 8))],
        compiler_params=params(60),
        cost_estimate=TINY,
        name="picked",
    )(slot_block, pi, *flat, *after)


def adam_kernel(block_ref, grad_ref, weight_ref, first_ref, second_ref, left_ref, right_ref, first_out, second_out, block_out):
    used = block_ref[pl.program_id(0)] >= 0

    @pl.when(used)
    def _():
        grad = grad_ref[0]
        left, right = split_two(left_ref[0]), split_two(right_ref[0])
        turned = split_two(side_by_side(dot_nn(grad, right[0]) + dot_nn(grad, right[1])))
        rotated = one_above_other(product(dot_tn, left, turned))
        first_new = beta_first * first_ref[0] + (1.0 - beta_first) * rotated
        second_new = beta_second * second_ref[0] + (1.0 - beta_second) * rotated * rotated
        first_out[0] = first_new
        second_out[0] = second_new
        step = split_two(step_of(first_new, second_new))
        back = split_two(side_by_side(product(dot_nt, step, right)))
        back = one_above_other(product(dot_nn, left, back))
        weights = weight_ref[0]
        block_out[0] = weights - rate_matrix * (back + weight_decay * weights)

    @pl.when(jnp.logical_not(used))
    def _():
        for ref in (first_out, second_out, block_out):
            ref[...] = jnp.zeros(ref.shape, F32)


def pack_kernel(spots, targets, counts, block_ref, *refs):
    n_in = sum(counts)
    ins, outs, (slots_ref, all_scr) = refs[:n_in], refs[n_in:-2], refs[-2:]
    at = 0
    for count, found in zip(counts, spots):
        for page, (width, target) in enumerate(found):
            total = ins[at][page, :, :width]
            for ref in ins[at + 1 : at + count]:
                total = total + ref[page, : total.shape[0], :width].astype(F32)
            all_scr[:, target : target + width] = total
        at += count
    for ref, start in zip(outs, targets):
        ref[...] = all_scr[:, start : start + ref.shape[1]]

    def one(slot, carry):
        block = jnp.maximum(block_ref[slot], 0)
        column = pl.multiple_of(block * BW, BW)
        slots_ref[slot] = all_scr[:, pl.ds(column, BW)].astype(BF16)
        return carry

    lax.fori_loop(0, slots_ref.shape[0], one, 0)


def packed(slot_block, groups, spots, targets):
    rows = groups[0][0].shape[1]
    vmem = pl.BlockSpec(memory_space=pltpu.VMEM)
    parts = [part for group in groups for part in group]
    total = (130 + 1) * BW
    return pl.pallas_call(
        functools.partial(
            pack_kernel, spots, [start for start, _ in targets], [len(g) for g in groups]
        ),
        in_specs=[pl.BlockSpec(memory_space=pltpu.SMEM)] + [vmem] * len(parts),
        out_specs=[vmem] * (len(targets) + 1),
        out_shape=[jax.ShapeDtypeStruct((rows, width), F32) for _, width in targets]
        + [jax.ShapeDtypeStruct((slot_block.shape[0], rows, BW), BF16)],
        scratch_shapes=[pltpu.VMEM((rows, total), F32)],
        compiler_params=params(60),
        cost_estimate=TINY,
        name="packed",
    )(slot_block, *parts)


def rotated_adam(slot_block, grads, weights, first_moment, second_moment, left, right):
    capacity = first_moment.shape[0]
    slab = pl.BlockSpec((1, D, BW), lambda s, b: (s, 0, 0))
    basis = pl.BlockSpec((1, BW, BW), lambda s, b: (s, 0, 0))
    return pl.pallas_call(
        adam_kernel,
        grid_spec=pltpu.PrefetchScalarGridSpec(
            num_scalar_prefetch=1,
            grid=(capacity,),
            in_specs=[slab, slab, slab, slab, basis, basis],
            out_specs=[slab] * 3,
        ),
        out_shape=[jax.ShapeDtypeStruct((capacity, D, BW), F32)] * 3,
        compiler_params=params(60),
        cost_estimate=TINY,
        name="rotated_adam",
    )(slot_block, grads, weights, first_moment, second_moment, left, right)


def vector_adam(vectors, grad_vectors, vector_first, vector_second):
    first_new = beta_first * vector_first + (1.0 - beta_first) * grad_vectors
    second_new = beta_second * vector_second + (1.0 - beta_second) * grad_vectors * grad_vectors
    return (second_new, vectors - rate_vector * step_of(first_new, second_new))


def hand_out(moving, arrived, after=()):
    at = 0
    for r in moving:
        came = arrived[at : at + len(r.next)]
        at += len(r.next)
        kind = r.next[0][0]
        if kind == "long":
            r.fold(came, after)
        elif kind == "short":
            r.share(came, after)
        else:
            r.end(came)
            r.next = []


def on_device(
    places,
    inputs,
    cotangent,
    starts,
    query_weight,
    key_weight,
    value_weight,
    out_weight,
    gate_weight,
    up_weight,
    down_weight,
    vectors,
    owner_slot,
    first_moment,
    second_moment,
    basis_left,
    basis_right,
    vector_first,
    vector_second,
):
    n_dev, shard_rows = places.n_dev, places.rows
    here = inputs.shape[2]
    seq_index = lax.axis_index("seq")
    vec_here = vectors.shape[0]

    out_t, down_t = out_weight.T, down_weight.T
    natural = places.natural_rows()
    pi = (jnp.arange(D, dtype=jnp.int32)[:, None] == natural[None, :]).astype(BF16)
    riding = (
        jnp.arange(n_dev, dtype=jnp.int32)[:, None] * shard_rows == natural[None, :]
    ).astype(BF16)
    vector_rows = jnp.pad(vectors.reshape(1, vec_here), ((0, shard_rows - 1), (0, 128 - vec_here)))
    cot = cotangent[:, 0].reshape(-1, D)
    cot_p = dot_nn(cot, pi).astype(BF16)
    cot_t = lax.dot_general(
        pi, cot, (((0,), (1,)), ((), ())), preferred_element_type=F32
    ).astype(BF16)
    attention_line = stacked_rows(
        line_parts(
            places,
            rounded(
                [query_weight, key_weight, value_weight, out_t, vector_rows],
                places.padded,
                [(0, 0, 0, QW), (0, 1, 0, KW), (0, 2, 0, KW), (0, 3, 0, QW), (0, 4, 0, 128)],
            ),
        ),
        after=(cot_p, cot_t),
    )
    feed_parts = [gate_weight, up_weight, down_t]

    def shard_of(chunks, after):
        spans = [(m, m, OFFSETS[n], CHUNKS[n]) for n in chunks for m in range(3)]
        return rounded(feed_parts, places.padded, spans, after=after)

    shard_a = shard_of((0,), ())
    backwards = [(-k % places.line, places.line) for k in range(1, places.line)]
    attention, *arrived = spread(attention_line, [(kind, shard_a) for kind in backwards])
    line_a = stacked_rows([shard_a] + arrived)
    shard_b = shard_of((1,), (attention,))
    short_a, long_a = send(line_a, places.short), send(line_a, places.long)
    attention_pages, attention = attention, attention[0]
    riders = attention[:, QKV + QW :]
    vectors_full = dot_nn(riding, riders)[:, :vec_here].reshape(-1)
    gains = jnp.pad(vectors_full[: 2 * D].reshape(2, D), ((0, 6), (0, 0))).astype(BF16)
    gains = dot_nn(gains, pi)
    gain_attn, gain_mlp = gains[0:1], gains[1:2]
    bias = vectors_full[2 * D :].reshape(1, QKV)

    spots = seq_index * here + jnp.arange(here, dtype=jnp.int32)
    own_starts = starts[:, 0]
    before = own_starts[:, None, :] <= spots[None, :, None]
    doc_begin = jnp.max(jnp.where(before, own_starts[:, None, :], 0), axis=2)
    relative = (spots[None, :] - doc_begin).astype(F32).reshape(-1)
    frequency = jnp.power(
        rope_theta, -jnp.arange(0, HEAD_SIZE, 2, dtype=F32) / HEAD_SIZE
    )
    angles = relative[:, None] * frequency[None, :]
    cos, sin = jnp.cos(angles), jnp.sin(angles)
    cos = jnp.concatenate([cos] * 4, axis=1)
    sin = jnp.concatenate([-sin, sin, -sin, sin], axis=1)
    begin = doc_begin + here - seq_index * here
    lo = begin[:, ::128] // 128
    begin = begin[:, None, :]

    x = inputs[:, 0].reshape(-1, D)
    xp, nl, q, k, v, kv = project(
        x, pi, attention, gain_attn, bias, cos, sin, after=(line_a, shard_b)
    )
    line_b = stacked_rows(line_parts(places, shard_b), after=(q,))
    far_a = send(short_a, places.long)
    short_b, long_b = send(line_b, places.short), send(line_b, places.long)
    shard_c = shard_of((2,), (line_b,))

    back = [(2 * n + 1, 2 * n) for n in range(n_dev // 2)]

    def streams(array):
        return array.reshape(MICRO, here, array.shape[-1])

    heads = (
        lo,
        streams(q),
        streams(kv[:, :KW]),
        streams(k),
        streams(kv[:, KW:]),
        streams(v),
        begin,
    )
    attended, lse = attend(*heads, after=(line_b, short_a, shard_c))
    attended_flat = attended.reshape(-1, QW)
    residual, normed, normed_t = middle(
        attended_flat, xp, attention, gain_mlp, after=(short_b,)
    )
    far_b = send(short_b, places.long)
    shard_last = shard_of((2,), (attended,))
    line_c = stacked_rows(line_parts(places, shard_c, shard_last), after=(normed,))
    shard_d = shard_of((3,), (line_b,))

    sums = None
    reductions, feed_pieces = [], []

    pieces = [[line_a, short_a, long_a, far_a], [line_b, short_b, long_b, far_b]]
    lines = [line_c]
    for n, wide in enumerate(CHUNKS):
        coming = (0, CHUNKS[n + 2]) if n + 2 < len(CHUNKS) else None
        moving = [r for r in reductions if r.next]
        loads = [load for r in moving for load in r.next]
        if n == 0:
            loads = [(kind, shard_d) for kind in backwards]
        mlp, d_normed, kept, passed, far, *arrived = feed(
            n, wide, normed, normed_t, cot_p, cot_t, sums, pieces[n],
            lines[n] if coming else None, coming, loads,
        )
        sums = (mlp, d_normed)
        feed_pieces.append(list(pieces[n]) + [far])
        if coming:
            pieces.append([arrived.pop(0)])
        if n == 0:
            lines.append(stacked_rows([shard_d] + arrived))
        hand_out(moving, arrived)
        reductions.append(Reduce(places, kept, passed))

    along = {"long": places.long, "short": places.short}

    def set_off(moving):
        return [
            send(array, along[kind] if kind in along else places.ahead[kind[0]])
            for r in moving
            for kind, array in r.next
        ]

    def operands(moving):
        return tuple(array for r in moving for _, array in r.next)

    moving, newest = [r for r in reductions[:-1] if r.next], reductions[-1:]
    arrived, arrived_late = set_off(moving), set_off(newest)
    output, d_res, d_att, own_out, other_out, d_gain_mlp = middle_back(
        residual, sums[0], sums[1], cot_p, attended_flat, pi, attention, gain_mlp,
        after=operands(moving + newest),
    )
    ended = tuple(arrived[: places.line - 1])
    hand_out(moving, arrived, (d_att,))
    moving = [r for r in reductions[:-1] if r.next]
    arrived = set_off(moving)
    dq, dkv, dkv_recv = attend_back(
        *heads, attended, streams(d_att), lse, after=operands(moving) + ended
    )
    dkv_recv = send(dkv_recv, back)
    hand_out(newest, arrived_late, (dq,))
    hand_out(moving, arrived, (dq,))
    moving = [r for r in reductions if r.next]
    input_grad, own_in, other_in, d_gain_attn, d_bias, *arrived = project_back(
        dq.reshape(-1, QW), dkv.reshape(-1, 2 * KW), dkv_recv.reshape(-1, 2 * KW),
        cos, sin, nl, xp, d_res, pi, attention, gain_attn,
        [load for r in moving for load in r.next],
    )
    hand_out(moving, arrived)

    d_gains = jnp.concatenate([d_gain_attn, d_gain_mlp, jnp.zeros((6, D), F32)], axis=0)
    high, rest = split_two(d_gains)
    d_gains = dot_nt(high, pi) + dot_nt(rest, pi)
    d_vectors = jnp.concatenate([d_gains[0], d_gains[1], d_bias[0]])
    d_vectors = jnp.pad(d_vectors.reshape(n_dev, vec_here), ((0, 0), (0, 128 - vec_here)))
    riders = dot_tn(riding, d_vectors.astype(BF16)).astype(BF16)
    moving = [r for r in reductions if r.next]
    grad_in, *arrived = reduce_tail(
        places,
        [own_out, own_in, riders[:HALF]],
        [other_out, other_in, riders[HALF:]],
        [load for r in moving for load in r.next],
    )
    hand_out(moving, arrived)

    capacity = first_moment.shape[0]
    slot_count = n_dev * capacity
    slot_block = (
        jnp.full((slot_count,), -1, jnp.int32)
        .at[owner_slot]
        .set(jnp.arange(owner_slot.shape[0], dtype=jnp.int32))
    )
    spots = [
        [(w, 2048 + m * FF + o) for m in range(3)] for o, w in zip(OFFSETS, CHUNKS)
    ]
    groups = [r.parts for r in reductions]
    for start, width, target in ((0, QW, QKV), (QW, QKV, 0), (QW + QKV, BW, 130 * BW)):
        groups.append([grad_in[:, :, start : start + width]])
        spots.append([(width, target)])
    targets = [
        (0, QW), (QW, KW), (QW + KW, KW), (QKV, QW),
        (2048, FF), (2048 + FF, FF), (2048 + 2 * FF, FF), (130 * BW, BW),
    ]
    (
        grad_query, grad_key, grad_value, grad_out_t, grad_gate, grad_up, grad_down_t, rider_sums, slots,
    ) = packed(slot_block, groups, spots, targets)
    grad_vectors = rider_sums[0, :vec_here]
    owned_grads = lax.all_to_all(
        slots,
        BOTH,
        split_axis=0,
        concat_axis=1,
        tiled=True,
    )
    local_block = lax.dynamic_slice_in_dim(
        slot_block, lax.axis_index(BOTH) * capacity, capacity, 0
    )
    spans = [[(0, 16)]]
    for o, w in zip(OFFSETS, CHUNKS):
        first, count = o // BW, w // BW
        spans.append(
            [(16 + 38 * m + first, 16 + 38 * m + first + count) for m in range(3)]
        )
    owned_weights = picked(
        local_block, pi, [[attention_pages]] + feed_pieces, spans, after=(slots,)
    )
    new_first, new_second, new_blocks = rotated_adam(
        local_block, owned_grads, owned_weights, first_moment, second_moment, basis_left, basis_right
    )
    vector_second_new, vector_new = vector_adam(vectors, grad_vectors, vector_first, vector_second)
    return (
        output.reshape(inputs.shape),
        input_grad.reshape(inputs.shape),
        grad_query,
        grad_key,
        grad_value,
        grad_out_t.T,
        grad_gate,
        grad_up,
        grad_down_t.T,
        grad_vectors,
        new_first,
        new_second,
        new_blocks,
        vector_second_new,
        vector_new,
    )


def solution(mesh):
    rows = P(("dp", "seq"), None)
    columns = P(None, ("dp", "seq"))
    tokens = P(None, "dp", "seq", None)
    slots = P(("dp", "seq"), None, None)
    line = P(("dp", "seq"))
    places = Places(mesh.shape["dp"], mesh.shape["seq"])
    return jax.shard_map(
        functools.partial(on_device, places),
        mesh=mesh,
        in_specs=(
            tokens, tokens, P(None, "dp", None), rows, rows, rows, columns, rows, rows, columns,
            line, P(), slots, slots, slots, slots, line, line,
        ),
        out_specs=(
            tokens, tokens, rows, rows, rows, columns, rows, rows, columns, line,
            slots, slots, slots, line, line,
        ),
        check_vma=False,
    )
```

```python
import functools
import math

import jax
import jax.numpy as jnp
import numpy as np
from jax import lax
from jax.experimental import pallas as pl
from jax.experimental.pallas import tpu as pltpu
from jax.sharding import PartitionSpec as P

D = 896
QUERY_HEADS = 14
KEY_VALUE_HEADS = 2
HEAD_SIZE = 64
BW = 128
MICRO = 2
STEP = 10
QW = 896
KW = 128
QKV = QW + 2 * KW
FF = 4864

norm_epsilon = 1e-06
rope_theta = 1000000.0
beta_first = 0.9
beta_second = 0.999
adam_epsilon = 1e-08
weight_decay = 0.01
rate_matrix = 0.1
rate_vector = 0.5
masked_value = -1e30

F32 = jnp.float32
BF16 = jnp.bfloat16
BOTH = ("dp", "seq")

TILE = 256
CHUNKS = (1280, 1280, 1280, 1024)
OFFSETS = (0, 1280, 2560, 3840)
QUARTER = 112
HALF = 448
TOKEN_TILE = 256

HEAD_SETS = (
    ((0, 1, 2, 3), 0, 0),
    ((0, 1, 2), 1, 0),
    ((3, 4, 5, 6), 1, 1),
    ((4, 5, 6), 0, 1),
)
SET_ROWS = (0, 512, 896, 1408)
ALL_ROWS = 1792


def params(mib, **more):
    return pltpu.CompilerParams(vmem_limit_bytes=mib * 1024 * 1024, **more)


def dot_nn(a, b):
    return lax.dot_general(a, b, (((1,), (0,)), ((), ())), preferred_element_type=F32)


def dot_nt(a, b):
    return lax.dot_general(a, b, (((1,), (1,)), ((), ())), preferred_element_type=F32)


def dot_tn(a, b):
    return lax.dot_general(a, b, (((0,), (0,)), ((), ())), preferred_element_type=F32)


def following(kernel, n_in, after):
    def wrapped(*refs):
        return kernel(*refs[:n_in], *refs[n_in + len(after) :])

    return wrapped


TINY = pl.CostEstimate(flops=1, bytes_accessed=1, transcendentals=0)
ANYWHERE = pl.BlockSpec(memory_space=pl.ANY)


class Places:
    def __init__(self, n_dp, n_seq):
        self.line = n_dp // 4
        self.rows = D // (n_dp * n_seq)
        self.n_dev = n_dp * n_seq
        self.padded = -(-self.rows // 16) * 16

        def pairs(move):
            found = []
            for z in range(self.line):
                for x in range(2):
                    for c in range(2):
                        for y in range(2):
                            tz, tx, tc, ty = move(z, x, c, y)
                            found.append(
                                (((z * 2 + x) * 2 + c) * 2 + y, ((tz * 2 + tx) * 2 + tc) * 2 + ty)
                            )
            return found

        self.sibling = pairs(lambda z, x, c, y: (z, x, 1 - c, y))
        self.long = pairs(lambda z, x, c, y: (z, 1 - x, c, y) if c == 0 else (z, x, c, 1 - y))
        self.short = pairs(lambda z, x, c, y: (z, 1 - x, c, y) if c == 1 else (z, x, c, 1 - y))
        self.ahead = [
            pairs(lambda z, x, c, y, k=k: ((z + k) % self.line, x, c, y)) for k in range(self.line)
        ]

    def natural_rows(self):
        dp = lax.axis_index("dp")
        y = lax.axis_index("seq")
        z, x, c = dp // 4, (dp // 2) % 2, dp % 2
        place = jnp.arange(D, dtype=jnp.int32)
        dc, da, db = place // HALF, (place // (2 * QUARTER)) % 2, (place // QUARTER) % 2
        dz, inner = (place % QUARTER) // self.rows, place % self.rows
        c_own = c ^ dc
        x_own = x ^ jnp.where(c_own == 0, da, db)
        y_own = y ^ jnp.where(c_own == 0, db, da)
        z_own = (z + dz) % self.line
        return self.rows * (((z_own * 2 + x_own) * 2 + c_own) * 2 + y_own) + inner


def send(array, pairs):
    return lax.ppermute(array, BOTH, pairs)


def line_parts(places, shard, last=None):
    count = places.line
    return [shard] + [
        send(shard if last is None or k < count - 1 else last, places.ahead[-k % count])
        for k in range(1, count)
    ]


def stack_kernel(count, *refs):
    ins, (out, scr) = refs[:count], refs[count:]
    rows = QUARTER // count
    for k, ref in enumerate(ins):
        scr[rows * k : rows * (k + 1), :] = ref[0, :rows].astype(F32)
    out[0] = scr[...].astype(BF16)


def stacked_rows(parts, after=()):
    pages, rows, width = parts[0].shape
    return pl.pallas_call(
        following(functools.partial(stack_kernel, len(parts)), len(parts), after),
        grid=(pages,),
        in_specs=[pl.BlockSpec((1, rows, width), lambda m: (m, 0, 0))] * len(parts)
        + [ANYWHERE] * len(after),
        out_specs=pl.BlockSpec((1, QUARTER, width), lambda m: (m, 0, 0)),
        out_shape=jax.ShapeDtypeStruct((pages, QUARTER, width), BF16),
        scratch_shapes=[pltpu.VMEM((QUARTER, width), F32)],
        compiler_params=params(60),
        cost_estimate=TINY,
        name="stacked_rows",
    )(*parts, *after)


def neighbours():
    dp, seq = lax.axis_index("dp"), lax.axis_index("seq")
    core = lax.rem(dp, 2)
    first = dp + 2 - 4 * lax.rem(dp // 2, 2)
    sibling = (dp + 1 - 2 * core, seq)
    long = (jnp.where(core == 0, first, dp), jnp.where(core == 0, seq, 1 - seq))
    short = (jnp.where(core == 0, dp, first), jnp.where(core == 0, 1 - seq, seq))
    return sibling, long, short


def greet(devices):
    barrier = pltpu.get_barrier_semaphore()
    for device in devices:
        pl.semaphore_signal(barrier, inc=1, device_id=device, device_id_type=pl.DeviceIdType.MESH)
    pl.semaphore_wait(barrier, len(devices))


def push(src, dst, sems, n, device):
    return pltpu.make_async_remote_copy(
        src_ref=src,
        dst_ref=dst,
        send_sem=sems.at[0, n],
        recv_sem=sems.at[1, n],
        device_id=device,
        device_id_type=pl.DeviceIdType.MESH,
    )


def quarter(ref, k):
    return ref.at[:, pl.ds(QUARTER * k, QUARTER), :]


def device_of(kind):
    if isinstance(kind, str):
        return dict(zip(("sibling", "long", "short"), neighbours()))[kind]
    ahead, line = kind
    dp = lax.axis_index("dp")
    return (lax.rem(dp // 4 + ahead, line) * 4 + lax.rem(dp, 4), lax.axis_index("seq"))


def greet_kinds(kinds):
    found = []
    for kind in kinds:
        if kind not in found:
            found.append(kind)
    greet([device_of(kind) for kind in found])


def carried(kinds, srcs, dsts, sems):
    return [
        push(src, dst, sems, n, device_of(kind))
        for n, (kind, src, dst) in enumerate(zip(kinds, srcs, dsts))
    ]


def carrying(kernel, kinds, n_in, n_out):
    count = len(kinds)

    def wrapped(*refs):
        ins, srcs = refs[:n_in], refs[n_in : n_in + count]
        at = n_in + count
        outs, dsts = refs[at : at + n_out], refs[at + n_out : at + n_out + count]
        scratch, sems = refs[at + n_out + count : -1], refs[-1]

        @pl.when(pl.program_id(0) == 0)
        def _():
            greet_kinds(kinds)
            for move in carried(kinds, srcs, dsts, sems):
                move.start()

        kernel(*ins, *outs, *scratch)

        @pl.when(pl.program_id(0) == pl.num_programs(0) - 1)
        def _():
            for move in carried(kinds, srcs, dsts, sems):
                move.wait()

    return wrapped


def like(array):
    return jax.ShapeDtypeStruct(array.shape, array.dtype)


def spread_kernel(kinds, own, *refs):
    count = len(kinds)
    srcs, out, dsts, (sems, here_sem, more_sems) = (
        refs[:count], refs[count], refs[count + 1 : 2 * count + 1], refs[2 * count + 1 :],
    )
    sibling, long, short = neighbours()
    greet_kinds(("sibling", "long", "short") + tuple(kinds))
    for move in carried(kinds, srcs, dsts, more_sems):
        move.start()
    here = pltpu.make_async_copy(own, quarter(out, 0), here_sem)
    moves = [
        push(own, quarter(out, 1), sems, 0, short),
        push(own, quarter(out, 2), sems, 1, long),
        push(own, quarter(out, 4), sems, 2, sibling),
    ]
    here.start()
    for move in moves:
        move.start()
    for k, first in ((1, 3), (2, None), (3, None)):
        moves[{1: 0, 2: 1, 3: 3}[k]].wait_recv()
        if first is not None:
            moves.append(push(quarter(out, 1), quarter(out, 3), sems, 3, long))
            moves[-1].start()
        moves.append(push(quarter(out, k), quarter(out, 4 + k), sems, 3 + k, sibling))
        moves[-1].start()
    here.wait()
    for n, move in enumerate(moves):
        move.wait_send()
        if n not in (0, 1, 3):
            move.wait_recv()
    for move in carried(kinds, srcs, dsts, more_sems):
        move.wait()


def spread(own, loads):
    kinds = tuple(kind for kind, _ in loads)
    return pl.pallas_call(
        functools.partial(spread_kernel, kinds),
        in_specs=[ANYWHERE] * (1 + len(loads)),
        out_specs=[ANYWHERE] * (1 + len(loads)),
        out_shape=[jax.ShapeDtypeStruct((1, D, own.shape[2]), BF16)] + [like(a) for _, a in loads],
        scratch_shapes=[
            pltpu.SemaphoreType.DMA((2, 7)),
            pltpu.SemaphoreType.DMA,
            pltpu.SemaphoreType.DMA((2, max(1, len(loads)))),
        ],
        compiler_params=params(60, collective_id=8, has_side_effects=True),
        cost_estimate=TINY,
        name="spread",
    )(own, *[array for _, array in loads])


def fold_kernel(count, *refs):
    total = refs[0][...].astype(F32)
    for ref in refs[1:count]:
        total = total + ref[...].astype(F32)
    refs[count][...] = total.astype(BF16)


def fold(terms, rows, after=()):
    pages, _, width = terms[0][0].shape

    def spec(block):
        return pl.BlockSpec((1, rows, width), lambda m: (m, block, 0))

    return pl.pallas_call(
        following(functools.partial(fold_kernel, len(terms)), len(terms), after),
        grid=(pages,),
        in_specs=[spec(block) for _, block in terms] + [ANYWHERE] * len(after),
        out_specs=spec(0),
        out_shape=jax.ShapeDtypeStruct((pages, rows, width), BF16),
        compiler_params=params(60),
        cost_estimate=TINY,
        name="fold",
    )(*[array for array, _ in terms], *after)


def share_kernel(count, rows, *refs):
    scr = refs[-1]
    outs = refs[count:-1]
    total = refs[0][0].astype(F32)
    for ref in refs[1:count]:
        total = total + ref[0].astype(F32)
    scr[...] = total
    for k, ref in enumerate(outs):
        ref[0, :rows] = scr[rows * k : rows * (k + 1), :].astype(ref.dtype)


def share(terms, rows, padded, line, after=()):
    pages, _, width = terms[0].shape
    part = [
        pl.BlockSpec((1, padded if k else rows, width), lambda m: (m, 0, 0)) for k in range(line)
    ]
    return pl.pallas_call(
        following(functools.partial(share_kernel, len(terms), rows), len(terms), after),
        grid=(pages,),
        in_specs=[pl.BlockSpec((1, QUARTER, width), lambda m: (m, 0, 0))] * len(terms)
        + [ANYWHERE] * len(after),
        out_specs=part,
        out_shape=[
            jax.ShapeDtypeStruct((pages, padded if k else rows, width), BF16 if k else F32)
            for k in range(line)
        ],
        scratch_shapes=[pltpu.VMEM((QUARTER, width), F32)],
        compiler_params=params(60),
        cost_estimate=TINY,
        name="share",
    )(*terms, *after)


class Reduce:
    def __init__(self, places, kept, passed):
        self.places, self.terms = places, [kept]
        self.next = [("long", passed)]

    def fold(self, arrived, after):
        self.terms.append(arrived[0])
        self.next = [("short", fold([(t, 1) for t in self.terms], QUARTER, after))]

    def share(self, arrived, after):
        self.terms.append(arrived[0])
        line = self.places.line
        mine, *parts = share(self.terms, self.places.rows, self.places.padded, line, after)
        self.parts = [mine]
        self.next = [((k + 1, line), part) for k, part in enumerate(parts)]

    def end(self, arrived):
        self.parts += list(arrived)


def tail_kernel(line, rows, widths, load_kinds, *refs):
    parts_n, count = len(widths), len(load_kinds)
    owns, others = refs[:parts_n], refs[parts_n : 2 * parts_n]
    at = 2 * parts_n
    srcs, out, dsts = refs[at : at + count], refs[at + count], refs[at + count + 1 : at + 2 * count + 1]
    came, half, came_half, quart, came_quart, keep, parts, came_parts, sems, load_sems = refs[
        at + 2 * count + 1 :
    ]
    starts = [sum(widths[:n]) for n in range(parts_n)]
    spans = [slice(start, start + width) for start, width in zip(starts, widths)]
    sibling, long, short = neighbours()
    greet_kinds(["sibling", "long", "short"] + [(k, line) for k in range(1, line)])
    moves = []

    def go(src, dst, device):
        moves.append(push(src, dst, sems, len(moves), device))
        moves[-1].start()
        return moves[-1]

    first = [go(others[n], came.at[:, span], sibling) for n, span in enumerate(spans)]
    for move in carried(load_kinds, srcs, dsts, load_sems):
        move.start()
    two = 2 * QUARTER
    second, third, last = [], [], []
    for n, span in enumerate(spans):
        first[n].wait_recv()
        half[:, span] = (owns[n][two:].astype(F32) + came[two:, span].astype(F32)).astype(BF16)
        second.append(go(half.at[:, span], came_half.at[:, span], long))
        keep[:, span] = owns[n][:two].astype(F32) + came[:two, span].astype(F32)
    for n, span in enumerate(spans):
        second[n].wait_recv()
        total = keep[QUARTER:, span] + came_half[QUARTER:, span].astype(F32)
        quart[:, span] = total.astype(BF16)
        third.append(go(quart.at[:, span], came_quart.at[:, span], short))
        keep[:QUARTER, span] = keep[:QUARTER, span] + came_half[:QUARTER, span].astype(F32)
    for n, span in enumerate(spans):
        third[n].wait_recv()
        keep[:QUARTER, span] = keep[:QUARTER, span] + came_quart[:, span].astype(F32)
        for k in range(1, line):
            parts[k - 1, :rows, span] = keep[rows * k : rows * (k + 1), span].astype(BF16)
            last.append(
                go(parts.at[k - 1, :, span], came_parts.at[k - 1, :, span], device_of((k, line)))
            )
    for n, span in enumerate(spans):
        total = keep[:rows, span]
        for k in range(1, line):
            last[n * (line - 1) + k - 1].wait_recv()
            total = total + came_parts[k - 1, :rows, span].astype(F32)
        out[0, :, span] = total
    for move in moves:
        move.wait_send()
    for move in carried(load_kinds, srcs, dsts, load_sems):
        move.wait()


def reduce_tail(places, owns, others, loads):
    widths, line, padded = [a.shape[1] for a in owns], places.line, places.padded
    width = sum(widths)
    vmem = pl.BlockSpec(memory_space=pltpu.VMEM)
    return pl.pallas_call(
        functools.partial(
            tail_kernel, line, places.rows, widths, tuple(kind for kind, _ in loads)
        ),
        in_specs=[vmem] * (2 * len(owns)) + [ANYWHERE] * len(loads),
        out_specs=[vmem] + [ANYWHERE] * len(loads),
        out_shape=[jax.ShapeDtypeStruct((1, places.rows, width), F32)] + [like(a) for _, a in loads],
        scratch_shapes=[
            pltpu.VMEM((HALF, width), BF16),
            pltpu.VMEM((2 * QUARTER, width), BF16),
            pltpu.VMEM((2 * QUARTER, width), BF16),
            pltpu.VMEM((QUARTER, width), BF16),
            pltpu.VMEM((QUARTER, width), BF16),
            pltpu.VMEM((2 * QUARTER, width), F32),
            pltpu.VMEM((line - 1, padded, width), BF16),
            pltpu.VMEM((line - 1, padded, width), BF16),
            pltpu.SemaphoreType.DMA((2, len(owns) * (2 + line))),
            pltpu.SemaphoreType.DMA((2, max(1, len(loads)))),
        ],
        compiler_params=params(56, collective_id=11, has_side_effects=True),
        cost_estimate=TINY,
        name="reduce_tail",
    )(*owns, *others, *[array for _, array in loads])


def round_kernel(spans, *refs):
    ins, out = refs[:-1], refs[-1]
    at = [0] * out.shape[0]
    for page, which, offset, width in spans:
        piece = ins[which][:, offset : offset + width]
        out[page, : piece.shape[0], at[page] : at[page] + width] = piece.astype(BF16)
        at[page] += width


def rounded(parts, padded, spans, after=()):
    pages = 1 + max(page for page, _, _, _ in spans)
    width = sum(width for page, _, _, width in spans if page == 0)
    return pl.pallas_call(
        following(functools.partial(round_kernel, spans), len(parts), after),
        in_specs=[pl.BlockSpec(memory_space=pltpu.VMEM)] * len(parts) + [ANYWHERE] * len(after),
        out_specs=pl.BlockSpec(memory_space=pltpu.VMEM),
        out_shape=jax.ShapeDtypeStruct((pages, padded, width), BF16),
        compiler_params=params(60),
        cost_estimate=TINY,
        name="rounded",
    )(*parts, *after)


def swap_halves(tile, low_half):
    return jnp.where(low_half, pltpu.roll(tile, 96, 1), pltpu.roll(tile, 32, 1))


def project_kernel(x_ref, pi_ref, *refs):
    (
        w_ref, gain_ref, bias_ref, cos_ref, sin_ref, xp_ref, nl_ref, q_ref, k_ref, v_ref, came_hbm,
        kv_scr, sems,
    ) = refs
    step, steps = pl.program_id(0), kv_scr.shape[0] // TOKEN_TILE
    seq = lax.axis_index("seq")
    other = (lax.axis_index("dp"), 1 - seq)

    def hand_on(n):
        rows = pl.ds(pl.multiple_of(n * TOKEN_TILE, TOKEN_TILE), TOKEN_TILE)
        return push(kv_scr.at[rows, :], came_hbm.at[rows, :], sems, n, other)

    @pl.when(step == 0)
    def _():
        greet([other])

    xp = dot_nn(x_ref[...], pi_ref[...])
    inv = lax.rsqrt(jnp.sum(xp * xp, axis=1, keepdims=True) * (1.0 / D) + norm_epsilon)
    nl = (xp * inv * gain_ref[...]).astype(BF16)
    xp_ref[...] = xp.astype(BF16)
    nl_ref[...] = nl
    lin = dot_nn(nl, w_ref[:, :QKV]) + bias_ref[...]
    cos, sin = cos_ref[...], sin_ref[...]
    low = lax.broadcasted_iota(jnp.int32, cos.shape, 1) % HEAD_SIZE < HEAD_SIZE // 2
    for t in range(8):
        piece = lin[:, 128 * t : 128 * (t + 1)]
        turned = (piece * cos + swap_halves(piece, low) * sin).astype(BF16)
        if t < 7:
            q_ref[:, 128 * t : 128 * (t + 1)] = (turned.astype(F32) * 0.125).astype(BF16)
        else:
            k_ref[...] = turned
            kv_scr[pl.ds(pl.multiple_of(step * TOKEN_TILE, TOKEN_TILE), TOKEN_TILE), :KW] = turned
    value = lin[:, QW + KW :].astype(BF16)
    v_ref[...] = value
    kv_scr[pl.ds(pl.multiple_of(step * TOKEN_TILE, TOKEN_TILE), TOKEN_TILE), KW:] = value

    @pl.when(seq == 0)
    def _():
        hand_on(step).start()

    @pl.when((step == steps - 1) & (seq == 0))
    def _():
        for n in range(steps):
            hand_on(n).wait_send()

    @pl.when((step == steps - 1) & (seq == 1))
    def _():
        for n in range(steps):
            hand_on(n).wait_recv()


def project(x, pi, weights, gain, bias, cos, sin, after=()):
    rows = x.shape[0]
    width = weights.shape[1]

    def tile(cols):
        return pl.BlockSpec((TOKEN_TILE, cols), lambda t: (t, 0))

    def whole(r, c):
        return pl.BlockSpec((r, c), lambda t: (0, 0))

    shapes = [(D, BF16), (D, BF16), (QW, BF16), (KW, BF16), (KW, BF16)]
    return pl.pallas_call(
        following(project_kernel, 7, after),
        grid=(rows // TOKEN_TILE,),
        in_specs=[tile(D), whole(D, D)]
        + [whole(D, width)]
        + [whole(1, D), whole(1, QKV), tile(128), tile(128)]
        + [ANYWHERE] * len(after),
        out_specs=[tile(c) for c, _ in shapes] + [ANYWHERE],
        out_shape=[jax.ShapeDtypeStruct((rows, c), t) for c, t in shapes + [(2 * KW, BF16)]],
        scratch_shapes=[
            pltpu.VMEM((rows, 2 * KW), BF16),
            pltpu.SemaphoreType.DMA((2, rows // TOKEN_TILE)),
        ],
        compiler_params=params(56, collective_id=12, has_side_effects=True),
        cost_estimate=TINY,
        name="project",
    )(x, pi, weights, gain, bias, cos, sin, *after)


def padded_heads(recv, own, out, turned):
    for part, ref in enumerate((recv, own)):
        natural = ref[0].astype(F32)
        span = pl.ds(512 * part, 512)
        if out is not None:
            lane = lax.broadcasted_iota(jnp.int32, (512, 128), 1)
            crossed = pltpu.roll(natural, 64, 1)
            for s, (_, half, head) in enumerate(HEAD_SETS):
                source = natural if half == head else crossed
                keep = (lane >= 64) if half else (lane < 64)
                out[s, span, :] = jnp.where(keep, source, 0.0).astype(BF16)
        if turned is not None:
            flat = natural.T
            other = jnp.concatenate([flat[64:], flat[:64]], axis=0)
            row = lax.broadcasted_iota(jnp.int32, (128, 512), 0)
            for s, (_, half, head) in enumerate(HEAD_SETS):
                source = flat if half == head else other
                keep = (row >= 64) if half else (row < 64)
                turned[s, :, span] = jnp.where(keep, source, 0.0).astype(BF16)


def block_bias(kb, i, begin):
    shape = (128, 128)
    key = kb * 128 + lax.broadcasted_iota(jnp.int32, shape, 0)
    query = 512 + i * 128 + lax.broadcasted_iota(jnp.int32, shape, 1)
    return jnp.where((key >= begin) & (key <= query), 0.0, masked_value)


def stacked(tile_of, pairs):
    return jnp.concatenate([tile_of(p) for p in pairs], axis=0)


def turned_block(ref, out):
    for p in range(7):
        cols = slice(128 * p, 128 * (p + 1))
        out[:, cols] = ref[0, :, cols].astype(F32).T.astype(BF16)


def pair_columns(s):
    pairs = HEAD_SETS[s][0]
    return slice(128 * pairs[0], 128 * (pairs[-1] + 1))


def columns_of(s, n=None):
    pairs = HEAD_SETS[s][0]
    if n is None:
        return slice(SET_ROWS[s], SET_ROWS[s] + 128 * len(pairs))
    return slice(SET_ROWS[s] + 128 * n, SET_ROWS[s] + 128 * (n + 1))


def eights(value):
    return value.reshape(value.shape[0] // 8, 8, value.shape[1])


def attend_kernel(
    lo_ref, q_ref, kr_ref, ko_ref, vr_ref, vo_ref, ds_ref, o_ref, lse_ref, kp, vt, qt, s_scr, m_scr, l_scr, acc
):
    b, i = pl.program_id(0), pl.program_id(1)

    @pl.when(i == 0)
    def _():
        padded_heads(kr_ref, ko_ref, kp, None)
        padded_heads(vr_ref, vo_ref, None, vt)

    lo, hi = lo_ref[b, i], i + 5
    begin = ds_ref[0]
    turned_block(q_ref, qt)
    m_scr[...] = jnp.full(m_scr.shape, masked_value, F32)
    l_scr[...] = jnp.zeros(l_scr.shape, F32)
    acc[...] = jnp.zeros(acc.shape, F32)

    def scores(kb, carry):
        bias = block_bias(kb, i, begin)
        keys = pl.ds(pl.multiple_of(kb * 128, 128), 128)
        raws = [dot_nn(kp[s, keys, :], qt[:, pair_columns(s)]) for s in range(4)]
        for s, (pairs, _, _) in enumerate(HEAD_SETS):
            cols = columns_of(s)
            value = raws[s] + jnp.concatenate([bias] * len(pairs), axis=1)
            s_scr[kb, :, cols] = value
            m_scr[:, cols] = jnp.maximum(m_scr[:, cols], jnp.max(eights(value), axis=0))
        return carry

    lax.fori_loop(lo, hi, scores, 0)
    top = jnp.max(m_scr[...], axis=0, keepdims=True)

    def weigh(kb, carry):
        keys = pl.ds(pl.multiple_of(kb * 128, 128), 128)
        probs = [jnp.exp(s_scr[kb, :, columns_of(s)] - top[:, columns_of(s)]) for s in range(4)]
        parts = [dot_nn(vt[s, :, keys], probs[s].astype(BF16)) for s in range(4)]
        for s in range(4):
            cols = columns_of(s)
            l_scr[:, cols] += jnp.sum(eights(probs[s]), axis=0)
            acc[:, cols] += parts[s]
        return carry

    lax.fori_loop(lo, hi, weigh, 0)
    total = jnp.sum(l_scr[...], axis=0, keepdims=True)
    lse = top + jnp.log(total)
    share = 1.0 / total
    outs = [None] * 7
    for s, (pairs, half, _) in enumerate(HEAD_SETS):
        for n, p in enumerate(pairs):
            cols = columns_of(s, n)
            part = acc[:, cols] * share[:, cols]
            outs[p] = part if outs[p] is None else outs[p] + part
            head = 2 * p + half
            lse_ref[0, head : head + 1, :] = lse[:, cols]
    for p in range(7):
        o_ref[0, :, 128 * p : 128 * (p + 1)] = outs[p].T.astype(BF16)


def attend_specs():
    def block(cols):
        return pl.BlockSpec((1, 128, cols), lambda b, i, lo: (b, i, 0))

    def lanes(rows):
        return pl.BlockSpec((1, rows, 128), lambda b, i, lo: (b, 0, i))

    def stream(cols):
        return pl.BlockSpec((1, 512, cols), lambda b, i, lo: (b, 0, 0))

    return block, lanes, stream


def attend(lo, q, k_recv, k_own, v_recv, v_own, begin, after=()):
    block, lanes, stream = attend_specs()
    return pl.pallas_call(
        following(attend_kernel, 7, after),
        grid_spec=pltpu.PrefetchScalarGridSpec(
            num_scalar_prefetch=1,
            grid=(MICRO, 4),
            in_specs=[block(QW)] + [stream(KW)] * 4 + [lanes(1)] + [ANYWHERE] * len(after),
            out_specs=[block(QW), lanes(16)],
            scratch_shapes=[
                pltpu.VMEM((4, 1024, 128), BF16),
                pltpu.VMEM((4, 128, 1024), BF16),
                pltpu.VMEM((128, QW), BF16),
                pltpu.VMEM((8, 128, ALL_ROWS), F32),
                pltpu.VMEM((8, ALL_ROWS), F32),
                pltpu.VMEM((8, ALL_ROWS), F32),
                pltpu.VMEM((128, ALL_ROWS), F32),
            ],
        ),
        out_shape=[
            jax.ShapeDtypeStruct((MICRO, 512, QW), BF16),
            jax.ShapeDtypeStruct((MICRO, 16, 512), F32),
        ],
        compiler_params=params(56),
        cost_estimate=TINY,
        name="attend",
    )(lo, q, k_recv, k_own, v_recv, v_own, begin, *after)


def attend_back_kernel(
    lo_ref, q_ref, kr_ref, ko_ref, vr_ref, vo_ref, ds_ref, o_ref, do_ref, lse_ref,
    dq_ref, own_ref, recv_ref, kp, vp, kt, qt, dot_t, dk, dv, dq_acc,
):
    b, i = pl.program_id(0), pl.program_id(1)

    @pl.when(i == 0)
    def _():
        padded_heads(kr_ref, ko_ref, kp, kt)
        padded_heads(vr_ref, vo_ref, vp, None)
        dk[...] = jnp.zeros(dk.shape, F32)
        dv[...] = jnp.zeros(dv.shape, F32)

    lo, hi = lo_ref[b, i], i + 5
    begin = ds_ref[0]
    dq_acc[...] = jnp.zeros(dq_acc.shape, F32)
    turned_block(q_ref, qt)
    turned_block(do_ref, dot_t)
    pick = lax.broadcasted_iota(jnp.int32, (8, 128), 1) // 64 == lax.broadcasted_iota(
        jnp.int32, (8, 128), 0
    )
    pick = pick.astype(F32).astype(BF16)
    halves = []
    for p in range(7):
        cols = slice(128 * p, 128 * (p + 1))
        high, rest = split_two(o_ref[0, :, cols].astype(F32) * do_ref[0, :, cols].astype(F32))
        halves.append(dot_nt(pick, high) + dot_nt(pick, rest))
    lse, dots = [], []
    for pairs, half, _ in HEAD_SETS:
        heads = [2 * p + half for p in pairs]
        lse.append(jnp.concatenate([lse_ref[0, h : h + 1, :] for h in heads], axis=1))
        dots.append(jnp.concatenate([halves[p][half : half + 1] for p in pairs], axis=1))

    def one_block(kb, carry):
        bias = block_bias(kb, i, begin)
        keys = pl.ds(pl.multiple_of(kb * 128, 128), 128)
        work = []
        for s, (pairs, _, _) in enumerate(HEAD_SETS):
            cols = columns_of(s)
            x = stacked(lambda p: q_ref[0, :, 128 * p : 128 * (p + 1)], pairs)
            y = stacked(lambda p: do_ref[0, :, 128 * p : 128 * (p + 1)], pairs)
            raw = dot_nn(kp[s, keys, :], qt[:, pair_columns(s)]) + jnp.concatenate([bias] * len(pairs), axis=1)
            d_prob = dot_nn(vp[s, keys, :], dot_t[:, pair_columns(s)])
            work.append((s, cols, x, y, raw, d_prob))
        parts = []
        for s, cols, x, y, raw, d_prob in work:
            p = jnp.exp(raw - lse[s])
            d_score = (p * (d_prob - dots[s])).astype(BF16)
            parts.append((s, cols, x, y, p.astype(BF16), d_score))
        sums = [
            (s, cols, dot_nn(kt[s, :, keys], d_score), dot_nn(d_score, x), dot_nn(p, y))
            for s, cols, x, y, p, d_score in parts
        ]
        for s, cols, d_query, d_key, d_value in sums:
            dq_acc[:, cols] += d_query
            dk[s, keys, :] += d_key
            dv[s, keys, :] += d_value
        return carry

    lax.fori_loop(lo, hi, one_block, 0)
    sums = [None] * 7
    for s, (pairs, _, _) in enumerate(HEAD_SETS):
        for n, p in enumerate(pairs):
            part = dq_acc[:, columns_of(s, n)]
            sums[p] = part if sums[p] is None else sums[p] + part
    for p in range(7):
        dq_ref[0, :, 128 * p : 128 * (p + 1)] = (sums[p] * 0.125).T.astype(BF16)

    @pl.when(i == 3)
    def _():
        wide = lax.broadcasted_iota(jnp.int32, (512, 128), 1) < 64
        for part, ref in enumerate((recv_ref, own_ref)):
            rows = pl.ds(512 * part, 512)
            for n, grads in enumerate((dk, dv)):
                low = grads[0, rows, :] + pltpu.roll(grads[1, rows, :], 64, 1)
                high = grads[2, rows, :] + pltpu.roll(grads[3, rows, :], 64, 1)
                value = jnp.where(wide, low, high)
                ref[0, :, 128 * n : 128 * (n + 1)] = value.astype(ref.dtype)


def attend_back(lo, q, k_recv, k_own, v_recv, v_own, begin, out, d_out, lse, after=()):
    block, lanes, stream = attend_specs()
    return pl.pallas_call(
        following(attend_back_kernel, 10, after),
        grid_spec=pltpu.PrefetchScalarGridSpec(
            num_scalar_prefetch=1,
            grid=(MICRO, 4),
            in_specs=[block(QW)]
            + [stream(KW)] * 4
            + [lanes(1), block(QW), block(QW), lanes(16)]
            + [ANYWHERE] * len(after),
            out_specs=[block(QW), stream(256), stream(256)],
            scratch_shapes=[
                pltpu.VMEM((4, 1024, 128), BF16),
                pltpu.VMEM((4, 1024, 128), BF16),
                pltpu.VMEM((4, 128, 1024), BF16),
                pltpu.VMEM((128, QW), BF16),
                pltpu.VMEM((128, QW), BF16),
                pltpu.VMEM((4, 1024, 128), F32),
                pltpu.VMEM((4, 1024, 128), F32),
                pltpu.VMEM((128, ALL_ROWS), F32),
            ],
        ),
        out_shape=[
            jax.ShapeDtypeStruct((MICRO, 512, QW), BF16),
            jax.ShapeDtypeStruct((MICRO, 512, 256), F32),
            jax.ShapeDtypeStruct((MICRO, 512, 256), BF16),
        ],
        compiler_params=params(56),
        cost_estimate=TINY,
        name="attend_back",
    )(lo, q, k_recv, k_own, v_recv, v_own, begin, out, d_out, lse, *after)


def middle_kernel(att_ref, xp_ref, *refs):
    w_ref, gain_ref, res_ref, n_ref, nt_ref = refs
    residual = xp_ref[...].astype(F32) + dot_nt(att_ref[...], w_ref[:, QKV : QKV + QW])
    inv = lax.rsqrt(jnp.sum(residual * residual, axis=1, keepdims=True) * (1.0 / D) + norm_epsilon)
    normed = residual * inv * gain_ref[...]
    res_ref[...] = residual
    n_ref[...] = normed.astype(BF16)
    nt_ref[...] = normed.T.astype(BF16)


def middle(attended, xp, weights, gain, after=()):
    rows = xp.shape[0]
    width = weights.shape[1]

    def tile(cols):
        return pl.BlockSpec((TOKEN_TILE, cols), lambda t: (t, 0))

    def whole(r, c):
        return pl.BlockSpec((r, c), lambda t: (0, 0))

    return pl.pallas_call(
        following(middle_kernel, 4, after),
        grid=(rows // TOKEN_TILE,),
        in_specs=[tile(QW), tile(D)]
        + [whole(D, width)]
        + [whole(1, D)]
        + [ANYWHERE] * len(after),
        out_specs=[tile(D), tile(D), pl.BlockSpec((D, TOKEN_TILE), lambda t: (0, t))],
        out_shape=[
            jax.ShapeDtypeStruct((rows, D), F32),
            jax.ShapeDtypeStruct((rows, D), BF16),
            jax.ShapeDtypeStruct((D, rows), BF16),
        ],
        compiler_params=params(56),
        cost_estimate=TINY,
        name="middle",
    )(attended, xp, weights, gain, *after)


def middle_back_kernel(res_ref, mlp_ref, dn_ref, cot_ref, att_ref, pi_ref, *refs):
    w_ref, gain_ref, out_ref, dres_ref, datt_ref, own_ref, sib_ref, dgain_ref, g_scr = refs
    t = pl.program_id(0)

    @pl.when(t == 0)
    def _():
        g_scr[...] = jnp.zeros(g_scr.shape, F32)
        dgain_ref[...] = jnp.zeros(dgain_ref.shape, F32)

    residual = res_ref[...]
    inv = lax.rsqrt(jnp.sum(residual * residual, axis=1, keepdims=True) * (1.0 / D) + norm_epsilon)
    out_low = (residual + mlp_ref[...]).astype(BF16)
    out_ref[...] = dot_nt(out_low, pi_ref[...]).astype(BF16)
    d_normed = dn_ref[...]
    hat = residual * inv
    scaled = d_normed * gain_ref[...]
    dgain_ref[...] += jnp.sum(d_normed * hat, axis=0, keepdims=True)
    mean = jnp.sum(scaled * hat, axis=1, keepdims=True) * (1.0 / D)
    d_res = cot_ref[...].astype(F32) + inv * (scaled - hat * mean)
    dres_ref[...] = d_res
    low = d_res.astype(BF16)
    datt_ref[...] = dot_nn(low, w_ref[:, QKV : QKV + QW]).astype(BF16)
    g_scr[...] += dot_tn(low, att_ref[...])

    @pl.when(t == pl.num_programs(0) - 1)
    def _():
        own_ref[...] = g_scr[:HALF].astype(BF16)
        sib_ref[...] = g_scr[HALF:].astype(BF16)


def middle_back(residual, mlp, d_normed, cot, attended, pi, weights, gain, after=()):
    rows = residual.shape[0]
    width = weights.shape[1]

    def tile(cols):
        return pl.BlockSpec((TOKEN_TILE, cols), lambda t: (t, 0))

    def whole(r, c):
        return pl.BlockSpec((r, c), lambda t: (0, 0))

    return pl.pallas_call(
        following(middle_back_kernel, 8, after),
        grid=(rows // TOKEN_TILE,),
        in_specs=[tile(D)] * 4
        + [tile(QW), whole(D, D)]
        + [whole(D, width)]
        + [whole(1, D)]
        + [ANYWHERE] * len(after),
        out_specs=[tile(D), tile(D), tile(QW), whole(HALF, QW), whole(HALF, QW), whole(1, D)],
        out_shape=[
            jax.ShapeDtypeStruct((rows, D), BF16),
            jax.ShapeDtypeStruct((rows, D), F32),
            jax.ShapeDtypeStruct((rows, QW), BF16),
            jax.ShapeDtypeStruct((HALF, QW), BF16),
            jax.ShapeDtypeStruct((HALF, QW), BF16),
            jax.ShapeDtypeStruct((1, D), F32),
        ],
        scratch_shapes=[pltpu.VMEM((D, QW), F32)],
        compiler_params=params(56),
        cost_estimate=TINY,
        name="middle_back",
    )(residual, mlp, d_normed, cot, attended, pi, weights, gain, *after)


def feed_kernel(wide, started, n_pieces, coming, kinds, *refs):
    n_in = 4 + (2 if started else 0)
    n_hbm, nt_hbm, cot_hbm, cott_hbm = refs[:4]
    sums_in = refs[4:n_in]
    pieces = refs[n_in : n_in + n_pieces]
    n_in += n_pieces
    if coming:
        line_hbm = refs[n_in]
        n_in += 1
    srcs = refs[n_in : n_in + len(kinds)]
    n_in += len(kinds)
    mlp_hbm, dn_hbm, keep_hbm, pass_hbm, far_hbm = refs[n_in : n_in + 5]
    n_in += 5
    if coming:
        next_hbm = refs[n_in]
        n_in += 1
    dsts = refs[n_in : n_in + len(kinds)]
    n_in += len(kinds)
    (
        n_v, nt_v, cot_v, cott_v, w_v, mlp_v, dn_v, act_v, grad_v, came_v,
        in_sem, w_sem, w_send, w_recv, out_sem, g_sem, g_send, g_recv, next_sem, next_here,
        carry_sem,
    ) = refs[n_in:]
    rows_all = n_v.shape[0]
    steps = wide // TILE
    span = 512
    parts = rows_all // span
    sibling, long, short = neighbours()
    mesh_id = pl.DeviceIdType.MESH
    share_rows = HALF // n_pieces

    def tile_of(j):
        return pl.ds(pl.multiple_of(j * TILE, TILE), TILE)

    def weight_copy(k, j):
        return pltpu.make_async_copy(
            pieces[k].at[:, :, tile_of(j)],
            w_v.at[:, pl.ds(share_rows * k, share_rows), tile_of(j)],
            w_sem.at[k, j],
        )

    def weight_push(k, j):
        return pltpu.make_async_remote_copy(
            src_ref=pieces[k].at[:, :, tile_of(j)],
            dst_ref=w_v.at[:, pl.ds(HALF + share_rows * k, share_rows), tile_of(j)],
            send_sem=w_send.at[k, j],
            recv_sem=w_recv.at[k, j],
            device_id=sibling,
            device_id_type=mesh_id,
        )

    def gradient_push(j):
        return pltpu.make_async_remote_copy(
            src_ref=grad_v.at[:, pl.ds(HALF, HALF), tile_of(j)],
            dst_ref=came_v.at[:, :, tile_of(j)],
            send_sem=g_send.at[j],
            recv_sem=g_recv.at[j],
            device_id=sibling,
            device_id_type=mesh_id,
        )

    def sum_copies(j):
        return [
            pltpu.make_async_copy(
                grad_v.at[:, pl.ds(2 * QUARTER * h, 2 * QUARTER), tile_of(j)],
                hbm.at[:, :, tile_of(j)],
                g_sem.at[j, h],
            )
            for h, hbm in enumerate((keep_hbm, pass_hbm))
        ]

    def add_sibling(j):
        cols = tile_of(j)
        gradient_push(j).wait_recv()
        for m in range(3):
            total = grad_v[m, :HALF, cols].astype(F32) + came_v[m, :, cols].astype(F32)
            grad_v[m, :HALF, cols] = total.astype(BF16)
        for copy in sum_copies(j):
            copy.start()

    def span_of(part):
        return pl.ds(part * span, span)

    loads = [
        pltpu.make_async_copy(src, dst, in_sem.at[n])
        for n, (src, dst) in enumerate(
            [(n_hbm, n_v), (cot_hbm, cot_v), (nt_hbm, nt_v), (cott_hbm, cott_v)]
            + ([(sums_in[0], mlp_v), (sums_in[1], dn_v)] if started else [])
        )
    ]
    loads[0].start()
    greet_kinds(("sibling",) + (("long", "short") if coming else ()) + kinds)

    def fetch(j, carry):
        for k in range(n_pieces):
            weight_copy(k, j).start()
            weight_push(k, j).start()
        return carry

    fetch(0, 0)
    for copy in loads[1:4]:
        copy.start()
    lax.fori_loop(1, steps, fetch, 0)
    for copy in loads[4:]:
        copy.start()
    if coming:
        at, width = coming
        line = line_hbm.at[:, :, pl.ds(at, width)]
        line_copy = pltpu.make_async_copy(line, quarter(next_hbm, 0), next_here)
        moves = [
            push(line, quarter(next_hbm, 1), next_sem, 0, short),
            push(line, quarter(next_hbm, 2), next_sem, 1, long),
            push(quarter(next_hbm, 1), quarter(next_hbm, 3), next_sem, 2, long),
        ]
        line_copy.start()
        moves[0].start()
        moves[1].start()

    for move in carried(kinds, srcs, dsts, carry_sem):
        move.start()

    for copy in loads[:4]:
        copy.wait()

    def columns(j, carry):
        for k in range(n_pieces):
            weight_copy(k, j).wait()
            weight_push(k, j).wait_recv()
        cols = tile_of(j)
        for part in range(parts):
            rows = span_of(part)
            normed = n_v[rows, :]
            gate = dot_nn(normed, w_v[0, :, cols])
            up = dot_nn(normed, w_v[1, :, cols])
            d_hidden = dot_nn(cot_v[rows, :], w_v[2, :, cols])
            s = 1.0 / (1.0 + jnp.exp(-gate))
            silu = gate * s
            act_v[2, rows, cols] = (silu * up).astype(BF16)
            act_v[0, rows, cols] = (d_hidden * up * s * (1.0 + gate * (1.0 - s))).astype(BF16)
            act_v[1, rows, cols] = (d_hidden * silu).astype(BF16)
        for m, left in ((2, cott_v), (0, nt_v), (1, nt_v)):
            grad_v[m, :, cols] = dot_nn(left[...], act_v[m, :, cols]).astype(BF16)
        gradient_push(j).start()

        @pl.when(j > 0)
        def _():
            add_sibling(j - 1)

        return carry

    lax.fori_loop(0, steps, columns, 0)
    stores = [pltpu.make_async_copy(w_v.at[:, pl.ds(HALF, HALF), :], far_hbm, out_sem.at[parts, 0])]
    stores[0].start()
    if coming:
        moves[0].wait_recv()
        moves[2].start()
    for copy in loads[4:]:
        copy.wait()
    for part in range(parts):
        rows = span_of(part)
        for k in range(2):
            if k == 0:
                total, ref, hbm = dot_nt(act_v[2, rows, :], w_v[2]), mlp_v, mlp_hbm
            else:
                total = dot_nt(act_v[0, rows, :], w_v[0]) + dot_nt(act_v[1, rows, :], w_v[1])
                ref, hbm = dn_v, dn_hbm
            ref[rows, :] = total + ref[rows, :] if started else total
            if part == 0 and k == 0:
                add_sibling(steps - 1)
            stores.append(
                pltpu.make_async_copy(ref.at[rows, :], hbm.at[rows, :], out_sem.at[part, k])
            )
            stores[-1].start()

    def settle(j, carry):
        for k in range(n_pieces):
            weight_push(k, j).wait_send()
        gradient_push(j).wait_send()
        for copy in sum_copies(j):
            copy.wait()
        return carry

    lax.fori_loop(0, steps, settle, 0)
    for copy in stores:
        copy.wait()
    if coming:
        line_copy.wait()
        moves[0].wait_send()
        moves[1].wait()
        moves[2].wait()
    for move in carried(kinds, srcs, dsts, carry_sem):
        move.wait()


def feed(number, wide, normed, normed_t, cot, cot_t, sums, pieces, line, coming, loads):
    rows = normed.shape[0]
    started = sums is not None
    kinds = tuple(kind for kind, _ in loads)
    extra = (list(sums) if started else []) + list(pieces) + ([line] if coming else [])
    extra += [array for _, array in loads]
    n_in = 4 + len(extra)
    steps = wide // TILE
    half = jax.ShapeDtypeStruct((3, HALF, wide), BF16)
    two_quarters = jax.ShapeDtypeStruct((3, 2 * QUARTER, wide), BF16)
    return pl.pallas_call(
        functools.partial(feed_kernel, wide, started, len(pieces), coming, kinds),
        in_specs=[ANYWHERE] * n_in,
        out_specs=[ANYWHERE] * ((6 if coming else 5) + len(loads)),
        out_shape=[
            jax.ShapeDtypeStruct((rows, D), F32),
            jax.ShapeDtypeStruct((rows, D), F32),
            two_quarters,
            two_quarters,
            half,
        ]
        + ([jax.ShapeDtypeStruct((3, HALF, coming[1]), BF16)] if coming else [])
        + [like(array) for _, array in loads],
        scratch_shapes=[
            pltpu.VMEM((rows, D), BF16),
            pltpu.VMEM((D, rows), BF16),
            pltpu.VMEM((rows, D), BF16),
            pltpu.VMEM((D, rows), BF16),
            pltpu.VMEM((3, D, wide), BF16),
            pltpu.VMEM((rows, D), F32),
            pltpu.VMEM((rows, D), F32),
            pltpu.VMEM((3, rows, wide), BF16),
            pltpu.VMEM((3, D, wide), BF16),
            pltpu.VMEM((3, HALF, wide), BF16),
            pltpu.SemaphoreType.DMA((6,)),
            pltpu.SemaphoreType.DMA((len(pieces), steps)),
            pltpu.SemaphoreType.DMA((len(pieces), steps)),
            pltpu.SemaphoreType.DMA((len(pieces), steps)),
            pltpu.SemaphoreType.DMA((3, 2)),
            pltpu.SemaphoreType.DMA((steps, 2)),
            pltpu.SemaphoreType.DMA((steps,)),
            pltpu.SemaphoreType.DMA((steps,)),
            pltpu.SemaphoreType.DMA((2, 3)),
            pltpu.SemaphoreType.DMA,
            pltpu.SemaphoreType.DMA((2, max(1, len(loads)))),
        ],
        compiler_params=params(56, collective_id=number, has_side_effects=True),
        cost_estimate=TINY,
        name="feed",
    )(normed, normed_t, cot, cot_t, *extra)


def project_back_kernel(dq_ref, own_kv_ref, recv_kv_ref, cos_ref, sin_ref, nl_ref, xp_ref, dres_ref, pi_ref, *refs):
    w_ref, gain_ref, ig_ref, own_ref, sib_ref, dgain_ref, dbias_ref, g_scr = refs
    t = pl.program_id(0)

    @pl.when(t == 0)
    def _():
        g_scr[...] = jnp.zeros(g_scr.shape, F32)
        dgain_ref[...] = jnp.zeros(dgain_ref.shape, F32)
        dbias_ref[...] = jnp.zeros(dbias_ref.shape, F32)

    cos, sin = cos_ref[...], sin_ref[...]
    low = lax.broadcasted_iota(jnp.int32, cos.shape, 1) % HEAD_SIZE < HEAD_SIZE // 2
    parts = []
    dkv = (own_kv_ref[...] + recv_kv_ref[...].astype(F32)).astype(BF16)
    for n in range(8):
        piece = (dq_ref[:, 128 * n : 128 * (n + 1)] if n < 7 else dkv[:, :KW]).astype(F32)
        parts.append((piece * cos - swap_halves(piece, low) * sin).astype(BF16))
    parts.append(dkv[:, KW:])
    d_lin = jnp.concatenate(parts, axis=1)
    dbias_ref[...] += jnp.sum(d_lin.astype(F32), axis=0, keepdims=True)
    d_normed = dot_nt(d_lin, w_ref[:, :QKV])
    xp = xp_ref[...].astype(F32)
    inv = lax.rsqrt(jnp.sum(xp * xp, axis=1, keepdims=True) * (1.0 / D) + norm_epsilon)
    hat = xp * inv
    scaled = d_normed * gain_ref[...]
    dgain_ref[...] += jnp.sum(d_normed * hat, axis=0, keepdims=True)
    mean = jnp.sum(scaled * hat, axis=1, keepdims=True) * (1.0 / D)
    grad = dres_ref[...] + inv * (scaled - hat * mean)
    high = grad.astype(BF16)
    rest = (grad - high.astype(F32)).astype(BF16)
    ig_ref[...] = dot_nt(high, pi_ref[...]) + dot_nt(rest, pi_ref[...])
    g_scr[...] += dot_tn(nl_ref[...], d_lin)

    @pl.when(t == pl.num_programs(0) - 1)
    def _():
        own_ref[...] = g_scr[:HALF].astype(BF16)
        sib_ref[...] = g_scr[HALF:].astype(BF16)


def project_back(dq, own_kv, recv_kv, cos, sin, nl, xp, d_res, pi, weights, gain, after=()):
    rows = xp.shape[0]
    width = weights.shape[1]

    def tile(cols):
        return pl.BlockSpec((TOKEN_TILE, cols), lambda t: (t, 0))

    def whole(r, c):
        return pl.BlockSpec((r, c), lambda t: (0, 0))

    return pl.pallas_call(
        following(project_back_kernel, 11, after),
        grid=(rows // TOKEN_TILE,),
        in_specs=[tile(QW), tile(256), tile(256), tile(128), tile(128), tile(D), tile(D), tile(D)]
        + [whole(D, D)]
        + [whole(D, width)]
        + [whole(1, D)]
        + [ANYWHERE] * len(after),
        out_specs=[tile(D), whole(HALF, QKV), whole(HALF, QKV), whole(1, D), whole(1, QKV)],
        out_shape=[
            jax.ShapeDtypeStruct((rows, D), F32),
            jax.ShapeDtypeStruct((HALF, QKV), BF16),
            jax.ShapeDtypeStruct((HALF, QKV), BF16),
            jax.ShapeDtypeStruct((1, D), F32),
            jax.ShapeDtypeStruct((1, QKV), F32),
        ],
        scratch_shapes=[pltpu.VMEM((D, QKV), F32)],
        compiler_params=params(56),
        cost_estimate=TINY,
        name="project_back",
    )(dq, own_kv, recv_kv, cos, sin, nl, xp, d_res, pi, weights, gain, *after)


def step_of(first_new, second_new):
    return (
        first_new
        / (1.0 - beta_first**STEP)
        / (jnp.sqrt(second_new / (1.0 - beta_second**STEP)) + adam_epsilon)
    )


def split_two(value):
    high = value.astype(BF16)
    return high, (value - high.astype(F32)).astype(BF16)


def product(dot, a, b):
    return dot(a[0], b[0]) + (dot(a[0], b[1]) + dot(a[1], b[0]))


def side_by_side(value):
    return jnp.concatenate([value[BW * t : BW * (t + 1)] for t in range(D // BW)], axis=1)


def one_above_other(value):
    return jnp.concatenate([value[:, BW * t : BW * (t + 1)] for t in range(D // BW)], axis=0)


def pick_kernel(spans, counts, block_ref, pi_ref, *refs):
    arrays, at = [], 0
    for count in counts:
        arrays.append(refs[at : at + count])
        at += count
    out_ref, w_scr, sem = refs[at:]
    slots = out_ref.shape[0]

    def each(slot, act):
        block = block_ref[slot]
        for n, pieces in enumerate(arrays):
            for page, (low, high) in enumerate(spans[n]):

                @pl.when((block >= low) & (block < high))
                def _(pieces=pieces, page=page, low=low):
                    column = pl.multiple_of((block - low) * BW, BW)
                    row = 0
                    for k, piece in enumerate(pieces):
                        count = piece.shape[1]
                        act(
                            pltpu.make_async_copy(
                                piece.at[page, :, pl.ds(column, BW)],
                                w_scr.at[slot, pl.ds(row, count), :],
                                sem.at[slot, k],
                            )
                        )
                        row += count

    for slot in range(slots):
        each(slot, lambda copy: copy.start())
    for slot in range(slots):
        each(slot, lambda copy: copy.wait())
        out_ref[slot] = dot_nn(pi_ref[...], w_scr[slot])


def picked(slot_block, pi, arrays, spans, after=()):
    capacity = slot_block.shape[0]
    vmem = pl.BlockSpec(memory_space=pltpu.VMEM)
    flat = [p for a in arrays for p in a]
    return pl.pallas_call(
        following(
            functools.partial(pick_kernel, spans, [len(a) for a in arrays]), 2 + len(flat), after
        ),
        in_specs=[pl.BlockSpec(memory_space=pltpu.SMEM), vmem]
        + [ANYWHERE] * (len(flat) + len(after)),
        out_specs=vmem,
        out_shape=jax.ShapeDtypeStruct((capacity, D, BW), F32),
        scratch_shapes=[pltpu.VMEM((capacity, D, BW), BF16), pltpu.SemaphoreType.DMA((capacity, 8))],
        compiler_params=params(60),
        cost_estimate=TINY,
        name="picked",
    )(slot_block, pi, *flat, *after)


def adam_kernel(block_ref, grad_ref, weight_ref, first_ref, second_ref, left_ref, right_ref, first_out, second_out, block_out):
    used = block_ref[pl.program_id(0)] >= 0

    @pl.when(used)
    def _():
        grad = grad_ref[0]
        left, right = split_two(left_ref[0]), split_two(right_ref[0])
        turned = split_two(side_by_side(dot_nn(grad, right[0]) + dot_nn(grad, right[1])))
        rotated = one_above_other(product(dot_tn, left, turned))
        first_new = beta_first * first_ref[0] + (1.0 - beta_first) * rotated
        second_new = beta_second * second_ref[0] + (1.0 - beta_second) * rotated * rotated
        first_out[0] = first_new
        second_out[0] = second_new
        step = split_two(step_of(first_new, second_new))
        back = split_two(side_by_side(product(dot_nt, step, right)))
        back = one_above_other(product(dot_nn, left, back))
        weights = weight_ref[0]
        block_out[0] = weights - rate_matrix * (back + weight_decay * weights)

    @pl.when(jnp.logical_not(used))
    def _():
        for ref in (first_out, second_out, block_out):
            ref[...] = jnp.zeros(ref.shape, F32)


def pack_kernel(spots, targets, counts, block_ref, *refs):
    n_in = sum(counts)
    ins, outs, (slots_ref, all_scr) = refs[:n_in], refs[n_in:-2], refs[-2:]
    at = 0
    for count, found in zip(counts, spots):
        for page, (width, target) in enumerate(found):
            total = ins[at][page, :, :width]
            for ref in ins[at + 1 : at + count]:
                total = total + ref[page, : total.shape[0], :width].astype(F32)
            all_scr[:, target : target + width] = total
        at += count
    for ref, start in zip(outs, targets):
        ref[...] = all_scr[:, start : start + ref.shape[1]]

    def one(slot, carry):
        block = jnp.maximum(block_ref[slot], 0)
        column = pl.multiple_of(block * BW, BW)
        slots_ref[slot] = all_scr[:, pl.ds(column, BW)].astype(BF16)
        return carry

    lax.fori_loop(0, slots_ref.shape[0], one, 0)


def packed(slot_block, groups, spots, targets):
    rows = groups[0][0].shape[1]
    vmem = pl.BlockSpec(memory_space=pltpu.VMEM)
    parts = [part for group in groups for part in group]
    total = (130 + 1) * BW
    return pl.pallas_call(
        functools.partial(
            pack_kernel, spots, [start for start, _ in targets], [len(g) for g in groups]
        ),
        in_specs=[pl.BlockSpec(memory_space=pltpu.SMEM)] + [vmem] * len(parts),
        out_specs=[vmem] * (len(targets) + 1),
        out_shape=[jax.ShapeDtypeStruct((rows, width), F32) for _, width in targets]
        + [jax.ShapeDtypeStruct((slot_block.shape[0], rows, BW), BF16)],
        scratch_shapes=[pltpu.VMEM((rows, total), F32)],
        compiler_params=params(60),
        cost_estimate=TINY,
        name="packed",
    )(slot_block, *parts)


def rotated_adam(slot_block, grads, weights, first_moment, second_moment, left, right):
    capacity = first_moment.shape[0]
    slab = pl.BlockSpec((1, D, BW), lambda s, b: (s, 0, 0))
    basis = pl.BlockSpec((1, BW, BW), lambda s, b: (s, 0, 0))
    return pl.pallas_call(
        adam_kernel,
        grid_spec=pltpu.PrefetchScalarGridSpec(
            num_scalar_prefetch=1,
            grid=(capacity,),
            in_specs=[slab, slab, slab, slab, basis, basis],
            out_specs=[slab] * 3,
        ),
        out_shape=[jax.ShapeDtypeStruct((capacity, D, BW), F32)] * 3,
        compiler_params=params(60),
        cost_estimate=TINY,
        name="rotated_adam",
    )(slot_block, grads, weights, first_moment, second_moment, left, right)


def vector_adam(vectors, grad_vectors, vector_first, vector_second):
    first_new = beta_first * vector_first + (1.0 - beta_first) * grad_vectors
    second_new = beta_second * vector_second + (1.0 - beta_second) * grad_vectors * grad_vectors
    return (second_new, vectors - rate_vector * step_of(first_new, second_new))


def hand_out(moving, arrived, after=()):
    at = 0
    for r in moving:
        came = arrived[at : at + len(r.next)]
        at += len(r.next)
        kind = r.next[0][0]
        if kind == "long":
            r.fold(came, after)
        elif kind == "short":
            r.share(came, after)
        else:
            r.end(came)
            r.next = []


def on_device(
    places,
    inputs,
    cotangent,
    starts,
    query_weight,
    key_weight,
    value_weight,
    out_weight,
    gate_weight,
    up_weight,
    down_weight,
    vectors,
    owner_slot,
    first_moment,
    second_moment,
    basis_left,
    basis_right,
    vector_first,
    vector_second,
):
    n_dev, shard_rows = places.n_dev, places.rows
    here = inputs.shape[2]
    seq_index = lax.axis_index("seq")
    vec_here = vectors.shape[0]

    out_t, down_t = out_weight.T, down_weight.T
    natural = places.natural_rows()
    pi = (jnp.arange(D, dtype=jnp.int32)[:, None] == natural[None, :]).astype(BF16)
    riding = (
        jnp.arange(n_dev, dtype=jnp.int32)[:, None] * shard_rows == natural[None, :]
    ).astype(BF16)
    vector_rows = jnp.pad(vectors.reshape(1, vec_here), ((0, shard_rows - 1), (0, 128 - vec_here)))
    cot = cotangent[:, 0].reshape(-1, D)
    cot_p = dot_nn(cot, pi).astype(BF16)
    cot_t = lax.dot_general(
        pi, cot, (((0,), (1,)), ((), ())), preferred_element_type=F32
    ).astype(BF16)
    attention_line = stacked_rows(
        line_parts(
            places,
            rounded(
                [query_weight, key_weight, value_weight, out_t, vector_rows],
                places.padded,
                [(0, 0, 0, QW), (0, 1, 0, KW), (0, 2, 0, KW), (0, 3, 0, QW), (0, 4, 0, 128)],
            ),
        ),
        after=(cot_p, cot_t),
    )
    feed_parts = [gate_weight, up_weight, down_t]

    def shard_of(chunks, after):
        spans = [(m, m, OFFSETS[n], CHUNKS[n]) for n in chunks for m in range(3)]
        return rounded(feed_parts, places.padded, spans, after=after)

    shard_a = shard_of((0,), ())
    backwards = [(-k % places.line, places.line) for k in range(1, places.line)]
    attention, *arrived = spread(attention_line, [(kind, shard_a) for kind in backwards])
    line_a = stacked_rows([shard_a] + arrived)
    shard_b = shard_of((1,), (attention,))
    short_a, long_a = send(line_a, places.short), send(line_a, places.long)
    attention_pages, attention = attention, attention[0]
    riders = attention[:, QKV + QW :]
    vectors_full = dot_nn(riding, riders)[:, :vec_here].reshape(-1)
    gains = jnp.pad(vectors_full[: 2 * D].reshape(2, D), ((0, 6), (0, 0))).astype(BF16)
    gains = dot_nn(gains, pi)
    gain_attn, gain_mlp = gains[0:1], gains[1:2]
    bias = vectors_full[2 * D :].reshape(1, QKV)

    spots = seq_index * here + jnp.arange(here, dtype=jnp.int32)
    own_starts = starts[:, 0]
    before = own_starts[:, None, :] <= spots[None, :, None]
    doc_begin = jnp.max(jnp.where(before, own_starts[:, None, :], 0), axis=2)
    relative = (spots[None, :] - doc_begin).astype(F32).reshape(-1)
    frequency = jnp.power(
        rope_theta, -jnp.arange(0, HEAD_SIZE, 2, dtype=F32) / HEAD_SIZE
    )
    angles = relative[:, None] * frequency[None, :]
    cos, sin = jnp.cos(angles), jnp.sin(angles)
    cos = jnp.concatenate([cos] * 4, axis=1)
    sin = jnp.concatenate([-sin, sin, -sin, sin], axis=1)
    begin = doc_begin + here - seq_index * here
    lo = begin[:, ::128] // 128
    begin = begin[:, None, :]

    x = inputs[:, 0].reshape(-1, D)
    xp, nl, q, k, v, kv = project(
        x, pi, attention, gain_attn, bias, cos, sin, after=(line_a, shard_b)
    )
    line_b = stacked_rows(line_parts(places, shard_b), after=(q,))
    far_a = send(short_a, places.long)
    short_b, long_b = send(line_b, places.short), send(line_b, places.long)
    shard_c = shard_of((2,), (line_b,))

    back = [(2 * n + 1, 2 * n) for n in range(n_dev // 2)]

    def streams(array):
        return array.reshape(MICRO, here, array.shape[-1])

    heads = (
        lo,
        streams(q),
        streams(kv[:, :KW]),
        streams(k),
        streams(kv[:, KW:]),
        streams(v),
        begin,
    )
    attended, lse = attend(*heads, after=(line_b, short_a, shard_c))
    attended_flat = attended.reshape(-1, QW)
    residual, normed, normed_t = middle(
        attended_flat, xp, attention, gain_mlp, after=(short_b,)
    )
    far_b = send(short_b, places.long)
    shard_last = shard_of((2,), (attended,))
    line_c = stacked_rows(line_parts(places, shard_c, shard_last), after=(normed,))
    shard_d = shard_of((3,), (line_b,))

    sums = None
    reductions, feed_pieces = [], []

    pieces = [[line_a, short_a, long_a, far_a], [line_b, short_b, long_b, far_b]]
    lines = [line_c]
    for n, wide in enumerate(CHUNKS):
        coming = (0, CHUNKS[n + 2]) if n + 2 < len(CHUNKS) else None
        moving = [r for r in reductions if r.next]
        loads = [load for r in moving for load in r.next]
        if n == 0:
            loads = [(kind, shard_d) for kind in backwards]
        mlp, d_normed, kept, passed, far, *arrived = feed(
            n, wide, normed, normed_t, cot_p, cot_t, sums, pieces[n],
            lines[n] if coming else None, coming, loads,
        )
        sums = (mlp, d_normed)
        feed_pieces.append(list(pieces[n]) + [far])
        if coming:
            pieces.append([arrived.pop(0)])
        if n == 0:
            lines.append(stacked_rows([shard_d] + arrived))
        hand_out(moving, arrived)
        reductions.append(Reduce(places, kept, passed))

    along = {"long": places.long, "short": places.short}

    def set_off(moving):
        return [
            send(array, along[kind] if kind in along else places.ahead[kind[0]])
            for r in moving
            for kind, array in r.next
        ]

    def operands(moving):
        return tuple(array for r in moving for _, array in r.next)

    moving, newest = [r for r in reductions[:-1] if r.next], reductions[-1:]
    arrived, arrived_late = set_off(moving), set_off(newest)
    output, d_res, d_att, own_out, other_out, d_gain_mlp = middle_back(
        residual, sums[0], sums[1], cot_p, attended_flat, pi, attention, gain_mlp,
        after=operands(moving + newest),
    )
    ended = tuple(arrived[: places.line - 1])
    hand_out(moving, arrived, (d_att,))
    moving = [r for r in reductions[:-1] if r.next]
    arrived = set_off(moving)
    dq, dkv, dkv_recv = attend_back(
        *heads, attended, streams(d_att), lse, after=operands(moving) + ended
    )
    dkv_recv = send(dkv_recv, back)
    hand_out(newest, arrived_late, (dq,))
    hand_out(moving, arrived, (dq,))
    moving = [r for r in reductions if r.next and r.next[0][0] == "short"]
    arrived = set_off(moving)
    input_grad, own_in, other_in, d_gain_attn, d_bias = project_back(
        dq.reshape(-1, QW), dkv.reshape(-1, 2 * KW), dkv_recv.reshape(-1, 2 * KW),
        cos, sin, nl, xp, d_res, pi, attention, gain_attn, after=operands(moving),
    )
    hand_out(moving, arrived, (own_in,))

    d_gains = jnp.concatenate([d_gain_attn, d_gain_mlp, jnp.zeros((6, D), F32)], axis=0)
    high, rest = split_two(d_gains)
    d_gains = dot_nt(high, pi) + dot_nt(rest, pi)
    d_vectors = jnp.concatenate([d_gains[0], d_gains[1], d_bias[0]])
    d_vectors = jnp.pad(d_vectors.reshape(n_dev, vec_here), ((0, 0), (0, 128 - vec_here)))
    riders = dot_tn(riding, d_vectors.astype(BF16)).astype(BF16)
    moving = [r for r in reductions if r.next]
    grad_in, *arrived = reduce_tail(
        places,
        [own_out, own_in, riders[:HALF]],
        [other_out, other_in, riders[HALF:]],
        [load for r in moving for load in r.next],
    )
    hand_out(moving, arrived)

    capacity = first_moment.shape[0]
    slot_count = n_dev * capacity
    slot_block = (
        jnp.full((slot_count,), -1, jnp.int32)
        .at[owner_slot]
        .set(jnp.arange(owner_slot.shape[0], dtype=jnp.int32))
    )
    spots = [
        [(w, 2048 + m * FF + o) for m in range(3)] for o, w in zip(OFFSETS, CHUNKS)
    ]
    groups = [r.parts for r in reductions]
    for start, width, target in ((0, QW, QKV), (QW, QKV, 0), (QW + QKV, BW, 130 * BW)):
        groups.append([grad_in[:, :, start : start + width]])
        spots.append([(width, target)])
    targets = [
        (0, QW), (QW, KW), (QW + KW, KW), (QKV, QW),
        (2048, FF), (2048 + FF, FF), (2048 + 2 * FF, FF), (130 * BW, BW),
    ]
    (
        grad_query, grad_key, grad_value, grad_out_t, grad_gate, grad_up, grad_down_t, rider_sums, slots,
    ) = packed(slot_block, groups, spots, targets)
    grad_vectors = rider_sums[0, :vec_here]
    owned_grads = lax.all_to_all(
        slots,
        BOTH,
        split_axis=0,
        concat_axis=1,
        tiled=True,
    )
    local_block = lax.dynamic_slice_in_dim(
        slot_block, lax.axis_index(BOTH) * capacity, capacity, 0
    )
    spans = [[(0, 16)]]
    for o, w in zip(OFFSETS, CHUNKS):
        first, count = o // BW, w // BW
        spans.append(
            [(16 + 38 * m + first, 16 + 38 * m + first + count) for m in range(3)]
        )
    owned_weights = picked(
        local_block, pi, [[attention_pages]] + feed_pieces, spans, after=(slots,)
    )
    new_first, new_second, new_blocks = rotated_adam(
        local_block, owned_grads, owned_weights, first_moment, second_moment, basis_left, basis_right
    )
    vector_second_new, vector_new = vector_adam(vectors, grad_vectors, vector_first, vector_second)
    return (
        output.reshape(inputs.shape),
        input_grad.reshape(inputs.shape),
        grad_query,
        grad_key,
        grad_value,
        grad_out_t.T,
        grad_gate,
        grad_up,
        grad_down_t.T,
        grad_vectors,
        new_first,
        new_second,
        new_blocks,
        vector_second_new,
        vector_new,
    )


def solution(mesh):
    rows = P(("dp", "seq"), None)
    columns = P(None, ("dp", "seq"))
    tokens = P(None, "dp", "seq", None)
    slots = P(("dp", "seq"), None, None)
    line = P(("dp", "seq"))
    places = Places(mesh.shape["dp"], mesh.shape["seq"])
    return jax.shard_map(
        functools.partial(on_device, places),
        mesh=mesh,
        in_specs=(
            tokens, tokens, P(None, "dp", None), rows, rows, rows, columns, rows, rows, columns,
            line, P(), slots, slots, slots, slots, line, line,
        ),
        out_specs=(
            tokens, tokens, rows, rows, rows, columns, rows, rows, columns, line,
            slots, slots, slots, line, line,
        ),
        check_vma=False,
    )
```

```python
import functools
import math

import jax
import jax.numpy as jnp
import numpy as np
from jax import lax
from jax.experimental import pallas as pl
from jax.experimental.pallas import tpu as pltpu
from jax.sharding import PartitionSpec as P

D = 896
QUERY_HEADS = 14
KEY_VALUE_HEADS = 2
HEAD_SIZE = 64
BW = 128
MICRO = 2
STEP = 10
QW = 896
KW = 128
QKV = QW + 2 * KW
FF = 4864

norm_epsilon = 1e-06
rope_theta = 1000000.0
beta_first = 0.9
beta_second = 0.999
adam_epsilon = 1e-08
weight_decay = 0.01
rate_matrix = 0.1
rate_vector = 0.5
masked_value = -1e30

F32 = jnp.float32
BF16 = jnp.bfloat16
BOTH = ("dp", "seq")

TILE = 256
CHUNKS = (1280, 1280, 1280, 1024)
OFFSETS = (0, 1280, 2560, 3840)
QUARTER = 112
HALF = 448
TOKEN_TILE = 256

HEAD_SETS = (
    ((0, 1, 2, 3), 0, 0),
    ((0, 1, 2), 1, 0),
    ((3, 4, 5, 6), 1, 1),
    ((4, 5, 6), 0, 1),
)
SET_ROWS = (0, 512, 896, 1408)
ALL_ROWS = 1792


def params(mib, **more):
    return pltpu.CompilerParams(vmem_limit_bytes=mib * 1024 * 1024, **more)


def dot_nn(a, b):
    return lax.dot_general(a, b, (((1,), (0,)), ((), ())), preferred_element_type=F32)


def dot_nt(a, b):
    return lax.dot_general(a, b, (((1,), (1,)), ((), ())), preferred_element_type=F32)


def dot_tn(a, b):
    return lax.dot_general(a, b, (((0,), (0,)), ((), ())), preferred_element_type=F32)


def following(kernel, n_in, after):
    def wrapped(*refs):
        return kernel(*refs[:n_in], *refs[n_in + len(after) :])

    return wrapped


TINY = pl.CostEstimate(flops=1, bytes_accessed=1, transcendentals=0)
ANYWHERE = pl.BlockSpec(memory_space=pl.ANY)


class Places:
    def __init__(self, n_dp, n_seq):
        self.line = n_dp // 4
        self.rows = D // (n_dp * n_seq)
        self.n_dev = n_dp * n_seq
        self.padded = -(-self.rows // 16) * 16

        def pairs(move):
            found = []
            for z in range(self.line):
                for x in range(2):
                    for c in range(2):
                        for y in range(2):
                            tz, tx, tc, ty = move(z, x, c, y)
                            found.append(
                                (((z * 2 + x) * 2 + c) * 2 + y, ((tz * 2 + tx) * 2 + tc) * 2 + ty)
                            )
            return found

        self.sibling = pairs(lambda z, x, c, y: (z, x, 1 - c, y))
        self.long = pairs(lambda z, x, c, y: (z, 1 - x, c, y) if c == 0 else (z, x, c, 1 - y))
        self.short = pairs(lambda z, x, c, y: (z, 1 - x, c, y) if c == 1 else (z, x, c, 1 - y))
        self.ahead = [
            pairs(lambda z, x, c, y, k=k: ((z + k) % self.line, x, c, y)) for k in range(self.line)
        ]

    def natural_rows(self):
        dp = lax.axis_index("dp")
        y = lax.axis_index("seq")
        z, x, c = dp // 4, (dp // 2) % 2, dp % 2
        place = jnp.arange(D, dtype=jnp.int32)
        dc, da, db = place // HALF, (place // (2 * QUARTER)) % 2, (place // QUARTER) % 2
        dz, inner = (place % QUARTER) // self.rows, place % self.rows
        c_own = c ^ dc
        x_own = x ^ jnp.where(c_own == 0, da, db)
        y_own = y ^ jnp.where(c_own == 0, db, da)
        z_own = (z + dz) % self.line
        return self.rows * (((z_own * 2 + x_own) * 2 + c_own) * 2 + y_own) + inner


def send(array, pairs):
    return lax.ppermute(array, BOTH, pairs)


def line_parts(places, shard, last=None):
    count = places.line
    return [shard] + [
        send(shard if last is None or k < count - 1 else last, places.ahead[-k % count])
        for k in range(1, count)
    ]


def stack_kernel(count, *refs):
    ins, (out, scr) = refs[:count], refs[count:]
    rows = QUARTER // count
    for k, ref in enumerate(ins):
        scr[rows * k : rows * (k + 1), :] = ref[0, :rows].astype(F32)
    out[0] = scr[...].astype(BF16)


def stacked_rows(parts, after=()):
    pages, rows, width = parts[0].shape
    return pl.pallas_call(
        following(functools.partial(stack_kernel, len(parts)), len(parts), after),
        grid=(pages,),
        in_specs=[pl.BlockSpec((1, rows, width), lambda m: (m, 0, 0))] * len(parts)
        + [ANYWHERE] * len(after),
        out_specs=pl.BlockSpec((1, QUARTER, width), lambda m: (m, 0, 0)),
        out_shape=jax.ShapeDtypeStruct((pages, QUARTER, width), BF16),
        scratch_shapes=[pltpu.VMEM((QUARTER, width), F32)],
        compiler_params=params(60),
        cost_estimate=TINY,
        name="stacked_rows",
    )(*parts, *after)


def neighbours():
    dp, seq = lax.axis_index("dp"), lax.axis_index("seq")
    core = lax.rem(dp, 2)
    first = dp + 2 - 4 * lax.rem(dp // 2, 2)
    sibling = (dp + 1 - 2 * core, seq)
    long = (jnp.where(core == 0, first, dp), jnp.where(core == 0, seq, 1 - seq))
    short = (jnp.where(core == 0, dp, first), jnp.where(core == 0, 1 - seq, seq))
    return sibling, long, short


def greet(devices):
    barrier = pltpu.get_barrier_semaphore()
    for device in devices:
        pl.semaphore_signal(barrier, inc=1, device_id=device, device_id_type=pl.DeviceIdType.MESH)
    pl.semaphore_wait(barrier, len(devices))


def push(src, dst, sems, n, device):
    return pltpu.make_async_remote_copy(
        src_ref=src,
        dst_ref=dst,
        send_sem=sems.at[0, n],
        recv_sem=sems.at[1, n],
        device_id=device,
        device_id_type=pl.DeviceIdType.MESH,
    )


def quarter(ref, k):
    return ref.at[:, pl.ds(QUARTER * k, QUARTER), :]


def device_of(kind):
    if isinstance(kind, str):
        return dict(zip(("sibling", "long", "short"), neighbours()))[kind]
    ahead, line = kind
    dp = lax.axis_index("dp")
    return (lax.rem(dp // 4 + ahead, line) * 4 + lax.rem(dp, 4), lax.axis_index("seq"))


def greet_kinds(kinds):
    found = []
    for kind in kinds:
        if kind not in found:
            found.append(kind)
    greet([device_of(kind) for kind in found])


def carried(kinds, srcs, dsts, sems):
    return [
        push(src, dst, sems, n, device_of(kind))
        for n, (kind, src, dst) in enumerate(zip(kinds, srcs, dsts))
    ]


def carrying(kernel, kinds, n_in, n_out):
    count = len(kinds)

    def wrapped(*refs):
        ins, srcs = refs[:n_in], refs[n_in : n_in + count]
        at = n_in + count
        outs, dsts = refs[at : at + n_out], refs[at + n_out : at + n_out + count]
        scratch, sems = refs[at + n_out + count : -1], refs[-1]

        @pl.when(pl.program_id(0) == 0)
        def _():
            greet_kinds(kinds)
            for move in carried(kinds, srcs, dsts, sems):
                move.start()

        kernel(*ins, *outs, *scratch)

        @pl.when(pl.program_id(0) == pl.num_programs(0) - 1)
        def _():
            for move in carried(kinds, srcs, dsts, sems):
                move.wait()

    return wrapped


def like(array):
    return jax.ShapeDtypeStruct(array.shape, array.dtype)


def spread_kernel(kinds, own, *refs):
    count = len(kinds)
    srcs, out, dsts, (sems, here_sem, more_sems) = (
        refs[:count], refs[count], refs[count + 1 : 2 * count + 1], refs[2 * count + 1 :],
    )
    sibling, long, short = neighbours()
    greet_kinds(("sibling", "long", "short") + tuple(kinds))
    for move in carried(kinds, srcs, dsts, more_sems):
        move.start()
    here = pltpu.make_async_copy(own, quarter(out, 0), here_sem)
    moves = [
        push(own, quarter(out, 1), sems, 0, short),
        push(own, quarter(out, 2), sems, 1, long),
        push(own, quarter(out, 4), sems, 2, sibling),
    ]
    here.start()
    for move in moves:
        move.start()
    for k, first in ((1, 3), (2, None), (3, None)):
        moves[{1: 0, 2: 1, 3: 3}[k]].wait_recv()
        if first is not None:
            moves.append(push(quarter(out, 1), quarter(out, 3), sems, 3, long))
            moves[-1].start()
        moves.append(push(quarter(out, k), quarter(out, 4 + k), sems, 3 + k, sibling))
        moves[-1].start()
    here.wait()
    for n, move in enumerate(moves):
        move.wait_send()
        if n not in (0, 1, 3):
            move.wait_recv()
    for move in carried(kinds, srcs, dsts, more_sems):
        move.wait()


def spread(own, loads):
    kinds = tuple(kind for kind, _ in loads)
    return pl.pallas_call(
        functools.partial(spread_kernel, kinds),
        in_specs=[ANYWHERE] * (1 + len(loads)),
        out_specs=[ANYWHERE] * (1 + len(loads)),
        out_shape=[jax.ShapeDtypeStruct((1, D, own.shape[2]), BF16)] + [like(a) for _, a in loads],
        scratch_shapes=[
            pltpu.SemaphoreType.DMA((2, 7)),
            pltpu.SemaphoreType.DMA,
            pltpu.SemaphoreType.DMA((2, max(1, len(loads)))),
        ],
        compiler_params=params(60, collective_id=8, has_side_effects=True),
        cost_estimate=TINY,
        name="spread",
    )(own, *[array for _, array in loads])


def fold_kernel(count, *refs):
    total = refs[0][...].astype(F32)
    for ref in refs[1:count]:
        total = total + ref[...].astype(F32)
    refs[count][...] = total.astype(BF16)


def fold(terms, rows, after=()):
    pages, _, width = terms[0][0].shape

    def spec(block):
        return pl.BlockSpec((1, rows, width), lambda m: (m, block, 0))

    return pl.pallas_call(
        following(functools.partial(fold_kernel, len(terms)), len(terms), after),
        grid=(pages,),
        in_specs=[spec(block) for _, block in terms] + [ANYWHERE] * len(after),
        out_specs=spec(0),
        out_shape=jax.ShapeDtypeStruct((pages, rows, width), BF16),
        compiler_params=params(60),
        cost_estimate=TINY,
        name="fold",
    )(*[array for array, _ in terms], *after)


def share_kernel(count, rows, *refs):
    scr = refs[-1]
    outs = refs[count:-1]
    total = refs[0][0].astype(F32)
    for ref in refs[1:count]:
        total = total + ref[0].astype(F32)
    scr[...] = total
    for k, ref in enumerate(outs):
        ref[0, :rows] = scr[rows * k : rows * (k + 1), :].astype(ref.dtype)


def share(terms, rows, padded, line, after=()):
    pages, _, width = terms[0].shape
    part = [
        pl.BlockSpec((1, padded if k else rows, width), lambda m: (m, 0, 0)) for k in range(line)
    ]
    return pl.pallas_call(
        following(functools.partial(share_kernel, len(terms), rows), len(terms), after),
        grid=(pages,),
        in_specs=[pl.BlockSpec((1, QUARTER, width), lambda m: (m, 0, 0))] * len(terms)
        + [ANYWHERE] * len(after),
        out_specs=part,
        out_shape=[
            jax.ShapeDtypeStruct((pages, padded if k else rows, width), BF16 if k else F32)
            for k in range(line)
        ],
        scratch_shapes=[pltpu.VMEM((QUARTER, width), F32)],
        compiler_params=params(60),
        cost_estimate=TINY,
        name="share",
    )(*terms, *after)


class Reduce:
    def __init__(self, places, kept, passed):
        self.places, self.terms = places, [kept]
        self.next = [("long", passed)]

    def fold(self, arrived, after):
        self.terms.append(arrived[0])
        self.next = [("short", fold([(t, 1) for t in self.terms], QUARTER, after))]

    def share(self, arrived, after):
        self.terms.append(arrived[0])
        line = self.places.line
        mine, *parts = share(self.terms, self.places.rows, self.places.padded, line, after)
        self.parts = [mine]
        self.next = [((k + 1, line), part) for k, part in enumerate(parts)]

    def end(self, arrived):
        self.parts += list(arrived)


def tail_kernel(line, rows, widths, load_kinds, *refs):
    parts_n, count = len(widths), len(load_kinds)
    owns, others = refs[:parts_n], refs[parts_n : 2 * parts_n]
    at = 2 * parts_n
    srcs, out, dsts = refs[at : at + count], refs[at + count], refs[at + count + 1 : at + 2 * count + 1]
    came, half, came_half, quart, came_quart, keep, parts, came_parts, sems, load_sems = refs[
        at + 2 * count + 1 :
    ]
    starts = [sum(widths[:n]) for n in range(parts_n)]
    spans = [slice(start, start + width) for start, width in zip(starts, widths)]
    sibling, long, short = neighbours()
    greet_kinds(["sibling", "long", "short"] + [(k, line) for k in range(1, line)])
    moves = []

    def go(src, dst, device):
        moves.append(push(src, dst, sems, len(moves), device))
        moves[-1].start()
        return moves[-1]

    first = [go(others[n], came.at[:, span], sibling) for n, span in enumerate(spans)]
    for move in carried(load_kinds, srcs, dsts, load_sems):
        move.start()
    two = 2 * QUARTER
    second, third, last = [], [], []
    for n, span in enumerate(spans):
        first[n].wait_recv()
        half[:, span] = (owns[n][two:].astype(F32) + came[two:, span].astype(F32)).astype(BF16)
        second.append(go(half.at[:, span], came_half.at[:, span], long))
        keep[:, span] = owns[n][:two].astype(F32) + came[:two, span].astype(F32)
    for n, span in enumerate(spans):
        second[n].wait_recv()
        total = keep[QUARTER:, span] + came_half[QUARTER:, span].astype(F32)
        quart[:, span] = total.astype(BF16)
        third.append(go(quart.at[:, span], came_quart.at[:, span], short))
        keep[:QUARTER, span] = keep[:QUARTER, span] + came_half[:QUARTER, span].astype(F32)
    for n, span in enumerate(spans):
        third[n].wait_recv()
        keep[:QUARTER, span] = keep[:QUARTER, span] + came_quart[:, span].astype(F32)
        for k in range(1, line):
            parts[k - 1, :rows, span] = keep[rows * k : rows * (k + 1), span].astype(BF16)
            last.append(
                go(parts.at[k - 1, :, span], came_parts.at[k - 1, :, span], device_of((k, line)))
            )
    for n, span in enumerate(spans):
        total = keep[:rows, span]
        for k in range(1, line):
            last[n * (line - 1) + k - 1].wait_recv()
            total = total + came_parts[k - 1, :rows, span].astype(F32)
        out[0, :, span] = total
    for move in moves:
        move.wait_send()
    for move in carried(load_kinds, srcs, dsts, load_sems):
        move.wait()


def reduce_tail(places, owns, others, loads):
    widths, line, padded = [a.shape[1] for a in owns], places.line, places.padded
    width = sum(widths)
    vmem = pl.BlockSpec(memory_space=pltpu.VMEM)
    return pl.pallas_call(
        functools.partial(
            tail_kernel, line, places.rows, widths, tuple(kind for kind, _ in loads)
        ),
        in_specs=[vmem] * (2 * len(owns)) + [ANYWHERE] * len(loads),
        out_specs=[vmem] + [ANYWHERE] * len(loads),
        out_shape=[jax.ShapeDtypeStruct((1, places.rows, width), F32)] + [like(a) for _, a in loads],
        scratch_shapes=[
            pltpu.VMEM((HALF, width), BF16),
            pltpu.VMEM((2 * QUARTER, width), BF16),
            pltpu.VMEM((2 * QUARTER, width), BF16),
            pltpu.VMEM((QUARTER, width), BF16),
            pltpu.VMEM((QUARTER, width), BF16),
            pltpu.VMEM((2 * QUARTER, width), F32),
            pltpu.VMEM((line - 1, padded, width), BF16),
            pltpu.VMEM((line - 1, padded, width), BF16),
            pltpu.SemaphoreType.DMA((2, len(owns) * (2 + line))),
            pltpu.SemaphoreType.DMA((2, max(1, len(loads)))),
        ],
        compiler_params=params(56, collective_id=11, has_side_effects=True),
        cost_estimate=TINY,
        name="reduce_tail",
    )(*owns, *others, *[array for _, array in loads])


def round_kernel(spans, *refs):
    ins, out = refs[:-1], refs[-1]
    at = [0] * out.shape[0]
    for page, which, offset, width in spans:
        piece = ins[which][:, offset : offset + width]
        out[page, : piece.shape[0], at[page] : at[page] + width] = piece.astype(BF16)
        at[page] += width


def rounded(parts, padded, spans, after=()):
    pages = 1 + max(page for page, _, _, _ in spans)
    width = sum(width for page, _, _, width in spans if page == 0)
    return pl.pallas_call(
        following(functools.partial(round_kernel, spans), len(parts), after),
        in_specs=[pl.BlockSpec(memory_space=pltpu.VMEM)] * len(parts) + [ANYWHERE] * len(after),
        out_specs=pl.BlockSpec(memory_space=pltpu.VMEM),
        out_shape=jax.ShapeDtypeStruct((pages, padded, width), BF16),
        compiler_params=params(60),
        cost_estimate=TINY,
        name="rounded",
    )(*parts, *after)


def swap_halves(tile, low_half):
    return jnp.where(low_half, pltpu.roll(tile, 96, 1), pltpu.roll(tile, 32, 1))


def project_kernel(x_ref, pi_ref, *refs):
    (
        w_ref, gain_ref, bias_ref, cos_ref, sin_ref, xp_ref, nl_ref, q_ref, k_ref, v_ref, came_hbm,
        kv_scr, sems,
    ) = refs
    step, steps = pl.program_id(0), kv_scr.shape[0] // TOKEN_TILE
    seq = lax.axis_index("seq")
    other = (lax.axis_index("dp"), 1 - seq)

    def hand_on(n):
        rows = pl.ds(pl.multiple_of(n * TOKEN_TILE, TOKEN_TILE), TOKEN_TILE)
        return push(kv_scr.at[rows, :], came_hbm.at[rows, :], sems, n, other)

    @pl.when(step == 0)
    def _():
        greet([other])

    xp = dot_nn(x_ref[...], pi_ref[...])
    inv = lax.rsqrt(jnp.sum(xp * xp, axis=1, keepdims=True) * (1.0 / D) + norm_epsilon)
    nl = (xp * inv * gain_ref[...]).astype(BF16)
    xp_ref[...] = xp.astype(BF16)
    nl_ref[...] = nl
    lin = dot_nn(nl, w_ref[:, :QKV]) + bias_ref[...]
    cos, sin = cos_ref[...], sin_ref[...]
    low = lax.broadcasted_iota(jnp.int32, cos.shape, 1) % HEAD_SIZE < HEAD_SIZE // 2
    for t in range(8):
        piece = lin[:, 128 * t : 128 * (t + 1)]
        turned = (piece * cos + swap_halves(piece, low) * sin).astype(BF16)
        if t < 7:
            q_ref[:, 128 * t : 128 * (t + 1)] = (turned.astype(F32) * 0.125).astype(BF16)
        else:
            k_ref[...] = turned
            kv_scr[pl.ds(pl.multiple_of(step * TOKEN_TILE, TOKEN_TILE), TOKEN_TILE), :KW] = turned
    value = lin[:, QW + KW :].astype(BF16)
    v_ref[...] = value
    kv_scr[pl.ds(pl.multiple_of(step * TOKEN_TILE, TOKEN_TILE), TOKEN_TILE), KW:] = value

    @pl.when(seq == 0)
    def _():
        hand_on(step).start()

    @pl.when((step == steps - 1) & (seq == 0))
    def _():
        for n in range(steps):
            hand_on(n).wait_send()

    @pl.when((step == steps - 1) & (seq == 1))
    def _():
        for n in range(steps):
            hand_on(n).wait_recv()


def project(x, pi, weights, gain, bias, cos, sin, after=()):
    rows = x.shape[0]
    width = weights.shape[1]

    def tile(cols):
        return pl.BlockSpec((TOKEN_TILE, cols), lambda t: (t, 0))

    def whole(r, c):
        return pl.BlockSpec((r, c), lambda t: (0, 0))

    shapes = [(D, BF16), (D, BF16), (QW, BF16), (KW, BF16), (KW, BF16)]
    return pl.pallas_call(
        following(project_kernel, 7, after),
        grid=(rows // TOKEN_TILE,),
        in_specs=[tile(D), whole(D, D)]
        + [whole(D, width)]
        + [whole(1, D), whole(1, QKV), tile(128), tile(128)]
        + [ANYWHERE] * len(after),
        out_specs=[tile(c) for c, _ in shapes] + [ANYWHERE],
        out_shape=[jax.ShapeDtypeStruct((rows, c), t) for c, t in shapes + [(2 * KW, BF16)]],
        scratch_shapes=[
            pltpu.VMEM((rows, 2 * KW), BF16),
            pltpu.SemaphoreType.DMA((2, rows // TOKEN_TILE)),
        ],
        compiler_params=params(56, collective_id=12, has_side_effects=True),
        cost_estimate=TINY,
        name="project",
    )(x, pi, weights, gain, bias, cos, sin, *after)


def padded_heads(recv, own, out, turned):
    for part, ref in enumerate((recv, own)):
        natural = ref[0].astype(F32)
        span = pl.ds(512 * part, 512)
        if out is not None:
            lane = lax.broadcasted_iota(jnp.int32, (512, 128), 1)
            crossed = pltpu.roll(natural, 64, 1)
            for s, (_, half, head) in enumerate(HEAD_SETS):
                source = natural if half == head else crossed
                keep = (lane >= 64) if half else (lane < 64)
                out[s, span, :] = jnp.where(keep, source, 0.0).astype(BF16)
        if turned is not None:
            flat = natural.T
            other = jnp.concatenate([flat[64:], flat[:64]], axis=0)
            row = lax.broadcasted_iota(jnp.int32, (128, 512), 0)
            for s, (_, half, head) in enumerate(HEAD_SETS):
                source = flat if half == head else other
                keep = (row >= 64) if half else (row < 64)
                turned[s, :, span] = jnp.where(keep, source, 0.0).astype(BF16)


def block_bias(kb, i, begin):
    shape = (128, 128)
    key = kb * 128 + lax.broadcasted_iota(jnp.int32, shape, 0)
    query = 512 + i * 128 + lax.broadcasted_iota(jnp.int32, shape, 1)
    return jnp.where((key >= begin) & (key <= query), 0.0, masked_value)


def stacked(tile_of, pairs):
    return jnp.concatenate([tile_of(p) for p in pairs], axis=0)


def turned_block(ref, out):
    for p in range(7):
        cols = slice(128 * p, 128 * (p + 1))
        out[:, cols] = ref[0, :, cols].astype(F32).T.astype(BF16)


def pair_columns(s):
    pairs = HEAD_SETS[s][0]
    return slice(128 * pairs[0], 128 * (pairs[-1] + 1))


def columns_of(s, n=None):
    pairs = HEAD_SETS[s][0]
    if n is None:
        return slice(SET_ROWS[s], SET_ROWS[s] + 128 * len(pairs))
    return slice(SET_ROWS[s] + 128 * n, SET_ROWS[s] + 128 * (n + 1))


def eights(value):
    return value.reshape(value.shape[0] // 8, 8, value.shape[1])


def attend_kernel(
    lo_ref, q_ref, kr_ref, ko_ref, vr_ref, vo_ref, ds_ref, o_ref, lse_ref, kp, vt, qt, s_scr, m_scr, l_scr, acc
):
    b, i = pl.program_id(0), pl.program_id(1)

    @pl.when(i == 0)
    def _():
        padded_heads(kr_ref, ko_ref, kp, None)
        padded_heads(vr_ref, vo_ref, None, vt)

    lo, hi = lo_ref[b, i], i + 5
    begin = ds_ref[0]
    turned_block(q_ref, qt)
    m_scr[...] = jnp.full(m_scr.shape, masked_value, F32)
    l_scr[...] = jnp.zeros(l_scr.shape, F32)
    acc[...] = jnp.zeros(acc.shape, F32)

    def scores(kb, carry):
        bias = block_bias(kb, i, begin)
        keys = pl.ds(pl.multiple_of(kb * 128, 128), 128)
        raws = [dot_nn(kp[s, keys, :], qt[:, pair_columns(s)]) for s in range(4)]
        for s, (pairs, _, _) in enumerate(HEAD_SETS):
            cols = columns_of(s)
            value = raws[s] + jnp.concatenate([bias] * len(pairs), axis=1)
            s_scr[kb, :, cols] = value
            m_scr[:, cols] = jnp.maximum(m_scr[:, cols], jnp.max(eights(value), axis=0))
        return carry

    lax.fori_loop(lo, hi, scores, 0)
    top = jnp.max(m_scr[...], axis=0, keepdims=True)

    def weigh(kb, carry):
        keys = pl.ds(pl.multiple_of(kb * 128, 128), 128)
        probs = [jnp.exp(s_scr[kb, :, columns_of(s)] - top[:, columns_of(s)]) for s in range(4)]
        parts = [dot_nn(vt[s, :, keys], probs[s].astype(BF16)) for s in range(4)]
        for s in range(4):
            cols = columns_of(s)
            l_scr[:, cols] += jnp.sum(eights(probs[s]), axis=0)
            acc[:, cols] += parts[s]
        return carry

    lax.fori_loop(lo, hi, weigh, 0)
    total = jnp.sum(l_scr[...], axis=0, keepdims=True)
    lse = top + jnp.log(total)
    share = 1.0 / total
    outs = [None] * 7
    for s, (pairs, half, _) in enumerate(HEAD_SETS):
        for n, p in enumerate(pairs):
            cols = columns_of(s, n)
            part = acc[:, cols] * share[:, cols]
            outs[p] = part if outs[p] is None else outs[p] + part
            head = 2 * p + half
            lse_ref[0, head : head + 1, :] = lse[:, cols]
    for p in range(7):
        o_ref[0, :, 128 * p : 128 * (p + 1)] = outs[p].T.astype(BF16)


def attend_specs():
    def block(cols):
        return pl.BlockSpec((1, 128, cols), lambda b, i, lo: (b, i, 0))

    def lanes(rows):
        return pl.BlockSpec((1, rows, 128), lambda b, i, lo: (b, 0, i))

    def stream(cols):
        return pl.BlockSpec((1, 512, cols), lambda b, i, lo: (b, 0, 0))

    return block, lanes, stream


def attend(lo, q, k_recv, k_own, v_recv, v_own, begin, after=()):
    block, lanes, stream = attend_specs()
    return pl.pallas_call(
        following(attend_kernel, 7, after),
        grid_spec=pltpu.PrefetchScalarGridSpec(
            num_scalar_prefetch=1,
            grid=(MICRO, 4),
            in_specs=[block(QW)] + [stream(KW)] * 4 + [lanes(1)] + [ANYWHERE] * len(after),
            out_specs=[block(QW), lanes(16)],
            scratch_shapes=[
                pltpu.VMEM((4, 1024, 128), BF16),
                pltpu.VMEM((4, 128, 1024), BF16),
                pltpu.VMEM((128, QW), BF16),
                pltpu.VMEM((8, 128, ALL_ROWS), F32),
                pltpu.VMEM((8, ALL_ROWS), F32),
                pltpu.VMEM((8, ALL_ROWS), F32),
                pltpu.VMEM((128, ALL_ROWS), F32),
            ],
        ),
        out_shape=[
            jax.ShapeDtypeStruct((MICRO, 512, QW), BF16),
            jax.ShapeDtypeStruct((MICRO, 16, 512), F32),
        ],
        compiler_params=params(56),
        cost_estimate=TINY,
        name="attend",
    )(lo, q, k_recv, k_own, v_recv, v_own, begin, *after)


def attend_back_kernel(
    lo_ref, q_ref, kr_ref, ko_ref, vr_ref, vo_ref, ds_ref, o_ref, do_ref, lse_ref,
    dq_ref, own_ref, recv_ref, kp, vp, kt, qt, dot_t, dk, dv, dq_acc,
):
    b, i = pl.program_id(0), pl.program_id(1)

    @pl.when(i == 0)
    def _():
        padded_heads(kr_ref, ko_ref, kp, kt)
        padded_heads(vr_ref, vo_ref, vp, None)
        dk[...] = jnp.zeros(dk.shape, F32)
        dv[...] = jnp.zeros(dv.shape, F32)

    lo, hi = lo_ref[b, i], i + 5
    begin = ds_ref[0]
    dq_acc[...] = jnp.zeros(dq_acc.shape, F32)
    turned_block(q_ref, qt)
    turned_block(do_ref, dot_t)
    pick = lax.broadcasted_iota(jnp.int32, (8, 128), 1) // 64 == lax.broadcasted_iota(
        jnp.int32, (8, 128), 0
    )
    pick = pick.astype(F32).astype(BF16)
    halves = []
    for p in range(7):
        cols = slice(128 * p, 128 * (p + 1))
        high, rest = split_two(o_ref[0, :, cols].astype(F32) * do_ref[0, :, cols].astype(F32))
        halves.append(dot_nt(pick, high) + dot_nt(pick, rest))
    lse, dots = [], []
    for pairs, half, _ in HEAD_SETS:
        heads = [2 * p + half for p in pairs]
        lse.append(jnp.concatenate([lse_ref[0, h : h + 1, :] for h in heads], axis=1))
        dots.append(jnp.concatenate([halves[p][half : half + 1] for p in pairs], axis=1))

    def one_block(kb, carry):
        bias = block_bias(kb, i, begin)
        keys = pl.ds(pl.multiple_of(kb * 128, 128), 128)
        work = []
        for s, (pairs, _, _) in enumerate(HEAD_SETS):
            cols = columns_of(s)
            x = stacked(lambda p: q_ref[0, :, 128 * p : 128 * (p + 1)], pairs)
            y = stacked(lambda p: do_ref[0, :, 128 * p : 128 * (p + 1)], pairs)
            raw = dot_nn(kp[s, keys, :], qt[:, pair_columns(s)]) + jnp.concatenate([bias] * len(pairs), axis=1)
            d_prob = dot_nn(vp[s, keys, :], dot_t[:, pair_columns(s)])
            work.append((s, cols, x, y, raw, d_prob))
        parts = []
        for s, cols, x, y, raw, d_prob in work:
            p = jnp.exp(raw - lse[s])
            d_score = (p * (d_prob - dots[s])).astype(BF16)
            parts.append((s, cols, x, y, p.astype(BF16), d_score))
        sums = [
            (s, cols, dot_nn(kt[s, :, keys], d_score), dot_nn(d_score, x), dot_nn(p, y))
            for s, cols, x, y, p, d_score in parts
        ]
        for s, cols, d_query, d_key, d_value in sums:
            dq_acc[:, cols] += d_query
            dk[s, keys, :] += d_key
            dv[s, keys, :] += d_value
        return carry

    lax.fori_loop(lo, hi, one_block, 0)
    sums = [None] * 7
    for s, (pairs, _, _) in enumerate(HEAD_SETS):
        for n, p in enumerate(pairs):
            part = dq_acc[:, columns_of(s, n)]
            sums[p] = part if sums[p] is None else sums[p] + part
    for p in range(7):
        dq_ref[0, :, 128 * p : 128 * (p + 1)] = (sums[p] * 0.125).T.astype(BF16)

    @pl.when(i == 3)
    def _():
        wide = lax.broadcasted_iota(jnp.int32, (512, 128), 1) < 64
        for part, ref in enumerate((recv_ref, own_ref)):
            rows = pl.ds(512 * part, 512)
            for n, grads in enumerate((dk, dv)):
                low = grads[0, rows, :] + pltpu.roll(grads[1, rows, :], 64, 1)
                high = grads[2, rows, :] + pltpu.roll(grads[3, rows, :], 64, 1)
                value = jnp.where(wide, low, high)
                ref[0, :, 128 * n : 128 * (n + 1)] = value.astype(ref.dtype)


def attend_back(lo, q, k_recv, k_own, v_recv, v_own, begin, out, d_out, lse, after=()):
    block, lanes, stream = attend_specs()
    return pl.pallas_call(
        following(attend_back_kernel, 10, after),
        grid_spec=pltpu.PrefetchScalarGridSpec(
            num_scalar_prefetch=1,
            grid=(MICRO, 4),
            in_specs=[block(QW)]
            + [stream(KW)] * 4
            + [lanes(1), block(QW), block(QW), lanes(16)]
            + [ANYWHERE] * len(after),
            out_specs=[block(QW), stream(256), stream(256)],
            scratch_shapes=[
                pltpu.VMEM((4, 1024, 128), BF16),
                pltpu.VMEM((4, 1024, 128), BF16),
                pltpu.VMEM((4, 128, 1024), BF16),
                pltpu.VMEM((128, QW), BF16),
                pltpu.VMEM((128, QW), BF16),
                pltpu.VMEM((4, 1024, 128), F32),
                pltpu.VMEM((4, 1024, 128), F32),
                pltpu.VMEM((128, ALL_ROWS), F32),
            ],
        ),
        out_shape=[
            jax.ShapeDtypeStruct((MICRO, 512, QW), BF16),
            jax.ShapeDtypeStruct((MICRO, 512, 256), F32),
            jax.ShapeDtypeStruct((MICRO, 512, 256), BF16),
        ],
        compiler_params=params(56),
        cost_estimate=TINY,
        name="attend_back",
    )(lo, q, k_recv, k_own, v_recv, v_own, begin, out, d_out, lse, *after)


def middle_kernel(att_ref, xp_ref, *refs):
    w_ref, gain_ref, res_ref, n_ref, nt_ref = refs
    residual = xp_ref[...].astype(F32) + dot_nt(att_ref[...], w_ref[:, QKV : QKV + QW])
    inv = lax.rsqrt(jnp.sum(residual * residual, axis=1, keepdims=True) * (1.0 / D) + norm_epsilon)
    normed = residual * inv * gain_ref[...]
    res_ref[...] = residual
    n_ref[...] = normed.astype(BF16)
    nt_ref[...] = normed.T.astype(BF16)


def middle(attended, xp, weights, gain, after=()):
    rows = xp.shape[0]
    width = weights.shape[1]

    def tile(cols):
        return pl.BlockSpec((2 * TOKEN_TILE, cols), lambda t: (t, 0))

    def whole(r, c):
        return pl.BlockSpec((r, c), lambda t: (0, 0))

    return pl.pallas_call(
        following(middle_kernel, 4, after),
        grid=(rows // (2 * TOKEN_TILE),),
        in_specs=[tile(QW), tile(D)]
        + [whole(D, width)]
        + [whole(1, D)]
        + [ANYWHERE] * len(after),
        out_specs=[tile(D), tile(D), pl.BlockSpec((D, 2 * TOKEN_TILE), lambda t: (0, t))],
        out_shape=[
            jax.ShapeDtypeStruct((rows, D), F32),
            jax.ShapeDtypeStruct((rows, D), BF16),
            jax.ShapeDtypeStruct((D, rows), BF16),
        ],
        compiler_params=params(56),
        cost_estimate=TINY,
        name="middle",
    )(attended, xp, weights, gain, *after)


def middle_back_kernel(res_ref, mlp_ref, dn_ref, cot_ref, att_ref, pi_ref, *refs):
    w_ref, gain_ref, out_ref, dres_ref, datt_ref, own_ref, sib_ref, dgain_ref, g_scr = refs
    t = pl.program_id(0)

    @pl.when(t == 0)
    def _():
        g_scr[...] = jnp.zeros(g_scr.shape, F32)
        dgain_ref[...] = jnp.zeros(dgain_ref.shape, F32)

    residual = res_ref[...]
    inv = lax.rsqrt(jnp.sum(residual * residual, axis=1, keepdims=True) * (1.0 / D) + norm_epsilon)
    out_low = (residual + mlp_ref[...]).astype(BF16)
    out_ref[...] = dot_nt(out_low, pi_ref[...]).astype(BF16)
    d_normed = dn_ref[...]
    hat = residual * inv
    scaled = d_normed * gain_ref[...]
    dgain_ref[...] += jnp.sum(d_normed * hat, axis=0, keepdims=True)
    mean = jnp.sum(scaled * hat, axis=1, keepdims=True) * (1.0 / D)
    d_res = cot_ref[...].astype(F32) + inv * (scaled - hat * mean)
    dres_ref[...] = d_res
    low = d_res.astype(BF16)
    datt_ref[...] = dot_nn(low, w_ref[:, QKV : QKV + QW]).astype(BF16)
    g_scr[...] += dot_tn(low, att_ref[...])

    @pl.when(t == pl.num_programs(0) - 1)
    def _():
        own_ref[...] = g_scr[:HALF].astype(BF16)
        sib_ref[...] = g_scr[HALF:].astype(BF16)


def middle_back(residual, mlp, d_normed, cot, attended, pi, weights, gain, after=()):
    rows = residual.shape[0]
    width = weights.shape[1]

    def tile(cols):
        return pl.BlockSpec((TOKEN_TILE, cols), lambda t: (t, 0))

    def whole(r, c):
        return pl.BlockSpec((r, c), lambda t: (0, 0))

    return pl.pallas_call(
        following(middle_back_kernel, 8, after),
        grid=(rows // TOKEN_TILE,),
        in_specs=[tile(D)] * 4
        + [tile(QW), whole(D, D)]
        + [whole(D, width)]
        + [whole(1, D)]
        + [ANYWHERE] * len(after),
        out_specs=[tile(D), tile(D), tile(QW), whole(HALF, QW), whole(HALF, QW), whole(1, D)],
        out_shape=[
            jax.ShapeDtypeStruct((rows, D), BF16),
            jax.ShapeDtypeStruct((rows, D), F32),
            jax.ShapeDtypeStruct((rows, QW), BF16),
            jax.ShapeDtypeStruct((HALF, QW), BF16),
            jax.ShapeDtypeStruct((HALF, QW), BF16),
            jax.ShapeDtypeStruct((1, D), F32),
        ],
        scratch_shapes=[pltpu.VMEM((D, QW), F32)],
        compiler_params=params(56),
        cost_estimate=TINY,
        name="middle_back",
    )(residual, mlp, d_normed, cot, attended, pi, weights, gain, *after)


def feed_kernel(wide, started, n_pieces, coming, kinds, *refs):
    n_in = 4 + (2 if started else 0)
    n_hbm, nt_hbm, cot_hbm, cott_hbm = refs[:4]
    sums_in = refs[4:n_in]
    pieces = refs[n_in : n_in + n_pieces]
    n_in += n_pieces
    if coming:
        line_hbm = refs[n_in]
        n_in += 1
    srcs = refs[n_in : n_in + len(kinds)]
    n_in += len(kinds)
    mlp_hbm, dn_hbm, keep_hbm, pass_hbm, far_hbm = refs[n_in : n_in + 5]
    n_in += 5
    if coming:
        next_hbm = refs[n_in]
        n_in += 1
    dsts = refs[n_in : n_in + len(kinds)]
    n_in += len(kinds)
    (
        n_v, nt_v, cot_v, cott_v, w_v, mlp_v, dn_v, act_v, grad_v, came_v,
        in_sem, w_sem, w_send, w_recv, out_sem, g_sem, g_send, g_recv, next_sem, next_here,
        carry_sem,
    ) = refs[n_in:]
    rows_all = n_v.shape[0]
    steps = wide // TILE
    span = 256
    parts = rows_all // span
    sibling, long, short = neighbours()
    mesh_id = pl.DeviceIdType.MESH
    share_rows = HALF // n_pieces

    def tile_of(j):
        return pl.ds(pl.multiple_of(j * TILE, TILE), TILE)

    def weight_copy(k, j):
        return pltpu.make_async_copy(
            pieces[k].at[:, :, tile_of(j)],
            w_v.at[:, pl.ds(share_rows * k, share_rows), tile_of(j)],
            w_sem.at[k, j],
        )

    def weight_push(k, j):
        return pltpu.make_async_remote_copy(
            src_ref=pieces[k].at[:, :, tile_of(j)],
            dst_ref=w_v.at[:, pl.ds(HALF + share_rows * k, share_rows), tile_of(j)],
            send_sem=w_send.at[k, j],
            recv_sem=w_recv.at[k, j],
            device_id=sibling,
            device_id_type=mesh_id,
        )

    def gradient_push(j):
        return pltpu.make_async_remote_copy(
            src_ref=grad_v.at[:, pl.ds(HALF, HALF), tile_of(j)],
            dst_ref=came_v.at[:, :, tile_of(j)],
            send_sem=g_send.at[j],
            recv_sem=g_recv.at[j],
            device_id=sibling,
            device_id_type=mesh_id,
        )

    def sum_copies(j):
        return [
            pltpu.make_async_copy(
                grad_v.at[:, pl.ds(2 * QUARTER * h, 2 * QUARTER), tile_of(j)],
                hbm.at[:, :, tile_of(j)],
                g_sem.at[j, h],
            )
            for h, hbm in enumerate((keep_hbm, pass_hbm))
        ]

    def add_sibling(j):
        cols = tile_of(j)
        gradient_push(j).wait_recv()
        for m in range(3):
            total = grad_v[m, :HALF, cols].astype(F32) + came_v[m, :, cols].astype(F32)
            grad_v[m, :HALF, cols] = total.astype(BF16)
        for copy in sum_copies(j):
            copy.start()

    def span_of(part):
        return pl.ds(part * span, span)

    loads = [
        pltpu.make_async_copy(src, dst, in_sem.at[n])
        for n, (src, dst) in enumerate(
            [(n_hbm, n_v), (cot_hbm, cot_v), (nt_hbm, nt_v), (cott_hbm, cott_v)]
            + ([(sums_in[0], mlp_v), (sums_in[1], dn_v)] if started else [])
        )
    ]
    loads[0].start()
    greet_kinds(("sibling",) + (("long", "short") if coming else ()) + kinds)

    def fetch(j, carry):
        for k in range(n_pieces):
            weight_copy(k, j).start()
            weight_push(k, j).start()
        return carry

    fetch(0, 0)
    for copy in loads[1:4]:
        copy.start()
    lax.fori_loop(1, steps, fetch, 0)
    for copy in loads[4:]:
        copy.start()
    if coming:
        at, width = coming
        line = line_hbm.at[:, :, pl.ds(at, width)]
        line_copy = pltpu.make_async_copy(line, quarter(next_hbm, 0), next_here)
        moves = [
            push(line, quarter(next_hbm, 1), next_sem, 0, short),
            push(line, quarter(next_hbm, 2), next_sem, 1, long),
            push(quarter(next_hbm, 1), quarter(next_hbm, 3), next_sem, 2, long),
        ]
        line_copy.start()
        moves[0].start()
        moves[1].start()

    for move in carried(kinds, srcs, dsts, carry_sem):
        move.start()

    for copy in loads[:4]:
        copy.wait()

    def columns(j, carry):
        for k in range(n_pieces):
            weight_copy(k, j).wait()
            weight_push(k, j).wait_recv()
        cols = tile_of(j)
        for part in range(parts):
            rows = span_of(part)
            normed = n_v[rows, :]
            gate = dot_nn(normed, w_v[0, :, cols])
            up = dot_nn(normed, w_v[1, :, cols])
            d_hidden = dot_nn(cot_v[rows, :], w_v[2, :, cols])
            s = 1.0 / (1.0 + jnp.exp(-gate))
            silu = gate * s
            act_v[2, rows, cols] = (silu * up).astype(BF16)
            act_v[0, rows, cols] = (d_hidden * up * s * (1.0 + gate * (1.0 - s))).astype(BF16)
            act_v[1, rows, cols] = (d_hidden * silu).astype(BF16)
        for m, left in ((2, cott_v), (0, nt_v), (1, nt_v)):
            grad_v[m, :, cols] = dot_nn(left[...], act_v[m, :, cols]).astype(BF16)
        gradient_push(j).start()

        @pl.when(j > 0)
        def _():
            add_sibling(j - 1)

        return carry

    lax.fori_loop(0, steps, columns, 0)
    stores = [pltpu.make_async_copy(w_v.at[:, pl.ds(HALF, HALF), :], far_hbm, out_sem.at[parts, 0])]
    stores[0].start()
    if coming:
        moves[0].wait_recv()
        moves[2].start()
    for copy in loads[4:]:
        copy.wait()
    for part in range(parts):
        rows = span_of(part)
        for k in range(2):
            if k == 0:
                total, ref, hbm = dot_nt(act_v[2, rows, :], w_v[2]), mlp_v, mlp_hbm
            else:
                total = dot_nt(act_v[0, rows, :], w_v[0]) + dot_nt(act_v[1, rows, :], w_v[1])
                ref, hbm = dn_v, dn_hbm
            ref[rows, :] = total + ref[rows, :] if started else total
            if part == 0 and k == 0:
                add_sibling(steps - 1)
            stores.append(
                pltpu.make_async_copy(ref.at[rows, :], hbm.at[rows, :], out_sem.at[part, k])
            )
            stores[-1].start()

    def settle(j, carry):
        for k in range(n_pieces):
            weight_push(k, j).wait_send()
        gradient_push(j).wait_send()
        for copy in sum_copies(j):
            copy.wait()
        return carry

    lax.fori_loop(0, steps, settle, 0)
    for copy in stores:
        copy.wait()
    if coming:
        line_copy.wait()
        moves[0].wait_send()
        moves[1].wait()
        moves[2].wait()
    for move in carried(kinds, srcs, dsts, carry_sem):
        move.wait()


def feed(number, wide, normed, normed_t, cot, cot_t, sums, pieces, line, coming, loads):
    rows = normed.shape[0]
    started = sums is not None
    kinds = tuple(kind for kind, _ in loads)
    extra = (list(sums) if started else []) + list(pieces) + ([line] if coming else [])
    extra += [array for _, array in loads]
    n_in = 4 + len(extra)
    steps = wide // TILE
    half = jax.ShapeDtypeStruct((3, HALF, wide), BF16)
    two_quarters = jax.ShapeDtypeStruct((3, 2 * QUARTER, wide), BF16)
    return pl.pallas_call(
        functools.partial(feed_kernel, wide, started, len(pieces), coming, kinds),
        in_specs=[ANYWHERE] * n_in,
        out_specs=[ANYWHERE] * ((6 if coming else 5) + len(loads)),
        out_shape=[
            jax.ShapeDtypeStruct((rows, D), F32),
            jax.ShapeDtypeStruct((rows, D), F32),
            two_quarters,
            two_quarters,
            half,
        ]
        + ([jax.ShapeDtypeStruct((3, HALF, coming[1]), BF16)] if coming else [])
        + [like(array) for _, array in loads],
        scratch_shapes=[
            pltpu.VMEM((rows, D), BF16),
            pltpu.VMEM((D, rows), BF16),
            pltpu.VMEM((rows, D), BF16),
            pltpu.VMEM((D, rows), BF16),
            pltpu.VMEM((3, D, wide), BF16),
            pltpu.VMEM((rows, D), F32),
            pltpu.VMEM((rows, D), F32),
            pltpu.VMEM((3, rows, wide), BF16),
            pltpu.VMEM((3, D, wide), BF16),
            pltpu.VMEM((3, HALF, wide), BF16),
            pltpu.SemaphoreType.DMA((6,)),
            pltpu.SemaphoreType.DMA((len(pieces), steps)),
            pltpu.SemaphoreType.DMA((len(pieces), steps)),
            pltpu.SemaphoreType.DMA((len(pieces), steps)),
            pltpu.SemaphoreType.DMA((5, 2)),
            pltpu.SemaphoreType.DMA((steps, 2)),
            pltpu.SemaphoreType.DMA((steps,)),
            pltpu.SemaphoreType.DMA((steps,)),
            pltpu.SemaphoreType.DMA((2, 3)),
            pltpu.SemaphoreType.DMA,
            pltpu.SemaphoreType.DMA((2, max(1, len(loads)))),
        ],
        compiler_params=params(56, collective_id=number, has_side_effects=True),
        cost_estimate=TINY,
        name="feed",
    )(normed, normed_t, cot, cot_t, *extra)


def project_back_kernel(dq_ref, own_kv_ref, recv_kv_ref, cos_ref, sin_ref, nl_ref, xp_ref, dres_ref, pi_ref, *refs):
    w_ref, gain_ref, ig_ref, own_ref, sib_ref, dgain_ref, dbias_ref, g_scr = refs
    t = pl.program_id(0)

    @pl.when(t == 0)
    def _():
        g_scr[...] = jnp.zeros(g_scr.shape, F32)
        dgain_ref[...] = jnp.zeros(dgain_ref.shape, F32)
        dbias_ref[...] = jnp.zeros(dbias_ref.shape, F32)

    cos, sin = cos_ref[...], sin_ref[...]
    low = lax.broadcasted_iota(jnp.int32, cos.shape, 1) % HEAD_SIZE < HEAD_SIZE // 2
    parts = []
    dkv = (own_kv_ref[...] + recv_kv_ref[...].astype(F32)).astype(BF16)
    for n in range(8):
        piece = (dq_ref[:, 128 * n : 128 * (n + 1)] if n < 7 else dkv[:, :KW]).astype(F32)
        parts.append((piece * cos - swap_halves(piece, low) * sin).astype(BF16))
    parts.append(dkv[:, KW:])
    d_lin = jnp.concatenate(parts, axis=1)
    dbias_ref[...] += jnp.sum(d_lin.astype(F32), axis=0, keepdims=True)
    d_normed = dot_nt(d_lin, w_ref[:, :QKV])
    xp = xp_ref[...].astype(F32)
    inv = lax.rsqrt(jnp.sum(xp * xp, axis=1, keepdims=True) * (1.0 / D) + norm_epsilon)
    hat = xp * inv
    scaled = d_normed * gain_ref[...]
    dgain_ref[...] += jnp.sum(d_normed * hat, axis=0, keepdims=True)
    mean = jnp.sum(scaled * hat, axis=1, keepdims=True) * (1.0 / D)
    grad = dres_ref[...] + inv * (scaled - hat * mean)
    high = grad.astype(BF16)
    rest = (grad - high.astype(F32)).astype(BF16)
    ig_ref[...] = dot_nt(high, pi_ref[...]) + dot_nt(rest, pi_ref[...])
    g_scr[...] += dot_tn(nl_ref[...], d_lin)

    @pl.when(t == pl.num_programs(0) - 1)
    def _():
        own_ref[...] = g_scr[:HALF].astype(BF16)
        sib_ref[...] = g_scr[HALF:].astype(BF16)


def project_back(dq, own_kv, recv_kv, cos, sin, nl, xp, d_res, pi, weights, gain, after=()):
    rows = xp.shape[0]
    width = weights.shape[1]

    def tile(cols):
        return pl.BlockSpec((TOKEN_TILE, cols), lambda t: (t, 0))

    def whole(r, c):
        return pl.BlockSpec((r, c), lambda t: (0, 0))

    return pl.pallas_call(
        following(project_back_kernel, 11, after),
        grid=(rows // TOKEN_TILE,),
        in_specs=[tile(QW), tile(256), tile(256), tile(128), tile(128), tile(D), tile(D), tile(D)]
        + [whole(D, D)]
        + [whole(D, width)]
        + [whole(1, D)]
        + [ANYWHERE] * len(after),
        out_specs=[tile(D), whole(HALF, QKV), whole(HALF, QKV), whole(1, D), whole(1, QKV)],
        out_shape=[
            jax.ShapeDtypeStruct((rows, D), F32),
            jax.ShapeDtypeStruct((HALF, QKV), BF16),
            jax.ShapeDtypeStruct((HALF, QKV), BF16),
            jax.ShapeDtypeStruct((1, D), F32),
            jax.ShapeDtypeStruct((1, QKV), F32),
        ],
        scratch_shapes=[pltpu.VMEM((D, QKV), F32)],
        compiler_params=params(56),
        cost_estimate=TINY,
        name="project_back",
    )(dq, own_kv, recv_kv, cos, sin, nl, xp, d_res, pi, weights, gain, *after)


def step_of(first_new, second_new):
    return (
        first_new
        / (1.0 - beta_first**STEP)
        / (jnp.sqrt(second_new / (1.0 - beta_second**STEP)) + adam_epsilon)
    )


def split_two(value):
    high = value.astype(BF16)
    return high, (value - high.astype(F32)).astype(BF16)


def product(dot, a, b):
    return dot(a[0], b[0]) + (dot(a[0], b[1]) + dot(a[1], b[0]))


def side_by_side(value):
    return jnp.concatenate([value[BW * t : BW * (t + 1)] for t in range(D // BW)], axis=1)


def one_above_other(value):
    return jnp.concatenate([value[:, BW * t : BW * (t + 1)] for t in range(D // BW)], axis=0)


def pick_kernel(spans, counts, block_ref, pi_ref, *refs):
    arrays, at = [], 0
    for count in counts:
        arrays.append(refs[at : at + count])
        at += count
    out_ref, w_scr, sem = refs[at:]
    slots = out_ref.shape[0]

    def each(slot, act):
        block = block_ref[slot]
        for n, pieces in enumerate(arrays):
            for page, (low, high) in enumerate(spans[n]):

                @pl.when((block >= low) & (block < high))
                def _(pieces=pieces, page=page, low=low):
                    column = pl.multiple_of((block - low) * BW, BW)
                    row = 0
                    for k, piece in enumerate(pieces):
                        count = piece.shape[1]
                        act(
                            pltpu.make_async_copy(
                                piece.at[page, :, pl.ds(column, BW)],
                                w_scr.at[slot, pl.ds(row, count), :],
                                sem.at[slot, k],
                            )
                        )
                        row += count

    for slot in range(slots):
        each(slot, lambda copy: copy.start())
    for slot in range(slots):
        each(slot, lambda copy: copy.wait())
        out_ref[slot] = dot_nn(pi_ref[...], w_scr[slot])


def picked(slot_block, pi, arrays, spans, after=()):
    capacity = slot_block.shape[0]
    vmem = pl.BlockSpec(memory_space=pltpu.VMEM)
    flat = [p for a in arrays for p in a]
    return pl.pallas_call(
        following(
            functools.partial(pick_kernel, spans, [len(a) for a in arrays]), 2 + len(flat), after
        ),
        in_specs=[pl.BlockSpec(memory_space=pltpu.SMEM), vmem]
        + [ANYWHERE] * (len(flat) + len(after)),
        out_specs=vmem,
        out_shape=jax.ShapeDtypeStruct((capacity, D, BW), F32),
        scratch_shapes=[pltpu.VMEM((capacity, D, BW), BF16), pltpu.SemaphoreType.DMA((capacity, 8))],
        compiler_params=params(60),
        cost_estimate=TINY,
        name="picked",
    )(slot_block, pi, *flat, *after)


def adam_kernel(block_ref, grad_ref, weight_ref, first_ref, second_ref, left_ref, right_ref, first_out, second_out, block_out):
    used = block_ref[pl.program_id(0)] >= 0

    @pl.when(used)
    def _():
        grad = grad_ref[0]
        left, right = split_two(left_ref[0]), split_two(right_ref[0])
        turned = split_two(side_by_side(dot_nn(grad, right[0]) + dot_nn(grad, right[1])))
        rotated = one_above_other(product(dot_tn, left, turned))
        first_new = beta_first * first_ref[0] + (1.0 - beta_first) * rotated
        second_new = beta_second * second_ref[0] + (1.0 - beta_second) * rotated * rotated
        first_out[0] = first_new
        second_out[0] = second_new
        step = split_two(step_of(first_new, second_new))
        back = split_two(side_by_side(product(dot_nt, step, right)))
        back = one_above_other(product(dot_nn, left, back))
        weights = weight_ref[0]
        block_out[0] = weights - rate_matrix * (back + weight_decay * weights)

    @pl.when(jnp.logical_not(used))
    def _():
        for ref in (first_out, second_out, block_out):
            ref[...] = jnp.zeros(ref.shape, F32)


def pack_kernel(spots, targets, counts, block_ref, *refs):
    n_in = sum(counts)
    ins, outs, (slots_ref, all_scr) = refs[:n_in], refs[n_in:-2], refs[-2:]
    at = 0
    for count, found in zip(counts, spots):
        for page, (width, target) in enumerate(found):
            total = ins[at][page, :, :width]
            for ref in ins[at + 1 : at + count]:
                total = total + ref[page, : total.shape[0], :width].astype(F32)
            all_scr[:, target : target + width] = total
        at += count
    for ref, start in zip(outs, targets):
        ref[...] = all_scr[:, start : start + ref.shape[1]]

    def one(slot, carry):
        block = jnp.maximum(block_ref[slot], 0)
        column = pl.multiple_of(block * BW, BW)
        slots_ref[slot] = all_scr[:, pl.ds(column, BW)].astype(BF16)
        return carry

    lax.fori_loop(0, slots_ref.shape[0], one, 0)


def packed(slot_block, groups, spots, targets):
    rows = groups[0][0].shape[1]
    vmem = pl.BlockSpec(memory_space=pltpu.VMEM)
    parts = [part for group in groups for part in group]
    total = (130 + 1) * BW
    return pl.pallas_call(
        functools.partial(
            pack_kernel, spots, [start for start, _ in targets], [len(g) for g in groups]
        ),
        in_specs=[pl.BlockSpec(memory_space=pltpu.SMEM)] + [vmem] * len(parts),
        out_specs=[vmem] * (len(targets) + 1),
        out_shape=[jax.ShapeDtypeStruct((rows, width), F32) for _, width in targets]
        + [jax.ShapeDtypeStruct((slot_block.shape[0], rows, BW), BF16)],
        scratch_shapes=[pltpu.VMEM((rows, total), F32)],
        compiler_params=params(60),
        cost_estimate=TINY,
        name="packed",
    )(slot_block, *parts)


def rotated_adam(slot_block, grads, weights, first_moment, second_moment, left, right):
    capacity = first_moment.shape[0]
    slab = pl.BlockSpec((1, D, BW), lambda s, b: (s, 0, 0))
    basis = pl.BlockSpec((1, BW, BW), lambda s, b: (s, 0, 0))
    return pl.pallas_call(
        adam_kernel,
        grid_spec=pltpu.PrefetchScalarGridSpec(
            num_scalar_prefetch=1,
            grid=(capacity,),
            in_specs=[slab, slab, slab, slab, basis, basis],
            out_specs=[slab] * 3,
        ),
        out_shape=[jax.ShapeDtypeStruct((capacity, D, BW), F32)] * 3,
        compiler_params=params(60),
        cost_estimate=TINY,
        name="rotated_adam",
    )(slot_block, grads, weights, first_moment, second_moment, left, right)


def vector_adam(vectors, grad_vectors, vector_first, vector_second):
    first_new = beta_first * vector_first + (1.0 - beta_first) * grad_vectors
    second_new = beta_second * vector_second + (1.0 - beta_second) * grad_vectors * grad_vectors
    return (second_new, vectors - rate_vector * step_of(first_new, second_new))


def hand_out(moving, arrived, after=()):
    at = 0
    for r in moving:
        came = arrived[at : at + len(r.next)]
        at += len(r.next)
        kind = r.next[0][0]
        if kind == "long":
            r.fold(came, after)
        elif kind == "short":
            r.share(came, after)
        else:
            r.end(came)
            r.next = []


def on_device(
    places,
    inputs,
    cotangent,
    starts,
    query_weight,
    key_weight,
    value_weight,
    out_weight,
    gate_weight,
    up_weight,
    down_weight,
    vectors,
    owner_slot,
    first_moment,
    second_moment,
    basis_left,
    basis_right,
    vector_first,
    vector_second,
):
    n_dev, shard_rows = places.n_dev, places.rows
    here = inputs.shape[2]
    seq_index = lax.axis_index("seq")
    vec_here = vectors.shape[0]

    out_t, down_t = out_weight.T, down_weight.T
    natural = places.natural_rows()
    pi = (jnp.arange(D, dtype=jnp.int32)[:, None] == natural[None, :]).astype(BF16)
    riding = (
        jnp.arange(n_dev, dtype=jnp.int32)[:, None] * shard_rows == natural[None, :]
    ).astype(BF16)
    vector_rows = jnp.pad(vectors.reshape(1, vec_here), ((0, shard_rows - 1), (0, 128 - vec_here)))
    cot = cotangent[:, 0].reshape(-1, D)
    cot_p = dot_nn(cot, pi).astype(BF16)
    cot_t = lax.dot_general(
        pi, cot, (((0,), (1,)), ((), ())), preferred_element_type=F32
    ).astype(BF16)
    attention_line = stacked_rows(
        line_parts(
            places,
            rounded(
                [query_weight, key_weight, value_weight, out_t, vector_rows],
                places.padded,
                [(0, 0, 0, QW), (0, 1, 0, KW), (0, 2, 0, KW), (0, 3, 0, QW), (0, 4, 0, 128)],
            ),
        ),
        after=(cot_p, cot_t),
    )
    feed_parts = [gate_weight, up_weight, down_t]

    def shard_of(chunks, after):
        spans = [(m, m, OFFSETS[n], CHUNKS[n]) for n in chunks for m in range(3)]
        return rounded(feed_parts, places.padded, spans, after=after)

    shard_a = shard_of((0,), ())
    backwards = [(-k % places.line, places.line) for k in range(1, places.line)]
    attention, *arrived = spread(attention_line, [(kind, shard_a) for kind in backwards])
    line_a = stacked_rows([shard_a] + arrived)
    shard_b = shard_of((1,), (attention,))
    short_a, long_a = send(line_a, places.short), send(line_a, places.long)
    attention_pages, attention = attention, attention[0]
    riders = attention[:, QKV + QW :]
    vectors_full = dot_nn(riding, riders)[:, :vec_here].reshape(-1)
    gains = jnp.pad(vectors_full[: 2 * D].reshape(2, D), ((0, 6), (0, 0))).astype(BF16)
    gains = dot_nn(gains, pi)
    gain_attn, gain_mlp = gains[0:1], gains[1:2]
    bias = vectors_full[2 * D :].reshape(1, QKV)

    spots = seq_index * here + jnp.arange(here, dtype=jnp.int32)
    own_starts = starts[:, 0]
    before = own_starts[:, None, :] <= spots[None, :, None]
    doc_begin = jnp.max(jnp.where(before, own_starts[:, None, :], 0), axis=2)
    relative = (spots[None, :] - doc_begin).astype(F32).reshape(-1)
    frequency = jnp.power(
        rope_theta, -jnp.arange(0, HEAD_SIZE, 2, dtype=F32) / HEAD_SIZE
    )
    angles = relative[:, None] * frequency[None, :]
    cos, sin = jnp.cos(angles), jnp.sin(angles)
    cos = jnp.concatenate([cos] * 4, axis=1)
    sin = jnp.concatenate([-sin, sin, -sin, sin], axis=1)
    begin = doc_begin + here - seq_index * here
    lo = begin[:, ::128] // 128
    begin = begin[:, None, :]

    x = inputs[:, 0].reshape(-1, D)
    xp, nl, q, k, v, kv = project(
        x, pi, attention, gain_attn, bias, cos, sin, after=(line_a, shard_b)
    )
    line_b = stacked_rows(line_parts(places, shard_b), after=(q,))
    far_a = send(short_a, places.long)
    short_b, long_b = send(line_b, places.short), send(line_b, places.long)
    shard_c = shard_of((2,), (line_b,))

    back = [(2 * n + 1, 2 * n) for n in range(n_dev // 2)]

    def streams(array):
        return array.reshape(MICRO, here, array.shape[-1])

    heads = (
        lo,
        streams(q),
        streams(kv[:, :KW]),
        streams(k),
        streams(kv[:, KW:]),
        streams(v),
        begin,
    )
    attended, lse = attend(*heads, after=(line_b, short_a, shard_c))
    attended_flat = attended.reshape(-1, QW)
    residual, normed, normed_t = middle(
        attended_flat, xp, attention, gain_mlp, after=(short_b,)
    )
    far_b = send(short_b, places.long)
    shard_last = shard_of((2,), (attended,))
    line_c = stacked_rows(line_parts(places, shard_c, shard_last), after=(normed,))
    shard_d = shard_of((3,), (line_b,))

    sums = None
    reductions, feed_pieces = [], []

    pieces = [[line_a, short_a, long_a, far_a], [line_b, short_b, long_b, far_b]]
    lines = [line_c]
    for n, wide in enumerate(CHUNKS):
        coming = (0, CHUNKS[n + 2]) if n + 2 < len(CHUNKS) else None
        moving = [r for r in reductions if r.next]
        loads = [load for r in moving for load in r.next]
        if n == 0:
            loads = [(kind, shard_d) for kind in backwards]
        mlp, d_normed, kept, passed, far, *arrived = feed(
            n, wide, normed, normed_t, cot_p, cot_t, sums, pieces[n],
            lines[n] if coming else None, coming, loads,
        )
        sums = (mlp, d_normed)
        feed_pieces.append(list(pieces[n]) + [far])
        if coming:
            pieces.append([arrived.pop(0)])
        if n == 0:
            lines.append(stacked_rows([shard_d] + arrived))
        hand_out(moving, arrived)
        reductions.append(Reduce(places, kept, passed))

    along = {"long": places.long, "short": places.short}

    def set_off(moving):
        return [
            send(array, along[kind] if kind in along else places.ahead[kind[0]])
            for r in moving
            for kind, array in r.next
        ]

    def operands(moving):
        return tuple(array for r in moving for _, array in r.next)

    moving, newest = [r for r in reductions[:-1] if r.next], reductions[-1:]
    arrived, arrived_late = set_off(moving), set_off(newest)
    output, d_res, d_att, own_out, other_out, d_gain_mlp = middle_back(
        residual, sums[0], sums[1], cot_p, attended_flat, pi, attention, gain_mlp,
        after=operands(moving + newest),
    )
    ended = tuple(arrived[: places.line - 1])
    hand_out(moving, arrived, (d_att,))
    moving = [r for r in reductions[:-1] if r.next]
    arrived = set_off(moving)
    dq, dkv, dkv_recv = attend_back(
        *heads, attended, streams(d_att), lse, after=operands(moving) + ended
    )
    dkv_recv = send(dkv_recv, back)
    hand_out(newest, arrived_late, (dq,))
    hand_out(moving, arrived, (dq,))
    moving = [r for r in reductions if r.next and r.next[0][0] == "short"]
    arrived = set_off(moving)
    input_grad, own_in, other_in, d_gain_attn, d_bias = project_back(
        dq.reshape(-1, QW), dkv.reshape(-1, 2 * KW), dkv_recv.reshape(-1, 2 * KW),
        cos, sin, nl, xp, d_res, pi, attention, gain_attn, after=operands(moving),
    )
    hand_out(moving, arrived, (own_in,))

    d_gains = jnp.concatenate([d_gain_attn, d_gain_mlp, jnp.zeros((6, D), F32)], axis=0)
    high, rest = split_two(d_gains)
    d_gains = dot_nt(high, pi) + dot_nt(rest, pi)
    d_vectors = jnp.concatenate([d_gains[0], d_gains[1], d_bias[0]])
    d_vectors = jnp.pad(d_vectors.reshape(n_dev, vec_here), ((0, 0), (0, 128 - vec_here)))
    riders = dot_tn(riding, d_vectors.astype(BF16)).astype(BF16)
    moving = [r for r in reductions if r.next]
    grad_in, *arrived = reduce_tail(
        places,
        [own_out, own_in, riders[:HALF]],
        [other_out, other_in, riders[HALF:]],
        [load for r in moving for load in r.next],
    )
    hand_out(moving, arrived)

    capacity = first_moment.shape[0]
    slot_count = n_dev * capacity
    slot_block = (
        jnp.full((slot_count,), -1, jnp.int32)
        .at[owner_slot]
        .set(jnp.arange(owner_slot.shape[0], dtype=jnp.int32))
    )
    spots = [
        [(w, 2048 + m * FF + o) for m in range(3)] for o, w in zip(OFFSETS, CHUNKS)
    ]
    groups = [r.parts for r in reductions]
    for start, width, target in ((0, QW, QKV), (QW, QKV, 0), (QW + QKV, BW, 130 * BW)):
        groups.append([grad_in[:, :, start : start + width]])
        spots.append([(width, target)])
    targets = [
        (0, QW), (QW, KW), (QW + KW, KW), (QKV, QW),
        (2048, FF), (2048 + FF, FF), (2048 + 2 * FF, FF), (130 * BW, BW),
    ]
    (
        grad_query, grad_key, grad_value, grad_out_t, grad_gate, grad_up, grad_down_t, rider_sums, slots,
    ) = packed(slot_block, groups, spots, targets)
    grad_vectors = rider_sums[0, :vec_here]
    owned_grads = lax.all_to_all(
        slots,
        BOTH,
        split_axis=0,
        concat_axis=1,
        tiled=True,
    )
    local_block = lax.dynamic_slice_in_dim(
        slot_block, lax.axis_index(BOTH) * capacity, capacity, 0
    )
    spans = [[(0, 16)]]
    for o, w in zip(OFFSETS, CHUNKS):
        first, count = o // BW, w // BW
        spans.append(
            [(16 + 38 * m + first, 16 + 38 * m + first + count) for m in range(3)]
        )
    owned_weights = picked(
        local_block, pi, [[attention_pages]] + feed_pieces, spans, after=(slots,)
    )
    new_first, new_second, new_blocks = rotated_adam(
        local_block, owned_grads, owned_weights, first_moment, second_moment, basis_left, basis_right
    )
    vector_second_new, vector_new = vector_adam(vectors, grad_vectors, vector_first, vector_second)
    return (
        output.reshape(inputs.shape),
        input_grad.reshape(inputs.shape),
        grad_query,
        grad_key,
        grad_value,
        grad_out_t.T,
        grad_gate,
        grad_up,
        grad_down_t.T,
        grad_vectors,
        new_first,
        new_second,
        new_blocks,
        vector_second_new,
        vector_new,
    )


def solution(mesh):
    rows = P(("dp", "seq"), None)
    columns = P(None, ("dp", "seq"))
    tokens = P(None, "dp", "seq", None)
    slots = P(("dp", "seq"), None, None)
    line = P(("dp", "seq"))
    places = Places(mesh.shape["dp"], mesh.shape["seq"])
    return jax.shard_map(
        functools.partial(on_device, places),
        mesh=mesh,
        in_specs=(
            tokens, tokens, P(None, "dp", None), rows, rows, rows, columns, rows, rows, columns,
            line, P(), slots, slots, slots, slots, line, line,
        ),
        out_specs=(
            tokens, tokens, rows, rows, rows, columns, rows, rows, columns, line,
            slots, slots, slots, line, line,
        ),
        check_vma=False,
    )
```
